32 devices in a mesh: rep: 2 (over x), fsdp: 4 (over z), ctx: 4 (over y, core).
Axes of the slice: x: 2, y: 2, z: 4, core: 2. Of those that a mesh axis runs over, the one named last changes fastest.
Arguments:
- tokens: bfloat16 [8, 1024, 768], P(('rep', 'fsdp'), 'ctx'), may hold values from -2.5 to 2.5
- lengths: int32 [8], P(('rep', 'fsdp')), may hold values from 256 to 1024, as said below
- cotangent: bfloat16 [8, 1024, 768], P(('rep', 'fsdp'), 'ctx'), may hold values from -8 to 8
- w_qkv: bfloat16 [2, 3, 768, 768], P(None, None, 'fsdp'), may hold values from -0.21875 to 0.21875
- w_attn_out: bfloat16 [2, 768, 768], P(None, 'fsdp'), may hold values from -1.1953125 to 1.1953125
- w_in: bfloat16 [2, 768, 3072], P(None, 'fsdp'), may hold values from -0.21875 to 0.21875
- w_out: bfloat16 [2, 3072, 768], P(None, 'fsdp'), may hold values from -0.109375 to 0.109375
- bias_q: bfloat16 [2, 768], P(None, 'fsdp'), may hold values from -0.75 to 0.75
- bias_d: bfloat16 [2, 3, 768], P(None, None, 'fsdp'), may hold values from -0.25 to 0.25
- bias_ff: bfloat16 [2, 3072], P(None, 'fsdp'), may hold values from -0.75 to 0.75
- norm_gain: bfloat16 [2, 2, 768], P(None, None, 'fsdp'), may hold values from 0.5 to 1.5
- norm_shift: bfloat16 [2, 2, 768], P(None, None, 'fsdp'), may hold values from -0.75 to 0.75
Outputs:
- output_tokens: bfloat16 [8, 1024, 768], P(('rep', 'fsdp'), 'ctx')
- grad_tokens: float32 [8, 1024, 768], P(('rep', 'fsdp'), 'ctx')
- grad_w_qkv: float32 [2, 3, 768, 768], P(None, None, 'fsdp')
- grad_w_attn_out: float32 [2, 768, 768], P(None, 'fsdp')
- grad_w_in: float32 [2, 768, 3072], P(None, 'fsdp')
- grad_w_out: float32 [2, 3072, 768], P(None, 'fsdp')
- grad_bias_q: float32 [2, 768], P(None, 'fsdp')
- grad_bias_d: float32 [2, 3, 768], P(None, None, 'fsdp')
- grad_bias_ff: float32 [2, 3072], P(None, 'fsdp')
- grad_norm_gain: float32 [2, 2, 768], P(None, None, 'fsdp')
- grad_norm_shift: float32 [2, 2, 768], P(None, None, 'fsdp')
The draws below stay inside these ranges and needn't reach their ends.
Inputs may be any that keep to these rules, and one draw needn't show every extreme that they name: `lengths`: some sequence has exactly 1024 valid tokens and some other exactly 256.
All inputs are finite; a program needn't handle non-finite values.
Results may differ from the reference program's by a relative error of at most 0.02.
Values may be sent and summed in bfloat16 or wider, within the bound.
A program may use at most 256 MiB of HBM per device.

```python
import jax
import jax.numpy as jnp
from jax import lax

D = 768
HEADS = 12
HEAD = 64
FF = 3072
SEQ_LEN = 1024
SEQS = 8


def draw_lengths(key, part):
    drawn_lengths = jax.random.randint(key, (SEQS,), SEQ_LEN // 4, SEQ_LEN + 1)
    longest_at = jax.random.randint(jax.random.fold_in(key, 1), (), 0, SEQS)
    step_away = jax.random.randint(jax.random.fold_in(key, 2), (), 1, SEQS)
    shortest_at = (longest_at + step_away) % SEQS
    drawn_lengths = drawn_lengths.at[longest_at].set(SEQ_LEN)
    drawn_lengths = drawn_lengths.at[shortest_at].set(SEQ_LEN // 4)
    return drawn_lengths.astype(jnp.int32)


def spiked(values, stream_key, source, target, blocks, factor):
    owner, partner = [(jnp.arange(values.shape[position]) // (values.shape[position] // blocks)).reshape([-1 if axis == position else 1 for axis in range(values.ndim)]) for position in (source, target)]
    chosen = jax.random.permutation(stream_key, blocks)[partner]
    strong = (owner == chosen) | (owner == (partner + blocks // 2) % blocks)
    return jnp.where(strong, factor * values, values)


def block_scale(key, shape, cuts, low, top_value):
    factor_of = 1.0
    for axis_at, parts in cuts:
        heights = jax.random.uniform(jax.random.fold_in(jax.random.fold_in(key, 6), axis_at), (parts,), jnp.float32, low / len(cuts), top_value / len(cuts))
        factor_of = factor_of * jnp.repeat(jnp.exp(heights), shape[axis_at] // parts).reshape((-1,) + (1,) * (len(shape) - 1 - axis_at))
    return factor_of


def normal_values(key, shape, deviation, bound, pieces=(), dtype=jnp.bfloat16):
    entries = jax.random.normal(key, shape, jnp.float32) * deviation
    if len(pieces) > 0:
        entries = block_scale(key, shape, pieces, -0.22, 0.18) * entries
    return jnp.clip(entries, min=-bound, max=bound).astype(dtype)


def heavy_noise(key, shape, spread, limit, cuts, heavy, kind=jnp.bfloat16):
    values = spread * jax.random.normal(key, shape, jnp.float32)
    if cuts:
        values = values * block_scale(key, shape, cuts, -0.22, 0.18)
    return jnp.clip(spiked(values, jax.random.fold_in(key, 3), *heavy), -limit, limit).astype(kind)


def setup_inputs(seed: int = 0) -> dict:
    splits = jax.random.split(jax.random.key(seed), 13)
    tokens = normal_values(splits[0], (SEQS, SEQ_LEN, D), 1.0, 2.5, ((0, 8), (1, 4)))
    lengths = draw_lengths(jax.random.fold_in(splits[12], 71), 0)
    cotangent = heavy_noise(splits[2], (SEQS, SEQ_LEN, D), 1.0, 8.0, ((0, 8), (1, 4)), (0, 2, 8, 2.0))
    w_qkv = normal_values(splits[3], (2, 3, D, D), D ** -0.5, 0.21875, ((2, 4),))
    w_attn_out = normal_values(splits[4], (2, D, D), (0.015 * SEQ_LEN ** 0.5), 1.1953125, ((1, 4),))
    w_in = normal_values(splits[5], (2, D, FF), D ** -0.5, 0.21875, ((1, 4),))
    w_out = normal_values(splits[6], (2, FF, D), FF ** -0.5, 0.109375, ((1, 4),))
    bias_q = normal_values(splits[7], (2, D), 0.3, 0.75, ((1, 4),))
    bias_d = normal_values(splits[8], (2, 3, D), 0.1, 0.25, ((2, 4),))
    bias_ff = normal_values(splits[9], (2, FF), 0.3, 0.75, ((1, 4),))
    norm_gain = jnp.clip(1.0 + 0.1 * jax.random.normal(splits[10], (2, 2, D), jnp.float32), 0.5, 1.5).astype(jnp.bfloat16)
    norm_shift = normal_values(splits[11], (2, 2, D), 0.3, 0.75, ((2, 4),))
    return dict(tokens=tokens, lengths=lengths, cotangent=cotangent, w_qkv=w_qkv, w_attn_out=w_attn_out, w_in=w_in, w_out=w_out, bias_q=bias_q, bias_d=bias_d, bias_ff=bias_ff, norm_gain=norm_gain, norm_shift=norm_shift)


epsilon = 1e-05
score_scale = 0.125
masked_value = -1e+30
highest = lax.Precision.HIGHEST

@jax.custom_vjp
def low(v):
    return lax.optimization_barrier(v.astype(jnp.bfloat16)).astype(jnp.float32)

@jax.custom_vjp
def low_back(v):
    return v

def low_keep(v):
    return (low(v), None)

def low_pass(kept, grad):
    return (grad,)

def back_keep(v):
    return (v, None)

def back_low(kept, grad):
    return (low(grad),)
low.defvjp(low_keep, low_pass)
low_back.defvjp(back_keep, back_low)

def rounded_both(operand):
    return low(low_back(operand))

def matmul(operand_a, operand_b):
    return jnp.dot(operand_a, operand_b, precision=highest, preferred_element_type=jnp.float32)

def layer_norm(operand, scale_row, shift_row):
    center = operand - lax.optimization_barrier(jnp.mean(operand, axis=-1, keepdims=True))
    variance = lax.optimization_barrier(jnp.mean(center * center, axis=-1, keepdims=True))
    return center * lax.rsqrt(variance + epsilon) * scale_row + shift_row

def attention(queries, key_rows, value_rows, length):
    row_count = queries.shape[0]
    block_rows = min(512, row_count)
    key_ok = jnp.arange(row_count) < length
    key_heads = key_rows.reshape(row_count, HEADS, HEAD)
    value_heads = value_rows.reshape(row_count, HEADS, HEAD)

    def one_block(query_block):
        scores = jnp.einsum('qhd,khd->hqk', query_block, key_heads, precision=highest) * score_scale
        scores = jnp.where(key_ok[None, None, :], scores, masked_value)
        scores = low_back(scores)
        weights = low(jax.nn.softmax(scores, axis=-1))
        return jnp.einsum('hqk,khd->qhd', weights, value_heads, precision=highest)
    blocks = queries.reshape(row_count // block_rows, block_rows, HEADS, HEAD)
    result = lax.map(jax.checkpoint(one_block), blocks)
    return result.reshape(row_count, HEADS * HEAD)

def transformer_block(inputs, params, length):
    qkv_mats, out_mat, in_mat, down_mat, query_bias, bias_rows, ffn_bias, gains, shifts = params
    rounded = low(inputs)
    queries = rounded_both(matmul(rounded, qkv_mats[0]) + query_bias)
    key_rows = rounded_both(matmul(rounded, qkv_mats[1]))
    value_rows = rounded_both(matmul(rounded, qkv_mats[2]) + bias_rows[0])
    mixed = rounded_both(attention(queries, key_rows, value_rows, length))
    branch = low_back(matmul(mixed, out_mat) + bias_rows[1])
    normed = layer_norm(inputs + branch, gains[0], shifts[0])
    hidden = low_back(matmul(low(normed), in_mat) + ffn_bias)
    active = low(jax.nn.gelu(hidden, approximate=False))
    update = low_back(matmul(active, down_mat) + bias_rows[2])
    return layer_norm(normed + update, gains[1], shifts[1])

def reference(tokens, lengths, cotangent, w_qkv, w_attn_out, w_in, w_out, bias_q, bias_d, bias_ff, norm_gain, norm_shift):
    params = (w_qkv.astype(jnp.float32), w_attn_out.astype(jnp.float32), w_in.astype(jnp.float32), w_out.astype(jnp.float32), bias_q.astype(jnp.float32), bias_d.astype(jnp.float32), bias_ff.astype(jnp.float32), norm_gain.astype(jnp.float32), norm_shift.astype(jnp.float32))

    def run_blocks(weights, inputs, length):
        carried = inputs
        for layer_idx in range(2):
            carried = transformer_block(carried, tuple((item[layer_idx] for item in weights)), length)
        return carried

    def per_sequence(totals, items):
        seq_tokens, seq_cot, length = items
        valid_rows = (jnp.arange(SEQ_LEN) < length).astype(jnp.float32)
        output, pullback = jax.vjp(lambda weights, inputs: run_blocks(weights, inputs, length), params, seq_tokens.astype(jnp.float32))
        grad_params, grad_inputs = pullback(seq_cot.astype(jnp.float32) * valid_rows[:, None])
        totals = tuple((acc_item + part_item for acc_item, part_item in zip(totals, grad_params)))
        return (totals, (output.astype(jnp.bfloat16), grad_inputs))
    zeros = tuple((jnp.zeros_like(item) for item in params))
    totals, (outputs, grad_inputs) = lax.scan(per_sequence, zeros, (tokens, cotangent, lengths))
    return (outputs, grad_inputs, totals[0], totals[1], totals[2], totals[3], totals[4], totals[5], totals[6], totals[7], totals[8])
```

```python
import functools

import jax
import jax.numpy as jnp
from jax import lax
from jax.experimental import pallas as pl
from jax.experimental.pallas import tpu as pltpu
from jax.sharding import PartitionSpec as P

HEADS = 12
HEAD = 64
D = HEADS * HEAD
MESH = pl.DeviceIdType.MESH
BF = jnp.bfloat16
F32 = jnp.float32
MIB = 2**20

epsilon = 1e-05
score_scale = 0.125
masked_value = -1e30


class Place:
    def __init__(self, n, ny):
        self.n, self.ny = n, ny
        self.r = lax.axis_index("rep")
        self.z = lax.axis_index("fsdp")
        c = lax.axis_index("ctx")
        self.y, self.k = lax.div(c, 2), lax.rem(c, 2)
        self.p = lax.rem(self.r + self.y, 2)

    def shard(self, offset):
        return lax.rem(self.z + (offset + self.n), self.n)

    def at(self, dr=0, dz=0, dy=0, dk=0):
        r = lax.rem(self.r + dr, 2)
        y = lax.rem(self.y + (dy + self.ny), self.ny)
        k = lax.rem(self.k + dk, 2)
        return (r, self.shard(dz), 2 * y + k)

    def greet(self, others):
        barrier = pltpu.get_barrier_semaphore()
        for other in others:
            pl.semaphore_signal(barrier, inc=1, device_id=other, device_id_type=MESH)
        pl.semaphore_wait(barrier, len(others))

    def everyone(self):
        others = [self.at(dz=o) for o in range(1, self.n)]
        others += [self.at(dr=1), self.at(dk=1)]
        others += [self.at(dy=o) for o in range(1, self.ny)]
        return others


def remote(src, dst, send, recv, device):
    copy = pltpu.make_async_remote_copy(
        src_ref=src, dst_ref=dst, send_sem=send, recv_sem=recv, device_id=device, device_id_type=MESH
    )
    copy.start()
    return copy


class Gather:
    def __init__(self, place, full, by_shard, local, send, recv):
        self.place, self.full, self.by_shard = place, full, by_shard
        self.local, self.send, self.recv = local, send, recv
        self.n = place.n
        self.half = full.shape[2] // 2
        self.copies = []
        self.core_copies = []

    @staticmethod
    def count(n):
        return 6 * n - 4

    def part(self, shard, q0, count, k):
        rows = pl.ds(pl.multiple_of(k * self.half, self.half), self.half)
        if self.by_shard:
            return self.full.at[shard, pl.ds(q0, count), rows]
        return self.full.at[pl.ds(q0, count), shard, rows]

    def load(self, sources):
        self.loads = []
        for i, (q, count, source) in enumerate(sources):
            z = self.place.z
            if self.by_shard:
                target = self.full.at[z]
            elif count is None:
                target = self.full.at[q, z]
            else:
                target = self.full.at[pl.ds(q, count), z]
            copy = pltpu.make_async_copy(source, target, self.local.at[i])
            copy.start()
            self.loads.append(copy)

    def share(self, piece, slot, device, core=False):
        copy = remote(piece, piece, self.send.at[slot], self.recv.at[slot], device)
        (self.core_copies if core else self.copies).append(copy)
        return copy

    def core_share(self, shard, q0, count, slot):
        place = self.place
        base = self.n + 2 * (self.n - 1)
        self.share(self.part(shard, q0, count, place.k), base + slot, place.at(dk=1), core=True)

    def start(self):
        place, n = self.place, self.n
        for copy in self.loads:
            copy.wait()
        self.plus, self.minus = {}, {}
        self.xs, self.ys = {}, {}
        mine = self.part(place.z, 2 * place.p, 2, place.k)
        if n // 2 > 1:
            self.plus[1] = self.share(mine, 0, place.at(dz=1))
            self.minus[1] = self.share(mine, n // 2, place.at(dz=-1))
        else:
            self.plus[1] = self.share(self.part(place.z, 2 * place.p, 1, place.k), 0, place.at(dz=1))
            self.minus[1] = self.share(self.part(place.z, 2 * place.p + 1, 1, place.k), 1, place.at(dz=-1))

    def hop(self, d, forward):
        place, n = self.place, self.n
        sign = 1 if forward else -1
        table = self.plus if forward else self.minus
        table[d].wait_recv()
        shard = place.shard(-sign * d)
        q0 = 2 * place.p + (0 if forward else 1)
        base = 0 if forward else n // 2
        if d < n // 2:
            if d + 1 < n // 2:
                piece = self.part(shard, 2 * place.p, 2, place.k)
            else:
                piece = self.part(shard, q0, 1, place.k)
            table[d + 1] = self.share(piece, base + d, place.at(dz=sign))
        whole = d < n // 2
        distance = (sign * d) % n
        if whole or forward:
            slot = n + distance - 1
            self.xs[distance] = self.share(self.part(shard, 2 * place.p, 1, place.k), slot, place.at(dr=1))
        if whole or not forward:
            slot = n + (n - 1) + distance - 1
            self.ys[distance] = self.share(self.part(shard, 2 * place.p + 1, 1, place.k), slot, place.at(dy=1))
        if whole:
            self.core_share(shard, 2 * place.p, 2, base + d - 1)
        else:
            self.core_share(shard, q0, 1, base + d - 1)

    def hops(self, d):
        self.hop(d, True)
        self.hop(d, False)

    def cross(self, which):
        place, n = self.place, self.n
        table = (self.xs, self.ys)[which]
        for distance in sorted(table, key=lambda o: min(o, n - o)):
            table[distance].wait_recv()
            shard = place.shard(-distance)
            q = 2 * (1 - place.p) + which
            self.core_share(shard, q, 1, n + which * (n - 1) + distance - 1)

    def finish(self):
        for copy in self.core_copies:
            copy.wait_recv()

    def drain(self):
        for copy in self.core_copies + self.copies:
            copy.wait_send()

    def steps(self):
        out = [self.start]
        out += [functools.partial(self.hops, d) for d in range(1, self.n // 2 + 1)]
        out += [functools.partial(self.cross, 0), functools.partial(self.cross, 1), self.finish]
        return out


def weight_sources(b, qkv, ao, win, wout):
    return [
        [(0, 3, qkv.at[b]), (3, None, ao.at[b])],
        [(q, None, win.at[b, :, pl.ds(q * D, D)]) for q in range(4)],
        [(None, None, wout.at[b])],
    ]


def gather_kernel(n, ny, *refs):
    qkv, ao, win, wout, small = refs[:5]
    fulls, small_full = refs[5:11], refs[11]
    local, send, recv, small_send, small_recv = refs[12:]
    place = Place(n, ny)
    groups = []
    for g in range(6):
        b, kind = g // 3, g % 3
        group = Gather(place, fulls[g], kind == 2, local.at[g], send.at[g], recv.at[g])
        group.load(weight_sources(b, qkv, ao, win, wout)[kind])
        groups.append(group)
    own = pltpu.make_async_copy(small, small_full.at[place.z], small_send.at[0])
    own.start()
    place.greet(place.everyone())
    smalls = [
        remote(small, small_full.at[place.z], small_send.at[o], small_recv.at[o], place.at(dz=o))
        for o in range(1, n)
    ]
    steps = [group.steps() for group in groups]
    for t in range(len(steps[0]) + 5):
        for g in range(6):
            if 0 <= t - g < len(steps[g]):
                steps[g][t - g]()
    for group in groups:
        group.drain()
    own.wait()
    for copy in smalls:
        copy.wait()


def gather_weights(n, ny, qkv, ao, win, wout, small):
    rows = D // n
    shapes = [(4, n, rows, D), (4, n, rows, D), (n, 4, rows, D)] * 2
    out = [jax.ShapeDtypeStruct(shape, BF) for shape in shapes]
    out.append(jax.ShapeDtypeStruct((n,) + small.shape, BF))
    anywhere = pl.BlockSpec(memory_space=pl.ANY)
    return pl.pallas_call(
        functools.partial(gather_kernel, n, ny),
        out_shape=out,
        in_specs=[anywhere] * 5,
        out_specs=[anywhere] * 7,
        scratch_shapes=[
            pltpu.SemaphoreType.DMA((6, 4)),
            pltpu.SemaphoreType.DMA((6, Gather.count(n))),
            pltpu.SemaphoreType.DMA((6, Gather.count(n))),
            pltpu.SemaphoreType.DMA((n,)),
            pltpu.SemaphoreType.DMA((n,)),
        ],
        compiler_params=pltpu.CompilerParams(collective_id=0, has_side_effects=True),
        name="gather_weights",
    )(qkv, ao, win, wout, small)


class Reduce:
    def __init__(self, place, by_shard, slot, landing, local, send, recv):
        self.place, self.by_shard = place, by_shard
        self.half_in, self.plane_out, self.total = slot
        self.core_in, self.ring_in, self.plane_in = landing
        self.local, self.send, self.recv = local, send, recv
        self.n, self.ny = place.n, place.ny
        self.half = self.half_in.shape[2]
        self.copies, self.owns = [], []
        self.rings, self.planes = {}, {}

    @staticmethod
    def count(n, ny):
        return 4 + n + 2 * ny + 4

    @staticmethod
    def slot_buffers(n):
        half = D // n // 2
        return [pltpu.VMEM((n, 4, half, D), BF), pltpu.VMEM((2, 4, half, D), BF), pltpu.VMEM((4, half, D), F32)]

    @staticmethod
    def landing_buffers(n, ny):
        half = D // n // 2
        return [
            pltpu.VMEM((n, 4, half, D), BF),
            pltpu.VMEM((2, n // 2, 4, half, D), BF),
            pltpu.VMEM((2 * ny, 2, half, D), BF),
        ]

    def parts_of(self, grad, k):
        rows = pl.ds(pl.multiple_of(k * self.half, self.half), self.half)
        if self.by_shard:
            return [(pl.ds(0, 4), grad.at[:, :, rows])]
        return [(q, grad.at[q, :, rows]) for q in range(4)]

    def load(self, grad):
        self.loaded = []
        for i, (q, part) in enumerate(self.parts_of(grad, self.place.k)):
            copy = pltpu.make_async_copy(part, self.half_in.at[:, q], self.local.at[4 + i])
            copy.start()
            self.loaded.append(copy)

    def core(self, grad):
        self.cored = []
        for i, (q, part) in enumerate(self.parts_of(grad, 1 - self.place.k)):
            copy = remote(
                part, self.core_in.at[:, q], self.send.at[i], self.recv.at[i], self.place.at(dk=1)
            )
            self.cored.append(copy)
            self.copies.append(copy)

    def ring_send(self, d):
        place, n = self.place, self.n
        for sign in (1, -1):
            way = 0 if sign == 1 else 1
            shard = place.shard(sign * d)
            if d == n // 2:
                q0, count = 2 * way, 2
            else:
                q0, count = 0, 4
            slot = 4 + way * (n // 2) + d - 1
            copy = remote(
                self.half_in.at[shard, pl.ds(q0, count)],
                self.ring_in.at[way, d - 1, pl.ds(q0, count)],
                self.send.at[slot],
                self.recv.at[slot],
                place.at(dz=sign),
            )
            self.rings[(way, d)] = copy
            self.copies.append(copy)

    def add_into(self, target, source):
        target[...] = (target[...].astype(F32) + source[...].astype(F32)).astype(BF)

    def add_cores(self):
        for copy in self.loaded:
            copy.wait()
        for copy in self.cored:
            copy.wait_recv()

        def one(i, _):
            shard, q = lax.div(i, 4), lax.rem(i, 4)
            self.add_into(self.half_in.at[shard, q], self.core_in.at[shard, q])
            return 0

        lax.fori_loop(0, 4 * self.n, one, 0)
        self.ring_send(self.n // 2)

    def ring_step(self, d):
        place, n = self.place, self.n
        for sign in (1, -1):
            way = 0 if sign == 1 else 1
            self.rings[(way, d + 1)].wait_recv()
            shard = place.shard(sign * d)
            qs = range(4) if d + 1 < n // 2 else range(2 * way, 2 * way + 2)
            for q in qs:
                self.add_into(self.half_in.at[shard, q], self.ring_in.at[way, d, q])
        self.ring_send(d)

    def ring_end(self):
        place = self.place
        for way in (0, 1):
            self.rings[(way, 1)].wait_recv()
        for q in range(4):
            total = self.half_in[place.z, q].astype(F32)
            for way in (0, 1):
                if self.n > 2 or q // 2 == way:
                    total = total + self.ring_in[way, 0, q].astype(F32)
            self.plane_out[0, q] = total.astype(BF)
        self.plane_send(0)

    def plane_send(self, turn):
        place, ny = self.place, self.ny
        base = 4 + self.n + turn * ny
        slot = base
        qx = 2 * turn
        copy = remote(
            self.plane_out.at[turn, pl.ds(qx, 2)],
            self.plane_in.at[turn * ny],
            self.send.at[slot],
            self.recv.at[slot],
            place.at(dr=1),
        )
        self.planes[(turn, 0)] = copy
        self.copies.append(copy)
        for o in range(1, ny):
            copy = remote(
                self.plane_out.at[turn, pl.ds(2 - qx, 2)],
                self.plane_in.at[turn * ny + o],
                self.send.at[slot + o],
                self.recv.at[slot + o],
                place.at(dy=o),
            )
            self.planes[(turn, o)] = copy
            self.copies.append(copy)

    def plane_sum(self, turn, q):
        place, ny = self.place, self.ny
        over_x = (q // 2 == 0) == (turn == 0)
        own = self.plane_out[turn, q].astype(F32)
        if over_x:
            return own + self.plane_in[turn * ny, q % 2].astype(F32)
        if ny == 2:
            return own + self.plane_in[turn * ny + 1, q % 2].astype(F32)
        terms = [own] + [self.plane_in[turn * ny + o, q % 2].astype(F32) for o in range(1, ny)]
        total = jnp.zeros_like(own)
        for y in range(ny):
            offset = lax.rem(place.y - y + ny, ny)
            for o in range(ny):
                total = total + jnp.where(offset == o, terms[o], 0.0)
        return total

    def plane_mid(self):
        for o in range(self.ny):
            self.planes[(0, o)].wait_recv()
        for q in range(4):
            self.plane_out[1, q] = self.plane_sum(0, q).astype(BF)
        self.plane_send(1)

    def plane_end(self):
        for o in range(self.ny):
            self.planes[(1, o)].wait_recv()
        for q in range(4):
            self.total[q] = self.plane_sum(1, q)

    def deliver(self, targets):
        place = self.place
        base = 4 + self.n + 2 * self.ny
        self.outs = []
        for i, (q, count, target) in enumerate(targets):
            source = self.total.at[q] if count is None else self.total.at[pl.ds(q, count)]
            copy = remote(source, target, self.send.at[base + i], self.recv.at[base + i], place.at(dk=1))
            self.copies.append(copy)
            self.outs.append(copy)
            own = pltpu.make_async_copy(source, target, self.local.at[i])
            own.start()
            self.owns.append(own)

    def finish(self):
        for copy in self.outs:
            copy.wait_recv()

    def drain(self):
        for copy in self.copies:
            copy.wait_send()
        for copy in self.owns:
            copy.wait()


class SmallReduce:
    def __init__(self, place, total, landing, send, recv):
        self.place, self.total, self.landing, self.send, self.recv = place, total, landing, send, recv
        n, ny = place.n, place.ny
        self.stages = [
            [place.at(dk=1)],
            [place.at(dz=o) for o in range(1, n)],
            [place.at(dr=1)],
            [place.at(dy=o) for o in range(1, ny)],
        ]
        self.copies = []
        self.slot = 0

    @staticmethod
    def count(n, ny):
        return 1 + (n - 1) + 1 + (ny - 1)

    def start(self, stage):
        self.current = []
        for device in self.stages[stage]:
            slot = self.slot
            copy = remote(
                self.total.at[stage], self.landing.at[slot], self.send.at[slot], self.recv.at[slot], device
            )
            self.current.append((slot, copy))
            self.copies.append(copy)
            self.slot += 1

    def end(self, stage):
        place, ny = self.place, self.place.ny
        for _, copy in self.current:
            copy.wait_recv()
        terms = [self.total[stage]] + [self.landing[slot] for slot, _ in self.current]
        if stage == 3 and ny > 2:
            total = jnp.zeros_like(terms[0])
            for y in range(ny):
                offset = lax.rem(place.y - y + ny, ny)
                for o in range(ny):
                    total = total + jnp.where(offset == o, terms[o], 0.0)
        else:
            total = functools.reduce(lambda a, b: a + b, terms)
        self.total[stage + 1] = total

    def steps(self):
        out = [functools.partial(self.start, 0)]
        for stage in range(4):
            out.append(functools.partial(self.end, stage))
            if stage < 3:
                out.append(functools.partial(self.start, stage + 1))
        return out


SLOTS = 3


def reduce_kernel(n, ny, *refs):
    grads, small = refs[:6], refs[6]
    out_qkv, out_ao, out_in, out_out, out_small = refs[7:12]
    bufs = refs[12:]
    slots = [bufs[3 * s : 3 * s + 3] for s in range(SLOTS)]
    bufs = bufs[3 * SLOTS :]
    landings = [bufs[3 * g : 3 * g + 3] for g in range(6)]
    small_total, small_landing, local, send, recv, small_send, small_recv = bufs[18:]
    place = Place(n, ny)
    half = D // n // 2
    mine = pl.ds(pl.multiple_of(place.k * half, half), half)
    small_total[0] = small[...]
    order = [5, 4, 3, 2, 1, 0]
    groups = {}
    for i, g in enumerate(order):
        groups[g] = Reduce(
            place, g % 3 == 2, slots[i % SLOTS], landings[g], local.at[g], send.at[g], recv.at[g]
        )
    place.greet(place.everyone())
    for g in order:
        groups[g].core(grads[g])

    def targets(g):
        b, kind = g // 3, g % 3
        if kind == 0:
            return [(0, 3, out_qkv.at[b, :, mine]), (3, None, out_ao.at[b, mine])]
        if kind == 1:
            return [(q, None, out_in.at[b, mine, pl.ds(q * D, D)]) for q in range(4)]
        return [(0, 4, out_out.at[b, :, mine])]

    def begin(i):
        if i >= SLOTS:
            groups[order[i - SLOTS]].drain()
        groups[order[i]].load(grads[order[i]])

    def end(g):
        groups[g].plane_end()
        groups[g].deliver(targets(g))

    def steps(i):
        g = order[i]
        group = groups[g]
        out = [functools.partial(begin, i), group.add_cores]
        out += [functools.partial(group.ring_step, d) for d in range(n // 2 - 1, 0, -1)]
        out += [group.ring_end, group.plane_mid, functools.partial(end, g)]
        return out

    small_sum = SmallReduce(place, small_total, small_landing, small_send, small_recv)
    plans = [steps(i) for i in range(6)]
    length = len(plans[0])
    gap = max(1, -(-(length + 1) // SLOTS))
    small_steps = small_sum.steps()
    for t in range(length + gap * 5):
        for i in range(6):
            at = t - gap * i
            if 0 <= at < length:
                plans[i][at]()
        if small_steps:
            small_steps.pop(0)()
    while small_steps:
        small_steps.pop(0)()
    out_small[...] = small_total[4]
    for i, g in enumerate(order):
        groups[g].finish()
        if i >= 6 - SLOTS:
            groups[g].drain()
    for copy in small_sum.copies:
        copy.wait_send()


def reduce_grads(n, ny, grads, small):
    rows = D // n
    out = [
        jax.ShapeDtypeStruct((2, 3, rows, D), F32),
        jax.ShapeDtypeStruct((2, rows, D), F32),
        jax.ShapeDtypeStruct((2, rows, 4 * D), F32),
        jax.ShapeDtypeStruct((2, 4, rows, D), F32),
        jax.ShapeDtypeStruct(small.shape, F32),
    ]
    anywhere = pl.BlockSpec(memory_space=pl.ANY)
    vmem = pl.BlockSpec(memory_space=pltpu.VMEM)
    scratch = []
    for s in range(SLOTS):
        scratch += Reduce.slot_buffers(n)
    for g in range(6):
        scratch += Reduce.landing_buffers(n, ny)
    smalls = SmallReduce.count(n, ny)
    scratch += [
        pltpu.VMEM((5,) + small.shape, F32),
        pltpu.VMEM((smalls,) + small.shape, F32),
        pltpu.SemaphoreType.DMA((6, 8)),
        pltpu.SemaphoreType.DMA((6, Reduce.count(n, ny))),
        pltpu.SemaphoreType.DMA((6, Reduce.count(n, ny))),
        pltpu.SemaphoreType.DMA((smalls,)),
        pltpu.SemaphoreType.DMA((smalls,)),
    ]
    return pl.pallas_call(
        functools.partial(reduce_kernel, n, ny),
        out_shape=out,
        in_specs=[anywhere] * 6 + [vmem],
        out_specs=[anywhere] * 4 + [vmem],
        scratch_shapes=scratch,
        compiler_params=pltpu.CompilerParams(
            collective_id=1, has_side_effects=True, vmem_limit_bytes=60 * MIB
        ),
        name="reduce_grads",
    )(*grads, small)


def layer_norm(operand, scale_row, shift_row):
    center = operand - jnp.mean(operand, axis=-1, keepdims=True)
    variance = jnp.mean(center * center, axis=-1, keepdims=True)
    return center * lax.rsqrt(variance + epsilon) * scale_row + shift_row


def matmul(operand_a, operand_b):
    return jnp.dot(operand_a, operand_b, preferred_element_type=jnp.float32)


def matmul_left_t(operand_a, operand_b):
    return lax.dot_general(
        operand_a, operand_b, (((0,), (0,)), ((), ())), preferred_element_type=jnp.float32
    )


def matmul_right_t(operand_a, operand_b):
    return lax.dot_general(
        operand_a, operand_b, (((1,), (1,)), ((), ())), preferred_element_type=jnp.float32
    )


def head_slices(matrix, group_idx, row_count):
    piece_cols = lax.dynamic_slice_in_dim(matrix, group_idx * (2 * HEAD), 2 * HEAD, 1)
    return piece_cols.reshape(row_count, 2, HEAD)


def group_scores(query_part, key_part, key_ok):
    scores = (
        jnp.einsum("qhd,khd->hqk", query_part, key_part, preferred_element_type=jnp.float32)
        * score_scale
    )
    return jnp.where(key_ok[None, None, :], scores, masked_value)


def attend_forward(queries, key_all, value_all, key_ok):
    row_count = queries.shape[0]
    key_count = key_all.shape[0]

    def per_group(group_idx):
        query_part = head_slices(queries, group_idx, row_count)
        key_part = head_slices(key_all, group_idx, key_count)
        value_part = head_slices(value_all, group_idx, key_count)
        scores = group_scores(query_part, key_part, key_ok)
        peak = jnp.max(scores, axis=-1, keepdims=True)
        shifted_exp = jnp.exp(scores - peak)
        summed = jnp.sum(shifted_exp, axis=-1, keepdims=True)
        probs = (shifted_exp / summed).astype(jnp.bfloat16)
        mixed = jnp.einsum("hqk,khd->qhd", probs, value_part, preferred_element_type=jnp.float32)
        log_sum = peak[..., 0] + jnp.log(summed[..., 0])
        return (mixed.reshape(row_count, 2 * HEAD), log_sum)

    mixed, log_sum = lax.map(per_group, jnp.arange(HEADS // 2))
    return (mixed.transpose(1, 0, 2).reshape(row_count, HEADS * HEAD), log_sum)


def attend_backward(queries, key_all, value_all, key_ok, grad_mixed, log_sum):
    row_count = queries.shape[0]
    key_count = key_all.shape[0]

    def per_group(items):
        group_idx, group_lse = items
        query_part = head_slices(queries, group_idx, row_count)
        key_part = head_slices(key_all, group_idx, key_count)
        value_part = head_slices(value_all, group_idx, key_count)
        grad_part = head_slices(grad_mixed, group_idx, row_count)
        scores = group_scores(query_part, key_part, key_ok)
        probs = jnp.exp(scores - group_lse[..., None])
        grad_probs = jnp.einsum(
            "qhd,khd->hqk", grad_part, value_part, preferred_element_type=jnp.float32
        )
        inner = jnp.sum(probs * grad_probs, axis=-1, keepdims=True)
        grad_scores = (probs * (grad_probs - inner)).astype(jnp.bfloat16)
        grad_query = (
            jnp.einsum("hqk,khd->qhd", grad_scores, key_part, preferred_element_type=jnp.float32)
            * score_scale
        )
        grad_key = (
            jnp.einsum("hqk,qhd->khd", grad_scores, query_part, preferred_element_type=jnp.float32)
            * score_scale
        )
        grad_value = jnp.einsum(
            "hqk,qhd->khd",
            probs.astype(jnp.bfloat16),
            grad_part,
            preferred_element_type=jnp.float32,
        )
        return (
            grad_query.reshape(row_count, 2 * HEAD),
            grad_key.reshape(key_count, 2 * HEAD),
            grad_value.reshape(key_count, 2 * HEAD),
        )

    grad_query, grad_key, grad_value = lax.map(per_group, (jnp.arange(HEADS // 2), log_sum))
    grad_query = grad_query.transpose(1, 0, 2).reshape(row_count, HEADS * HEAD)
    grad_key = grad_key.transpose(1, 0, 2).reshape(key_count, HEADS * HEAD)
    grad_value = grad_value.transpose(1, 0, 2).reshape(key_count, HEADS * HEAD)
    return (grad_query, grad_key, grad_value)


def block_forward(inputs, weights_full, length):
    qkv_mats, out_mat, in_mat, down_mat, query_bias, bias_rows, ffn_bias, gains, shifts = (
        weights_full
    )
    gains_f = gains.astype(jnp.float32)
    shifts_f = shifts.astype(jnp.float32)
    rounded = inputs.astype(jnp.bfloat16)
    queries = (matmul(rounded, qkv_mats[0]) + query_bias.astype(jnp.float32)).astype(jnp.bfloat16)
    key_rows = matmul(rounded, qkv_mats[1]).astype(jnp.bfloat16)
    value_rows = (matmul(rounded, qkv_mats[2]) + bias_rows[0].astype(jnp.float32)).astype(
        jnp.bfloat16
    )
    key_all, value_all = (
        lax.all_gather(key_rows, "ctx", axis=0, tiled=True),
        lax.all_gather(value_rows, "ctx", axis=0, tiled=True),
    )
    key_ok = jnp.arange(key_all.shape[0]) < length
    mixed_sum, log_sum = attend_forward(queries, key_all, value_all, key_ok)
    mixed = mixed_sum.astype(jnp.bfloat16)
    first_sum = inputs + matmul(mixed, out_mat) + bias_rows[1].astype(jnp.float32)
    normed = layer_norm(first_sum, gains_f[0], shifts_f[0])
    hidden = jnp.concatenate([matmul(normed.astype(jnp.bfloat16), in_mat[q]) for q in range(4)], axis=1)
    hidden = hidden + ffn_bias.astype(jnp.float32)
    active = jax.nn.gelu(hidden, approximate=False).astype(jnp.bfloat16)
    second_sum = normed + matmul(active, down_mat) + bias_rows[2].astype(jnp.float32)
    output = layer_norm(second_sum, gains_f[1], shifts_f[1])
    kept_acts = (
        rounded,
        queries,
        key_all,
        value_all,
        key_ok,
        mixed,
        log_sum,
        first_sum,
        normed,
        hidden,
        active,
        second_sum,
    )
    return (output, kept_acts)


def block_backward(grad_output, weights_full, kept_acts):
    qkv_mats, out_mat, in_mat, down_mat, query_bias, bias_rows, ffn_bias, gains, shifts = (
        weights_full
    )
    (
        rounded,
        queries,
        key_all,
        value_all,
        key_ok,
        mixed,
        log_sum,
        first_sum,
        normed,
        hidden,
        active,
        second_sum,
    ) = kept_acts
    gains_f = gains.astype(jnp.float32)
    shifts_f = shifts.astype(jnp.float32)
    unused_second, pull_second = jax.vjp(layer_norm, second_sum, gains_f[1], shifts_f[1])
    grad_second, grad_gain_two, grad_shift_two = pull_second(grad_output)
    grad_update = grad_second.astype(jnp.bfloat16)
    grad_down = matmul_left_t(active, grad_update)
    grad_bias_three = jnp.sum(grad_update.astype(jnp.float32), axis=0)
    grad_active = matmul_right_t(grad_update, down_mat)
    unused_gelu, pull_gelu = jax.vjp(
        lambda pre_act: jax.nn.gelu(pre_act, approximate=False), hidden
    )
    grad_hidden = pull_gelu(grad_active)[0].astype(jnp.bfloat16)
    normed_bf = normed.astype(jnp.bfloat16)
    grad_in = jnp.stack([matmul_left_t(normed_bf, grad_hidden[:, q * D : q * D + D]) for q in range(4)])
    grad_ffn_bias = jnp.sum(grad_hidden.astype(jnp.float32), axis=0)
    grad_normed = grad_second + sum(
        matmul_right_t(grad_hidden[:, q * D : q * D + D], in_mat[q]) for q in range(4)
    )
    unused_first, pull_first = jax.vjp(layer_norm, first_sum, gains_f[0], shifts_f[0])
    grad_first, grad_gain_one, grad_shift_one = pull_first(grad_normed)
    grad_branch = grad_first.astype(jnp.bfloat16)
    grad_out_mat = matmul_left_t(mixed, grad_branch)
    grad_bias_two = jnp.sum(grad_branch.astype(jnp.float32), axis=0)
    grad_mixed = matmul_right_t(grad_branch, out_mat).astype(jnp.bfloat16)
    grad_query, grad_key_all, grad_value_all = attend_backward(
        queries, key_all, value_all, key_ok, grad_mixed, log_sum
    )
    grad_key, grad_value = (
        lax.psum_scatter(
            grad_key_all.astype(jnp.bfloat16), "ctx", scatter_dimension=0, tiled=True
        ).astype(jnp.float32),
        lax.psum_scatter(
            grad_value_all.astype(jnp.bfloat16), "ctx", scatter_dimension=0, tiled=True
        ).astype(jnp.float32),
    )
    grad_query = grad_query.astype(jnp.bfloat16)
    grad_key = grad_key.astype(jnp.bfloat16)
    grad_value = grad_value.astype(jnp.bfloat16)
    grad_qkv = jnp.stack(
        [
            matmul_left_t(rounded, grad_query),
            matmul_left_t(rounded, grad_key),
            matmul_left_t(rounded, grad_value),
        ],
        axis=0,
    )
    grad_query_bias = jnp.sum(grad_query.astype(jnp.float32), axis=0)
    grad_bias_value = jnp.sum(grad_value.astype(jnp.float32), axis=0)
    grad_inputs = (
        grad_first
        + matmul_right_t(grad_query, qkv_mats[0])
        + matmul_right_t(grad_key, qkv_mats[1])
        + matmul_right_t(grad_value, qkv_mats[2])
    )
    mats = (
        jnp.concatenate([grad_qkv, grad_out_mat[None]], axis=0).astype(jnp.bfloat16),
        grad_in.astype(jnp.bfloat16),
        grad_down.astype(jnp.bfloat16),
    )
    rows = jnp.stack(
        [
            grad_query_bias,
            grad_bias_value,
            grad_bias_two,
            grad_bias_three,
            grad_gain_one,
            grad_gain_two,
            grad_shift_one,
            grad_shift_two,
        ]
    )
    small = jnp.concatenate([rows, grad_ffn_bias.reshape(4, D)], axis=0)
    grads_block = (mats, small)
    return (grad_inputs, grads_block)


def body(
    tokens,
    lengths,
    cotangent,
    w_qkv,
    w_attn_out,
    w_in,
    w_out,
    bias_q,
    bias_d,
    bias_ff,
    norm_gain,
    norm_shift,
    n,
    ny,
):
    length = lengths[0]
    row_count = tokens.shape[1]
    width = D // n
    first_row = lax.axis_index("ctx") * row_count
    valid_rows = (first_row + jnp.arange(row_count) < length).astype(jnp.float32)
    small = jnp.concatenate(
        [
            bias_q,
            bias_d.reshape(6, width),
            norm_gain.reshape(4, width),
            norm_shift.reshape(4, width),
            bias_ff.reshape(8, width),
            jnp.zeros((8, width), BF),
        ],
        axis=0,
    )
    gathered = gather_weights(
        n, ny, w_qkv, w_attn_out, w_in, w_out.reshape(2, 4, width, D), small
    )
    fulls, small_full = gathered[:6], gathered[6]
    narrow = small_full[:, :16].transpose(1, 0, 2).reshape(16, D)
    ff = small_full[:, 16:24].reshape(n, 2, 4 * width).transpose(1, 0, 2).reshape(2, 4 * D)
    weights = []
    for b in range(2):
        first = fulls[3 * b].reshape(4, D, D)
        weights.append(
            (
                first[:3],
                first[3],
                fulls[3 * b + 1].reshape(4, D, D),
                fulls[3 * b + 2].reshape(4 * D, D),
                narrow[b],
                narrow[2 + 3 * b : 5 + 3 * b],
                ff[b],
                narrow[8 + 2 * b : 10 + 2 * b],
                narrow[12 + 2 * b : 14 + 2 * b],
            )
        )
    carried = tokens[0].astype(jnp.float32)
    kept_layers = []
    for layer_idx in range(2):
        carried, kept_acts = block_forward(carried, weights[layer_idx], length)
        kept_layers.append(kept_acts)
    output_tokens = carried.astype(jnp.bfloat16)[None]
    grad_carried = cotangent[0].astype(jnp.float32) * valid_rows[:, None]
    grads = [None] * 6
    smalls = [None, None]
    for layer_idx in (1, 0):
        grad_carried, (mats, smalls[layer_idx]) = block_backward(
            grad_carried, weights[layer_idx], kept_layers[layer_idx]
        )
        grads[3 * layer_idx] = mats[0].reshape(4, n, width, D)
        grads[3 * layer_idx + 1] = mats[1].reshape(4, n, width, D)
        grads[3 * layer_idx + 2] = mats[2].reshape(n, 4, width, D)
    small_grads = jnp.concatenate(smalls, axis=0)
    out_qkv, out_ao, out_in, out_out, small_sum = reduce_grads(n, ny, grads, small_grads)
    z = lax.axis_index("fsdp")
    small_sum = small_sum.reshape(2, 12, D)
    own = lax.dynamic_slice_in_dim(small_sum, z * width, width, 2)
    own_ff = lax.dynamic_slice_in_dim(small_sum[:, 8:].reshape(2, 4 * D), z * 4 * width, 4 * width, 1)
    return (
        output_tokens,
        grad_carried[None],
        out_qkv,
        out_ao,
        out_in,
        out_out.reshape(2, 4 * width, D),
        own[:, 0],
        own[:, 1:4],
        own_ff,
        own[:, 4:6],
        own[:, 6:8],
    )


def solution(mesh):
    placed = (
        P(("rep", "fsdp"), "ctx", None),
        P(("rep", "fsdp")),
        P(("rep", "fsdp"), "ctx", None),
        P(None, None, "fsdp", None),
        P(None, "fsdp", None),
        P(None, "fsdp", None),
        P(None, "fsdp", None),
        P(None, "fsdp"),
        P(None, None, "fsdp"),
        P(None, "fsdp"),
        P(None, None, "fsdp"),
        P(None, None, "fsdp"),
    )
    n, ny = mesh.shape["fsdp"], mesh.shape["ctx"] // 2
    return jax.shard_map(
        functools.partial(body, n=n, ny=ny),
        mesh=mesh,
        in_specs=placed,
        out_specs=(
            P(("rep", "fsdp"), "ctx", None),
            P(("rep", "fsdp"), "ctx", None),
            P(None, None, "fsdp", None),
            P(None, "fsdp", None),
            P(None, "fsdp", None),
            P(None, "fsdp", None),
            P(None, "fsdp"),
            P(None, None, "fsdp"),
            P(None, "fsdp"),
            P(None, None, "fsdp"),
            P(None, None, "fsdp"),
        ),
        check_vma=False,
    )
```

```python
import functools

import jax
import jax.numpy as jnp
from jax import lax
from jax.experimental import pallas as pl
from jax.experimental.pallas import tpu as pltpu
from jax.sharding import PartitionSpec as P

HEADS = 12
HEAD = 64
D = HEADS * HEAD
MESH = pl.DeviceIdType.MESH
BF = jnp.bfloat16
F32 = jnp.float32
MIB = 2**20

epsilon = 1e-05
score_scale = 0.125
masked_value = -1e30


class Place:
    def __init__(self, n, ny):
        self.n, self.ny = n, ny
        self.r = lax.axis_index("rep")
        self.z = lax.axis_index("fsdp")
        self.c = lax.axis_index("ctx")
        self.y, self.k = lax.div(self.c, 2), lax.rem(self.c, 2)
        self.e = lax.rem(self.y, 2)
        self.q = 2 * self.e + self.r
        self.qx = 2 * self.e + (1 - self.r)
        self.qy = 2 * (1 - self.e) + self.r
        self.qd = 2 * (1 - self.e) + (1 - self.r)

    def shard(self, offset):
        return lax.rem(self.z + (offset + self.n), self.n)

    def up(self, offset):
        return (self.r, self.shard(offset), self.c)

    def x(self):
        return (1 - self.r, self.z, self.c)

    def across(self):
        return (self.r, self.z, 2 * (self.y + 1 - 2 * self.e) + self.k)

    def row(self, offset, flip=0):
        y = lax.rem(self.y + offset, self.ny)
        k = self.k + flip * (1 - 2 * self.k)
        return (self.r, self.z, 2 * y + k)

    def core(self):
        return self.row(0, 1)

    def greet(self):
        others = [self.up(o) for o in range(1, self.n)]
        others += [self.x(), self.core()]
        others += [self.row(o) for o in range(1, self.ny)]
        barrier = pltpu.get_barrier_semaphore()
        for other in others:
            pl.semaphore_signal(barrier, inc=1, device_id=other, device_id_type=MESH)
        pl.semaphore_wait(barrier, len(others))


def remote(src, dst, send, recv, device):
    copy = pltpu.make_async_remote_copy(
        src_ref=src, dst_ref=dst, send_sem=send, recv_sem=recv, device_id=device, device_id_type=MESH
    )
    copy.start()
    return copy


def halves(half):
    first = -(-half // 32) * 16
    return [(0, first), (first, half - first)]


class Gather:
    def __init__(self, place, full, by_shard, local, send, recv):
        self.place, self.full, self.by_shard = place, full, by_shard
        self.local, self.send, self.recv = local, send, recv
        self.n = place.n
        self.half = full.shape[2] // 2
        self.pieces = halves(self.half)
        self.copies, self.core_copies = [], []

    @staticmethod
    def count(n):
        return 10 * (n - 1)

    def part(self, shard, q, piece=None):
        start, size = (0, self.half) if piece is None else piece
        rows = pl.ds(pl.multiple_of(self.place.k * self.half + start, 8), size)
        return self.full.at[shard, q, rows] if self.by_shard else self.full.at[q, shard, rows]

    def load(self, sources):
        self.loads = []
        z = self.place.z
        for i, (q, count, source) in enumerate(sources):
            if self.by_shard:
                target = self.full.at[z]
            elif count is None:
                target = self.full.at[q, z]
            else:
                target = self.full.at[pl.ds(q, count), z]
            copy = pltpu.make_async_copy(source, target, self.local.at[i])
            copy.start()
            self.loads.append(copy)

    def share(self, kind, offset, piece, device):
        slot = kind * (self.n - 1) + offset - 1
        copy = remote(piece, piece, self.send.at[slot], self.recv.at[slot], device)
        self.copies.append(copy)
        return copy

    def core_share(self, kind, offset, piece):
        copy = self.share(5 + kind, offset, piece, self.place.core())
        self.core_copies.append(copy)

    def start(self):
        place = self.place
        for copy in self.loads:
            copy.wait()
        mine = self.part(place.z, place.q)
        self.ups = [self.share(0, o, mine, place.up(o)) for o in range(1, self.n)]

    def plane(self):
        place = self.place
        self.xs, self.ys = [], []
        for o in range(1, self.n):
            self.ups[o - 1].wait_recv()
            piece = self.part(place.shard(-o), place.q)
            self.xs.append(self.share(1, o, piece, place.x()))
            self.ys.append(self.share(2, o, piece, place.across()))
            self.core_share(0, o, piece)

    def diagonal(self):
        place = self.place
        self.dys, self.dxs = [], []
        for o in range(1, self.n):
            shard = place.shard(-o)
            self.xs[o - 1].wait_recv()
            self.dys.append(self.share(3, o, self.part(shard, place.qx, self.pieces[0]), place.across()))
            self.core_share(1, o, self.part(shard, place.qx))
            self.ys[o - 1].wait_recv()
            self.dxs.append(self.share(4, o, self.part(shard, place.qy, self.pieces[1]), place.x()))
            self.core_share(2, o, self.part(shard, place.qy))

    def last(self):
        place = self.place
        for o in range(1, self.n):
            shard = place.shard(-o)
            self.dys[o - 1].wait_recv()
            self.core_share(3, o, self.part(shard, place.qd, self.pieces[0]))
            self.dxs[o - 1].wait_recv()
            self.core_share(4, o, self.part(shard, place.qd, self.pieces[1]))

    def finish(self):
        for copy in self.core_copies:
            copy.wait_recv()

    def drain(self):
        for copy in self.copies:
            copy.wait_send()

    def steps(self):
        return [self.start, self.plane, self.diagonal, self.last, self.finish]


def weight_sources(b, qkv, ao, win, wout):
    return [
        [(0, 3, qkv.at[b]), (3, None, ao.at[b])],
        [(q, None, win.at[b, :, pl.ds(q * D, D)]) for q in range(4)],
        [(None, None, wout.at[b])],
    ]


def gather_kernel(n, ny, *refs):
    qkv, ao, win, wout, small = refs[:5]
    outs, small_full = refs[5:11], refs[11]
    fulls = refs[12:18]
    local, send, recv, small_send, small_recv = refs[18:]
    place = Place(n, ny)
    groups = []
    for g in range(6):
        b, kind = g // 3, g % 3
        group = Gather(place, fulls[g], kind == 2, local.at[g], send.at[g], recv.at[g])
        group.load(weight_sources(b, qkv, ao, win, wout)[kind])
        groups.append(group)
    own = pltpu.make_async_copy(small, small_full.at[place.z], small_send.at[0])
    own.start()
    place.greet()
    smalls = [
        remote(small, small_full.at[place.z], small_send.at[o], small_recv.at[o], place.up(o))
        for o in range(1, n)
    ]
    steps = [group.steps() for group in groups]
    kept = []
    for t in range(len(steps[0]) + 5):
        for g in range(6):
            if 0 <= t - g < len(steps[g]):
                steps[g][t - g]()
                if t - g == len(steps[g]) - 1:
                    copy = pltpu.make_async_copy(fulls[g], outs[g], local.at[g, 4])
                    copy.start()
                    kept.append(copy)
    for group in groups:
        group.drain()
    for copy in kept:
        copy.wait()
    own.wait()
    for copy in smalls:
        copy.wait()


def gather_weights(n, ny, qkv, ao, win, wout, small):
    rows = D // n
    shapes = [(4, n, rows, D), (4, n, rows, D), (n, 4, rows, D)] * 2
    out = [jax.ShapeDtypeStruct(shape, BF) for shape in shapes]
    out.append(jax.ShapeDtypeStruct((n,) + small.shape, BF))
    anywhere = pl.BlockSpec(memory_space=pl.ANY)
    return pl.pallas_call(
        functools.partial(gather_kernel, n, ny),
        out_shape=out,
        in_specs=[anywhere] * 5,
        out_specs=[anywhere] * 7,
        scratch_shapes=[pltpu.VMEM(shape, BF) for shape in shapes]
        + [
            pltpu.SemaphoreType.DMA((6, 5)),
            pltpu.SemaphoreType.DMA((6, Gather.count(n))),
            pltpu.SemaphoreType.DMA((6, Gather.count(n))),
            pltpu.SemaphoreType.DMA((n,)),
            pltpu.SemaphoreType.DMA((n,)),
        ],
        compiler_params=pltpu.CompilerParams(
            collective_id=0, has_side_effects=True, vmem_limit_bytes=40 * MIB
        ),
        name="gather_weights",
    )(qkv, ao, win, wout, small)


class Reduce:
    def __init__(self, place, by_shard, slot, landing, out, local, send, recv):
        self.place, self.by_shard, self.out = place, by_shard, out
        (self.half_in,) = slot
        self.core_in, self.x_in, self.y_in, self.dx_in, self.dy_in, self.z_in, self.far_in = landing
        self.local, self.send, self.recv = local, send, recv
        self.n, self.ny = place.n, place.ny
        self.half = self.half_in.shape[2]
        self.pieces = halves(self.half)
        self.copies, self.owns = [], []
        self.slot = 0

    @staticmethod
    def count(n, ny):
        return 4 + 6 + (n - 1) + (ny // 2 - 1) + 9

    @staticmethod
    def slot_buffers(n):
        return [pltpu.VMEM((n, 4, D // n // 2, D), BF)]

    @staticmethod
    def landing_buffers(n, ny):
        half = D // n // 2
        (_, first), (_, second) = halves(half)
        return [
            pltpu.VMEM((n, 4, half, D), BF),
            pltpu.VMEM((n, half, D), BF),
            pltpu.VMEM((n, half, D), BF),
            pltpu.VMEM((n, first, D), BF),
            pltpu.VMEM((n, second, D), BF),
            pltpu.VMEM((n - 1, half, D), BF),
            pltpu.VMEM((max(1, ny // 2 - 1), half, D), BF),
        ]

    def share(self, src, dst, device):
        copy = remote(src, dst, self.send.at[self.slot], self.recv.at[self.slot], device)
        self.slot += 1
        self.copies.append(copy)
        return copy

    def parts_of(self, grad, k):
        rows = pl.ds(pl.multiple_of(k * self.half, self.half), self.half)
        if self.by_shard:
            return [(pl.ds(0, 4), grad.at[:, :, rows])]
        return [(q, grad.at[q, :, rows]) for q in range(4)]

    def load(self, grad):
        self.loaded = []
        for i, (q, part) in enumerate(self.parts_of(grad, self.place.k)):
            copy = pltpu.make_async_copy(part, self.half_in.at[:, q], self.local.at[i])
            copy.start()
            self.loaded.append(copy)

    def core(self, grad):
        self.cored = [
            self.share(part, self.core_in.at[:, q], self.place.core())
            for q, part in self.parts_of(grad, 1 - self.place.k)
        ]

    def add_into(self, target, *sources):
        total = target[...].astype(F32)
        for source in sources:
            total = total + source[...].astype(F32)
        target[...] = total.astype(BF)

    def add_cores(self):
        for copy in self.loaded:
            copy.wait()
        for copy in self.cored:
            copy.wait_recv()

        def one(i, _):
            shard, q = lax.div(i, 4), lax.rem(i, 4)
            self.add_into(self.half_in.at[shard, q], self.core_in.at[shard, q])
            return 0

        lax.fori_loop(0, 4 * self.n, one, 0)
        place = self.place
        (a, first), (b, second) = self.pieces
        top, low = pl.ds(a, first), pl.ds(b, second)
        self.dx = self.share(self.half_in.at[:, place.qd, top], self.dx_in, place.x())
        self.dy = self.share(self.half_in.at[:, place.qd, low], self.dy_in, place.across())
        self.planes = [
            self.share(self.half_in.at[:, place.qx, top], self.x_in.at[:, top], place.x()),
            self.share(self.half_in.at[:, place.qy, low], self.y_in.at[:, low], place.across()),
        ]

    def plane(self):
        place = self.place
        (a, first), (b, second) = self.pieces
        top, low = pl.ds(a, first), pl.ds(b, second)
        self.dx.wait_recv()

        def one(j, _):
            self.add_into(self.half_in.at[j, place.qy, top], self.dx_in.at[j])
            return 0

        lax.fori_loop(0, self.n, one, 0)
        self.planes.append(self.share(self.half_in.at[:, place.qy, top], self.y_in.at[:, top], place.across()))
        self.dy.wait_recv()

        def two(j, _):
            self.add_into(self.half_in.at[j, place.qx, low], self.dy_in.at[j])
            return 0

        lax.fori_loop(0, self.n, two, 0)
        self.planes.append(self.share(self.half_in.at[:, place.qx, low], self.x_in.at[:, low], place.x()))

    def depth(self):
        place = self.place
        for copy in self.planes:
            copy.wait_recv()

        def one(j, _):
            self.add_into(self.half_in.at[j, place.q], self.x_in.at[j], self.y_in.at[j])
            return 0

        lax.fori_loop(0, self.n, one, 0)
        self.deep = [
            self.share(self.half_in.at[place.shard(o), place.q], self.z_in.at[o - 1], place.up(o))
            for o in range(1, self.n)
        ]

    def mine(self, q, piece=None):
        start, size = (0, self.half) if piece is None else piece
        return self.out.at[q, pl.ds(pl.multiple_of(self.place.k * self.half + start, 8), size)]

    def total(self):
        place = self.place
        for copy in self.deep:
            copy.wait_recv()
        own = self.half_in.at[place.z, place.q]
        self.add_into(own, *[self.z_in.at[o - 1] for o in range(1, self.n)])
        if self.ny > 2:
            far = [self.share(own, self.far_in.at[i], place.row(2 * i + 2)) for i in range(self.ny // 2 - 1)]
            for copy in far:
                copy.wait_recv()
            mine = own[...].astype(F32)
            terms = [mine] + [self.far_in[i].astype(F32) for i in range(self.ny // 2 - 1)]
            total = jnp.zeros_like(mine)
            for y in range(0, self.ny, 2):
                offset = lax.rem(place.y - place.e - y + self.ny, self.ny)
                for i, term in enumerate(terms):
                    total = total + jnp.where(offset == 2 * i, term, 0.0)
            own[...] = total.astype(BF)
        copy = pltpu.make_async_copy(own, self.mine(place.q), self.local.at[4])
        copy.start()
        self.owns.append(copy)
        self.spread = [
            self.share(own, self.mine(place.q), place.x()),
            self.share(own, self.mine(place.q), place.across()),
        ]
        self.cores = [self.share(own, self.mine(place.q), place.core())]

    def forward(self, q, device, piece=None):
        return self.share(self.mine(q, piece), self.mine(q, piece), device)

    def turn(self):
        place = self.place
        self.spread[0].wait_recv()
        self.dy = self.forward(place.qx, place.across(), self.pieces[0])
        self.cores.append(self.forward(place.qx, place.core()))
        self.spread[1].wait_recv()
        self.dx = self.forward(place.qy, place.x(), self.pieces[1])
        self.cores.append(self.forward(place.qy, place.core()))

    def last(self):
        place = self.place
        self.dy.wait_recv()
        self.cores.append(self.forward(place.qd, place.core(), self.pieces[0]))
        self.dx.wait_recv()
        self.cores.append(self.forward(place.qd, place.core(), self.pieces[1]))

    def finish(self):
        for copy in self.cores:
            copy.wait_recv()

    def drain(self):
        for copy in self.copies:
            copy.wait_send()
        for copy in self.owns:
            copy.wait()

    def steps(self):
        return [self.add_cores, self.plane, self.depth, self.total, self.turn, self.last]


class SmallReduce:
    def __init__(self, place, total, landing, send, recv):
        self.place, self.total, self.landing, self.send, self.recv = place, total, landing, send, recv
        n, ny = place.n, place.ny
        self.stages = [
            [place.core()],
            [place.up(o) for o in range(1, n)],
            [place.x()],
            [place.row(o) for o in range(1, ny)],
        ]
        self.copies = []
        self.slot = 0

    @staticmethod
    def count(n, ny):
        return 1 + (n - 1) + 1 + (ny - 1)

    def start(self, stage):
        self.current = []
        for device in self.stages[stage]:
            slot = self.slot
            copy = remote(
                self.total.at[stage], self.landing.at[slot], self.send.at[slot], self.recv.at[slot], device
            )
            self.current.append((slot, copy))
            self.copies.append(copy)
            self.slot += 1

    def end(self, stage):
        place, ny = self.place, self.place.ny
        for _, copy in self.current:
            copy.wait_recv()
        terms = [self.total[stage]] + [self.landing[slot] for slot, _ in self.current]
        if stage == 3 and ny > 2:
            total = jnp.zeros_like(terms[0])
            for y in range(ny):
                offset = lax.rem(place.y - y + ny, ny)
                for o in range(ny):
                    total = total + jnp.where(offset == o, terms[o], 0.0)
        else:
            total = functools.reduce(lambda a, b: a + b, terms)
        self.total[stage + 1] = total

    def steps(self):
        out = [functools.partial(self.start, 0)]
        for stage in range(4):
            out.append(functools.partial(self.end, stage))
            if stage < 3:
                out.append(functools.partial(self.start, stage + 1))
        return out


SLOTS = 4


def reduce_kernel(n, ny, *refs):
    grads, small = refs[:6], refs[6]
    outs, out_small = refs[7:13], refs[13]
    bufs = refs[14:]
    slots = [bufs[s : s + 1] for s in range(SLOTS)]
    bufs = bufs[SLOTS:]
    landings = [bufs[7 * g : 7 * g + 7] for g in range(6)]
    small_total, small_landing, local, send, recv, small_send, small_recv = bufs[42:]
    place = Place(n, ny)
    small_total[0] = small[...]
    order = [5, 4, 3, 2, 1, 0]
    groups = {}
    for i, g in enumerate(order):
        groups[g] = Reduce(
            place, g % 3 == 2, slots[i % SLOTS], landings[g], outs[g], local.at[g], send.at[g], recv.at[g]
        )
    place.greet()
    for g in order:
        groups[g].core(grads[g])

    def begin(i):
        if i >= SLOTS:
            groups[order[i - SLOTS]].drain()
        groups[order[i]].load(grads[order[i]])

    small_sum = SmallReduce(place, small_total, small_landing, small_send, small_recv)
    plans = [[functools.partial(begin, i)] + groups[order[i]].steps() for i in range(6)]
    length = len(plans[0])
    gap = max(1, -(-length // SLOTS))
    small_steps = small_sum.steps()
    for t in range(length + gap * 5):
        for i in range(6):
            at = t - gap * i
            if 0 <= at < length:
                plans[i][at]()
        if small_steps:
            small_steps.pop(0)()
    while small_steps:
        small_steps.pop(0)()
    out_small[...] = small_total[4]
    for i, g in enumerate(order):
        groups[g].finish()
        if i >= 6 - SLOTS:
            groups[g].drain()
    for copy in small_sum.copies:
        copy.wait_send()


def reduce_grads(n, ny, grads, small):
    rows = D // n
    out = [jax.ShapeDtypeStruct((4, rows, D), BF)] * 6 + [jax.ShapeDtypeStruct(small.shape, F32)]
    anywhere = pl.BlockSpec(memory_space=pl.ANY)
    vmem = pl.BlockSpec(memory_space=pltpu.VMEM)
    scratch = []
    for s in range(SLOTS):
        scratch += Reduce.slot_buffers(n)
    for g in range(6):
        scratch += Reduce.landing_buffers(n, ny)
    smalls = SmallReduce.count(n, ny)
    scratch += [
        pltpu.VMEM((5,) + small.shape, F32),
        pltpu.VMEM((smalls,) + small.shape, F32),
        pltpu.SemaphoreType.DMA((6, 5)),
        pltpu.SemaphoreType.DMA((6, Reduce.count(n, ny))),
        pltpu.SemaphoreType.DMA((6, Reduce.count(n, ny))),
        pltpu.SemaphoreType.DMA((smalls,)),
        pltpu.SemaphoreType.DMA((smalls,)),
    ]
    return pl.pallas_call(
        functools.partial(reduce_kernel, n, ny),
        out_shape=out,
        in_specs=[anywhere] * 6 + [vmem],
        out_specs=[anywhere] * 6 + [vmem],
        scratch_shapes=scratch,
        compiler_params=pltpu.CompilerParams(
            collective_id=1, has_side_effects=True, vmem_limit_bytes=60 * MIB
        ),
        name="reduce_grads",
    )(*grads, small)


def layer_norm(operand, scale_row, shift_row):
    center = operand - jnp.mean(operand, axis=-1, keepdims=True)
    variance = jnp.mean(center * center, axis=-1, keepdims=True)
    return center * lax.rsqrt(variance + epsilon) * scale_row + shift_row


def matmul(operand_a, operand_b):
    return jnp.dot(operand_a, operand_b, preferred_element_type=jnp.float32)


def matmul_left_t(operand_a, operand_b):
    return lax.dot_general(
        operand_a, operand_b, (((0,), (0,)), ((), ())), preferred_element_type=jnp.float32
    )


def matmul_right_t(operand_a, operand_b):
    return lax.dot_general(
        operand_a, operand_b, (((1,), (1,)), ((), ())), preferred_element_type=jnp.float32
    )


def head_slices(matrix, group_idx, row_count):
    piece_cols = lax.dynamic_slice_in_dim(matrix, group_idx * (2 * HEAD), 2 * HEAD, 1)
    return piece_cols.reshape(row_count, 2, HEAD)


def group_scores(query_part, key_part, key_ok):
    scores = (
        jnp.einsum("qhd,khd->hqk", query_part, key_part, preferred_element_type=jnp.float32)
        * score_scale
    )
    return jnp.where(key_ok[None, None, :], scores, masked_value)


def attend_forward(queries, key_all, value_all, key_ok):
    row_count = queries.shape[0]
    key_count = key_all.shape[0]

    def per_group(group_idx):
        query_part = head_slices(queries, group_idx, row_count)
        key_part = head_slices(key_all, group_idx, key_count)
        value_part = head_slices(value_all, group_idx, key_count)
        scores = group_scores(query_part, key_part, key_ok)
        peak = jnp.max(scores, axis=-1, keepdims=True)
        shifted_exp = jnp.exp(scores - peak)
        summed = jnp.sum(shifted_exp, axis=-1, keepdims=True)
        probs = (shifted_exp / summed).astype(jnp.bfloat16)
        mixed = jnp.einsum("hqk,khd->qhd", probs, value_part, preferred_element_type=jnp.float32)
        log_sum = peak[..., 0] + jnp.log(summed[..., 0])
        return (mixed.reshape(row_count, 2 * HEAD), log_sum)

    mixed, log_sum = lax.map(per_group, jnp.arange(HEADS // 2))
    return (mixed.transpose(1, 0, 2).reshape(row_count, HEADS * HEAD), log_sum)


def attend_backward(queries, key_all, value_all, key_ok, grad_mixed, log_sum):
    row_count = queries.shape[0]
    key_count = key_all.shape[0]

    def per_group(items):
        group_idx, group_lse = items
        query_part = head_slices(queries, group_idx, row_count)
        key_part = head_slices(key_all, group_idx, key_count)
        value_part = head_slices(value_all, group_idx, key_count)
        grad_part = head_slices(grad_mixed, group_idx, row_count)
        scores = group_scores(query_part, key_part, key_ok)
        probs = jnp.exp(scores - group_lse[..., None])
        grad_probs = jnp.einsum(
            "qhd,khd->hqk", grad_part, value_part, preferred_element_type=jnp.float32
        )
        inner = jnp.sum(probs * grad_probs, axis=-1, keepdims=True)
        grad_scores = (probs * (grad_probs - inner)).astype(jnp.bfloat16)
        grad_query = (
            jnp.einsum("hqk,khd->qhd", grad_scores, key_part, preferred_element_type=jnp.float32)
            * score_scale
        )
        grad_key = (
            jnp.einsum("hqk,qhd->khd", grad_scores, query_part, preferred_element_type=jnp.float32)
            * score_scale
        )
        grad_value = jnp.einsum(
            "hqk,qhd->khd",
            probs.astype(jnp.bfloat16),
            grad_part,
            preferred_element_type=jnp.float32,
        )
        return (
            grad_query.reshape(row_count, 2 * HEAD),
            grad_key.reshape(key_count, 2 * HEAD),
            grad_value.reshape(key_count, 2 * HEAD),
        )

    grad_query, grad_key, grad_value = lax.map(per_group, (jnp.arange(HEADS // 2), log_sum))
    grad_query = grad_query.transpose(1, 0, 2).reshape(row_count, HEADS * HEAD)
    grad_key = grad_key.transpose(1, 0, 2).reshape(key_count, HEADS * HEAD)
    grad_value = grad_value.transpose(1, 0, 2).reshape(key_count, HEADS * HEAD)
    return (grad_query, grad_key, grad_value)


def block_forward(inputs, weights_full, length):
    qkv_mats, out_mat, in_mat, down_mat, query_bias, bias_rows, ffn_bias, gains, shifts = (
        weights_full
    )
    gains_f = gains.astype(jnp.float32)
    shifts_f = shifts.astype(jnp.float32)
    rounded = inputs.astype(jnp.bfloat16)
    queries = (matmul(rounded, qkv_mats[0]) + query_bias.astype(jnp.float32)).astype(jnp.bfloat16)
    key_rows = matmul(rounded, qkv_mats[1]).astype(jnp.bfloat16)
    value_rows = (matmul(rounded, qkv_mats[2]) + bias_rows[0].astype(jnp.float32)).astype(
        jnp.bfloat16
    )
    key_all, value_all = (
        lax.all_gather(key_rows, "ctx", axis=0, tiled=True),
        lax.all_gather(value_rows, "ctx", axis=0, tiled=True),
    )
    key_ok = jnp.arange(key_all.shape[0]) < length
    mixed_sum, log_sum = attend_forward(queries, key_all, value_all, key_ok)
    mixed = mixed_sum.astype(jnp.bfloat16)
    first_sum = inputs + matmul(mixed, out_mat) + bias_rows[1].astype(jnp.float32)
    normed = layer_norm(first_sum, gains_f[0], shifts_f[0])
    hidden = jnp.concatenate([matmul(normed.astype(jnp.bfloat16), in_mat[q]) for q in range(4)], axis=1)
    hidden = hidden + ffn_bias.astype(jnp.float32)
    active = jax.nn.gelu(hidden, approximate=False).astype(jnp.bfloat16)
    second_sum = normed + matmul(active, down_mat) + bias_rows[2].astype(jnp.float32)
    output = layer_norm(second_sum, gains_f[1], shifts_f[1])
    kept_acts = (
        rounded,
        queries,
        key_all,
        value_all,
        key_ok,
        mixed,
        log_sum,
        first_sum,
        normed,
        hidden,
        active,
        second_sum,
    )
    return (output, kept_acts)


def block_backward(grad_output, weights_full, kept_acts):
    qkv_mats, out_mat, in_mat, down_mat, query_bias, bias_rows, ffn_bias, gains, shifts = (
        weights_full
    )
    (
        rounded,
        queries,
        key_all,
        value_all,
        key_ok,
        mixed,
        log_sum,
        first_sum,
        normed,
        hidden,
        active,
        second_sum,
    ) = kept_acts
    gains_f = gains.astype(jnp.float32)
    shifts_f = shifts.astype(jnp.float32)
    unused_second, pull_second = jax.vjp(layer_norm, second_sum, gains_f[1], shifts_f[1])
    grad_second, grad_gain_two, grad_shift_two = pull_second(grad_output)
    grad_update = grad_second.astype(jnp.bfloat16)
    grad_down = matmul_left_t(active, grad_update)
    grad_bias_three = jnp.sum(grad_update.astype(jnp.float32), axis=0)
    grad_active = matmul_right_t(grad_update, down_mat)
    unused_gelu, pull_gelu = jax.vjp(
        lambda pre_act: jax.nn.gelu(pre_act, approximate=False), hidden
    )
    grad_hidden = pull_gelu(grad_active)[0].astype(jnp.bfloat16)
    normed_bf = normed.astype(jnp.bfloat16)
    grad_in = jnp.stack([matmul_left_t(normed_bf, grad_hidden[:, q * D : q * D + D]) for q in range(4)])
    grad_ffn_bias = jnp.sum(grad_hidden.astype(jnp.float32), axis=0)
    grad_normed = grad_second + sum(
        matmul_right_t(grad_hidden[:, q * D : q * D + D], in_mat[q]) for q in range(4)
    )
    unused_first, pull_first = jax.vjp(layer_norm, first_sum, gains_f[0], shifts_f[0])
    grad_first, grad_gain_one, grad_shift_one = pull_first(grad_normed)
    grad_branch = grad_first.astype(jnp.bfloat16)
    grad_out_mat = matmul_left_t(mixed, grad_branch)
    grad_bias_two = jnp.sum(grad_branch.astype(jnp.float32), axis=0)
    grad_mixed = matmul_right_t(grad_branch, out_mat).astype(jnp.bfloat16)
    grad_query, grad_key_all, grad_value_all = attend_backward(
        queries, key_all, value_all, key_ok, grad_mixed, log_sum
    )
    grad_key, grad_value = (
        lax.psum_scatter(
            grad_key_all.astype(jnp.bfloat16), "ctx", scatter_dimension=0, tiled=True
        ).astype(jnp.float32),
        lax.psum_scatter(
            grad_value_all.astype(jnp.bfloat16), "ctx", scatter_dimension=0, tiled=True
        ).astype(jnp.float32),
    )
    grad_query = grad_query.astype(jnp.bfloat16)
    grad_key = grad_key.astype(jnp.bfloat16)
    grad_value = grad_value.astype(jnp.bfloat16)
    grad_qkv = jnp.stack(
        [
            matmul_left_t(rounded, grad_query),
            matmul_left_t(rounded, grad_key),
            matmul_left_t(rounded, grad_value),
        ],
        axis=0,
    )
    grad_query_bias = jnp.sum(grad_query.astype(jnp.float32), axis=0)
    grad_bias_value = jnp.sum(grad_value.astype(jnp.float32), axis=0)
    grad_inputs = (
        grad_first
        + matmul_right_t(grad_query, qkv_mats[0])
        + matmul_right_t(grad_key, qkv_mats[1])
        + matmul_right_t(grad_value, qkv_mats[2])
    )
    mats = (
        jnp.concatenate([grad_qkv, grad_out_mat[None]], axis=0).astype(jnp.bfloat16),
        grad_in.astype(jnp.bfloat16),
        grad_down.astype(jnp.bfloat16),
    )
    rows = jnp.stack(
        [
            grad_query_bias,
            grad_bias_value,
            grad_bias_two,
            grad_bias_three,
            grad_gain_one,
            grad_gain_two,
            grad_shift_one,
            grad_shift_two,
        ]
    )
    small = jnp.concatenate([rows, grad_ffn_bias.reshape(4, D)], axis=0)
    grads_block = (mats, small)
    return (grad_inputs, grads_block)


def body(
    tokens,
    lengths,
    cotangent,
    w_qkv,
    w_attn_out,
    w_in,
    w_out,
    bias_q,
    bias_d,
    bias_ff,
    norm_gain,
    norm_shift,
    n,
    ny,
):
    length = lengths[0]
    row_count = tokens.shape[1]
    width = D // n
    first_row = lax.axis_index("ctx") * row_count
    valid_rows = (first_row + jnp.arange(row_count) < length).astype(jnp.float32)
    small = jnp.concatenate(
        [
            bias_q,
            bias_d.reshape(6, width),
            norm_gain.reshape(4, width),
            norm_shift.reshape(4, width),
            bias_ff.reshape(8, width),
            jnp.zeros((8, width), BF),
        ],
        axis=0,
    )
    gathered = gather_weights(
        n, ny, w_qkv, w_attn_out, w_in, w_out.reshape(2, 4, width, D), small
    )
    fulls, small_full = gathered[:6], gathered[6]
    narrow = small_full[:, :16].transpose(1, 0, 2).reshape(16, D)
    ff = small_full[:, 16:24].reshape(n, 2, 4 * width).transpose(1, 0, 2).reshape(2, 4 * D)
    weights = []
    for b in range(2):
        first = fulls[3 * b].reshape(4, D, D)
        weights.append(
            (
                first[:3],
                first[3],
                fulls[3 * b + 1].reshape(4, D, D),
                fulls[3 * b + 2].reshape(4 * D, D),
                narrow[b],
                narrow[2 + 3 * b : 5 + 3 * b],
                ff[b],
                narrow[8 + 2 * b : 10 + 2 * b],
                narrow[12 + 2 * b : 14 + 2 * b],
            )
        )
    carried = tokens[0].astype(jnp.float32)
    kept_layers = []
    for layer_idx in range(2):
        carried, kept_acts = block_forward(carried, weights[layer_idx], length)
        kept_layers.append(kept_acts)
    output_tokens = carried.astype(jnp.bfloat16)[None]
    grad_carried = cotangent[0].astype(jnp.float32) * valid_rows[:, None]
    grads = [None] * 6
    smalls = [None, None]
    for layer_idx in (1, 0):
        grad_carried, (mats, smalls[layer_idx]) = block_backward(
            grad_carried, weights[layer_idx], kept_layers[layer_idx]
        )
        grads[3 * layer_idx] = mats[0].reshape(4, n, width, D)
        grads[3 * layer_idx + 1] = mats[1].reshape(4, n, width, D)
        grads[3 * layer_idx + 2] = mats[2].reshape(n, 4, width, D)
    small_grads = jnp.concatenate(smalls, axis=0)
    *sums, small_sum = reduce_grads(n, ny, grads, small_grads)
    z = lax.axis_index("fsdp")
    small_sum = small_sum.reshape(2, 12, D)
    own = lax.dynamic_slice_in_dim(small_sum, z * width, width, 2)
    own_ff = lax.dynamic_slice_in_dim(small_sum[:, 8:].reshape(2, 4 * D), z * 4 * width, 4 * width, 1)
    return (
        output_tokens,
        grad_carried[None],
        jnp.stack([sums[0][:3], sums[3][:3]]).astype(F32),
        jnp.stack([sums[0][3], sums[3][3]]).astype(F32),
        jnp.stack([sums[1], sums[4]]).transpose(0, 2, 1, 3).reshape(2, width, 4 * D).astype(F32),
        jnp.stack([sums[2], sums[5]]).reshape(2, 4 * width, D).astype(F32),
        own[:, 0],
        own[:, 1:4],
        own_ff,
        own[:, 4:6],
        own[:, 6:8],
    )


def solution(mesh):
    placed = (
        P(("rep", "fsdp"), "ctx", None),
        P(("rep", "fsdp")),
        P(("rep", "fsdp"), "ctx", None),
        P(None, None, "fsdp", None),
        P(None, "fsdp", None),
        P(None, "fsdp", None),
        P(None, "fsdp", None),
        P(None, "fsdp"),
        P(None, None, "fsdp"),
        P(None, "fsdp"),
        P(None, None, "fsdp"),
        P(None, None, "fsdp"),
    )
    n, ny = mesh.shape["fsdp"], mesh.shape["ctx"] // 2
    return jax.shard_map(
        functools.partial(body, n=n, ny=ny),
        mesh=mesh,
        in_specs=placed,
        out_specs=(
            P(("rep", "fsdp"), "ctx", None),
            P(("rep", "fsdp"), "ctx", None),
            P(None, None, "fsdp", None),
            P(None, "fsdp", None),
            P(None, "fsdp", None),
            P(None, "fsdp", None),
            P(None, "fsdp"),
            P(None, None, "fsdp"),
            P(None, "fsdp"),
            P(None, None, "fsdp"),
            P(None, None, "fsdp"),
        ),
        check_vma=False,
    )
```

```python
import functools

import jax
import jax.numpy as jnp
from jax import lax
from jax.experimental import pallas as pl
from jax.experimental.pallas import tpu as pltpu
from jax.sharding import PartitionSpec as P

HEADS = 12
HEAD = 64
D = HEADS * HEAD
MESH = pl.DeviceIdType.MESH
BF = jnp.bfloat16
F32 = jnp.float32
MIB = 2**20

epsilon = 1e-05
score_scale = 0.125
masked_value = -1e30


class Place:
    def __init__(self, n, ny):
        self.n, self.ny = n, ny
        self.r = lax.axis_index("rep")
        self.z = lax.axis_index("fsdp")
        self.c = lax.axis_index("ctx")
        self.y, self.k = lax.div(self.c, 2), lax.rem(self.c, 2)
        self.e = lax.rem(self.y, 2)
        self.q = 2 * self.e + self.r
        self.qx = 2 * self.e + (1 - self.r)
        self.qy = 2 * (1 - self.e) + self.r
        self.qd = 2 * (1 - self.e) + (1 - self.r)

    def shard(self, offset):
        return lax.rem(self.z + (offset + self.n), self.n)

    def up(self, offset):
        return (self.r, self.shard(offset), self.c)

    def x(self):
        return (1 - self.r, self.z, self.c)

    def across(self):
        return (self.r, self.z, 2 * (self.y + 1 - 2 * self.e) + self.k)

    def row(self, offset, flip=0):
        y = lax.rem(self.y + offset, self.ny)
        k = self.k + flip * (1 - 2 * self.k)
        return (self.r, self.z, 2 * y + k)

    def core(self):
        return self.row(0, 1)

    def greet(self):
        others = [self.up(o) for o in range(1, self.n)]
        others += [self.x(), self.core()]
        others += [self.row(o) for o in range(1, self.ny)]
        barrier = pltpu.get_barrier_semaphore()
        for other in others:
            pl.semaphore_signal(barrier, inc=1, device_id=other, device_id_type=MESH)
        pl.semaphore_wait(barrier, len(others))


def remote(src, dst, send, recv, device):
    copy = pltpu.make_async_remote_copy(
        src_ref=src, dst_ref=dst, send_sem=send, recv_sem=recv, device_id=device, device_id_type=MESH
    )
    copy.start()
    return copy


def halves(half):
    first = -(-half // 32) * 16
    return [(0, first), (first, half - first)]


class Gather:
    def __init__(self, place, full, by_shard, local, send, recv):
        self.place, self.full, self.by_shard = place, full, by_shard
        self.local, self.send, self.recv = local, send, recv
        self.n = place.n
        self.half = full.shape[2] // 2
        self.pieces = halves(self.half)
        self.copies, self.core_copies = [], []

    @staticmethod
    def count(n):
        return 10 * (n - 1)

    def part(self, shard, q, piece=None):
        start, size = (0, self.half) if piece is None else piece
        rows = pl.ds(pl.multiple_of(self.place.k * self.half + start, 8), size)
        return self.full.at[shard, q, rows] if self.by_shard else self.full.at[q, shard, rows]

    def load(self, sources):
        self.loads = []
        z = self.place.z
        for i, (q, count, source) in enumerate(sources):
            if self.by_shard:
                target = self.full.at[z]
            elif count is None:
                target = self.full.at[q, z]
            else:
                target = self.full.at[pl.ds(q, count), z]
            copy = pltpu.make_async_copy(source, target, self.local.at[i])
            copy.start()
            self.loads.append(copy)

    def share(self, kind, offset, piece, device):
        slot = kind * (self.n - 1) + offset - 1
        copy = remote(piece, piece, self.send.at[slot], self.recv.at[slot], device)
        self.copies.append(copy)
        return copy

    def core_share(self, kind, offset, piece):
        copy = self.share(5 + kind, offset, piece, self.place.core())
        self.core_copies.append(copy)

    def start(self):
        place = self.place
        for copy in self.loads:
            copy.wait()
        mine = self.part(place.z, place.q)
        self.ups = [self.share(0, o, mine, place.up(o)) for o in range(1, self.n)]

    def plane(self):
        place = self.place
        self.xs, self.ys = [], []
        for o in range(1, self.n):
            self.ups[o - 1].wait_recv()
            piece = self.part(place.shard(-o), place.q)
            self.xs.append(self.share(1, o, piece, place.x()))
            self.ys.append(self.share(2, o, piece, place.across()))
            self.core_share(0, o, piece)

    def diagonal(self):
        place = self.place
        self.dys, self.dxs = [], []
        for o in range(1, self.n):
            shard = place.shard(-o)
            self.xs[o - 1].wait_recv()
            self.dys.append(self.share(3, o, self.part(shard, place.qx, self.pieces[0]), place.across()))
            self.core_share(1, o, self.part(shard, place.qx))
            self.ys[o - 1].wait_recv()
            self.dxs.append(self.share(4, o, self.part(shard, place.qy, self.pieces[1]), place.x()))
            self.core_share(2, o, self.part(shard, place.qy))

    def last(self):
        place = self.place
        for o in range(1, self.n):
            shard = place.shard(-o)
            self.dys[o - 1].wait_recv()
            self.core_share(3, o, self.part(shard, place.qd, self.pieces[0]))
            self.dxs[o - 1].wait_recv()
            self.core_share(4, o, self.part(shard, place.qd, self.pieces[1]))

    def finish(self):
        for copy in self.core_copies:
            copy.wait_recv()

    def drain(self):
        for copy in self.copies:
            copy.wait_send()

    def steps(self):
        return [self.start, self.plane, self.diagonal, self.last, self.finish]


def weight_sources(b, qkv, ao, win, wout):
    return [
        [(0, 3, qkv.at[b]), (3, None, ao.at[b])],
        [(q, None, win.at[b, :, pl.ds(q * D, D)]) for q in range(4)],
        [(None, None, wout.at[b])],
    ]


class Reduce:
    def __init__(self, place, grad, landing, out, local, send, recv, credit):
        self.place, self.grad, self.out = place, grad, out
        self.core_in, self.x_in, self.y_in, self.dx_in, self.dy_in, self.z_in, self.far_in = landing
        self.local, self.send, self.recv, self.credit = local, send, recv, credit
        self.n, self.ny = place.n, place.ny
        self.half = grad.shape[2] // 2
        self.top, self.low = halves(self.half)
        self.copies, self.cored, self.owns = [], [], []
        self.slot = 0
        self.plan = [self.add_cores, self.plane, self.depth, self.total, self.turn, self.last]

    @staticmethod
    def count(n, ny):
        return 4 + 6 + (n - 1) + (ny // 2 - 1) + 9

    @staticmethod
    def landing_buffers(n, ny):
        half = D // n // 2
        (_, first), (_, second) = halves(half)
        return [
            pltpu.VMEM((n, 4, half, D), BF),
            pltpu.VMEM((n, half, D), BF),
            pltpu.VMEM((n, half, D), BF),
            pltpu.VMEM((n, first, D), BF),
            pltpu.VMEM((n, second, D), BF),
            pltpu.VMEM((n - 1, half, D), BF),
            pltpu.VMEM((max(1, ny // 2 - 1), half, D), BF),
        ]

    def peers(self):
        place = self.place
        others = [place.up(o) for o in range(1, self.n)] + [place.x(), place.across(), place.core()]
        return others + [place.row(2 * i + 2) for i in range(self.ny // 2 - 1)]

    def release(self):
        for other in self.peers():
            pl.semaphore_signal(self.credit, inc=1, device_id=other, device_id_type=MESH)

    def acquire(self):
        pl.semaphore_wait(self.credit, len(self.peers()))

    def share(self, src, dst, device):
        copy = remote(src, dst, self.send.at[self.slot], self.recv.at[self.slot], device)
        self.slot += 1
        self.copies.append(copy)
        return copy

    def rows(self, k, piece=None):
        start, size = (0, self.half) if piece is None else piece
        return pl.ds(pl.multiple_of(k * self.half + start, 8), size)

    def own(self, shards, q, piece=None):
        return self.grad.at[shards, q, self.rows(self.place.k, piece)]

    def core(self, shards, q):
        source = self.grad.at[shards, q, self.rows(1 - self.place.k)]
        self.cored.append(self.share(source, self.core_in.at[shards, q], self.place.core()))

    def add_into(self, target, *sources):
        total = target[...].astype(F32)
        for source in sources:
            total = total + source[...].astype(F32)
        target[...] = total.astype(BF)

    def add_cores(self):
        for copy in self.cored:
            copy.wait_recv()

        def one(i, _):
            shard, q = lax.div(i, 4), lax.rem(i, 4)
            self.add_into(self.own(shard, q), self.core_in.at[shard, q])
            return 0

        lax.fori_loop(0, 4 * self.n, one, 0)
        place, every = self.place, slice(None)
        top, low = pl.ds(*self.top), pl.ds(*self.low)
        self.dx = self.share(self.own(every, place.qd, self.top), self.dx_in, place.x())
        self.dy = self.share(self.own(every, place.qd, self.low), self.dy_in, place.across())
        self.planes = [
            self.share(self.own(every, place.qx, self.top), self.x_in.at[:, top], place.x()),
            self.share(self.own(every, place.qy, self.low), self.y_in.at[:, low], place.across()),
        ]

    def plane(self):
        place, every = self.place, slice(None)
        top, low = pl.ds(*self.top), pl.ds(*self.low)
        self.dx.wait_recv()

        def one(j, _):
            self.add_into(self.own(j, place.qy, self.top), self.dx_in.at[j])
            return 0

        lax.fori_loop(0, self.n, one, 0)
        self.planes.append(
            self.share(self.own(every, place.qy, self.top), self.y_in.at[:, top], place.across())
        )
        self.dy.wait_recv()

        def two(j, _):
            self.add_into(self.own(j, place.qx, self.low), self.dy_in.at[j])
            return 0

        lax.fori_loop(0, self.n, two, 0)
        self.planes.append(self.share(self.own(every, place.qx, self.low), self.x_in.at[:, low], place.x()))

    def depth(self):
        place = self.place
        for copy in self.planes:
            copy.wait_recv()

        def one(j, _):
            self.add_into(self.own(j, place.q), self.x_in.at[j], self.y_in.at[j])
            return 0

        lax.fori_loop(0, self.n, one, 0)
        self.deep = [
            self.share(self.own(place.shard(o), place.q), self.z_in.at[o - 1], place.up(o))
            for o in range(1, self.n)
        ]

    def mine(self, q, piece=None):
        return self.out.at[q, self.rows(self.place.k, piece)]

    def total(self):
        place = self.place
        for copy in self.deep:
            copy.wait_recv()
        own = self.own(place.z, place.q)
        self.add_into(own, *[self.z_in.at[o - 1] for o in range(1, self.n)])
        if self.ny > 2:
            far = [self.share(own, self.far_in.at[i], place.row(2 * i + 2)) for i in range(self.ny // 2 - 1)]
            for copy in far:
                copy.wait_recv()
            mine = own[...].astype(F32)
            terms = [mine] + [self.far_in[i].astype(F32) for i in range(self.ny // 2 - 1)]
            total = jnp.zeros_like(mine)
            for y in range(0, self.ny, 2):
                offset = lax.rem(place.y - place.e - y + self.ny, self.ny)
                for i, term in enumerate(terms):
                    total = total + jnp.where(offset == 2 * i, term, 0.0)
            for copy in far:
                copy.wait_send()
            self.copies = [copy for copy in self.copies if all(copy is not other for other in far)]
            own[...] = total.astype(BF)
        copy = pltpu.make_async_copy(own, self.mine(place.q), self.local)
        copy.start()
        self.owns.append(copy)
        self.spread = [
            self.share(own, self.mine(place.q), place.x()),
            self.share(own, self.mine(place.q), place.across()),
        ]
        self.cores = [self.share(own, self.mine(place.q), place.core())]

    def forward(self, q, device, piece=None):
        return self.share(self.mine(q, piece), self.mine(q, piece), device)

    def turn(self):
        place = self.place
        self.spread[0].wait_recv()
        self.dy = self.forward(place.qx, place.across(), self.top)
        self.cores.append(self.forward(place.qx, place.core()))
        self.spread[1].wait_recv()
        self.dx = self.forward(place.qy, place.x(), self.low)
        self.cores.append(self.forward(place.qy, place.core()))

    def last(self):
        place = self.place
        self.dy.wait_recv()
        self.cores.append(self.forward(place.qd, place.core(), self.top))
        self.dx.wait_recv()
        self.cores.append(self.forward(place.qd, place.core(), self.low))

    def finish(self):
        for copy in self.cores:
            copy.wait_recv()

    def drain(self):
        for copy in self.copies:
            copy.wait_send()
        for copy in self.owns:
            copy.wait()
        self.copies, self.owns = [], []


class SmallReduce:
    def __init__(self, place, total, landing, send, recv):
        self.place, self.total, self.landing, self.send, self.recv = place, total, landing, send, recv
        n, ny = place.n, place.ny
        self.stages = [
            [place.core()],
            [place.up(o) for o in range(1, n)],
            [place.x()],
            [place.row(o) for o in range(1, ny)],
        ]
        self.copies = []
        self.slot = 0

    @staticmethod
    def count(n, ny):
        return 1 + (n - 1) + 1 + (ny - 1)

    def start(self, stage):
        self.current = []
        for device in self.stages[stage]:
            slot = self.slot
            copy = remote(
                self.total.at[stage], self.landing.at[slot], self.send.at[slot], self.recv.at[slot], device
            )
            self.current.append((slot, copy))
            self.copies.append(copy)
            self.slot += 1

    def end(self, stage):
        place, ny = self.place, self.place.ny
        for _, copy in self.current:
            copy.wait_recv()
        terms = [self.total[stage]] + [self.landing[slot] for slot, _ in self.current]
        if stage == 3 and ny > 2:
            total = jnp.zeros_like(terms[0])
            for y in range(ny):
                offset = lax.rem(place.y - y + ny, ny)
                for o in range(ny):
                    total = total + jnp.where(offset == o, terms[o], 0.0)
        else:
            total = functools.reduce(lambda a, b: a + b, terms)
        self.total[stage + 1] = total

    def steps(self):
        out = [functools.partial(self.start, 0)]
        for stage in range(4):
            out.append(functools.partial(self.end, stage))
            if stage < 3:
                out.append(functools.partial(self.start, stage + 1))
        return out


def matmul(operand_a, operand_b):
    return jnp.dot(operand_a, operand_b, preferred_element_type=F32)


def matmul_left_t(operand_a, operand_b):
    return lax.dot_general(operand_a, operand_b, (((0,), (0,)), ((), ())), preferred_element_type=F32)


def matmul_right_t(operand_a, operand_b):
    return lax.dot_general(operand_a, operand_b, (((1,), (1,)), ((), ())), preferred_element_type=F32)


def unit(ref, index, columns=None):
    block = ref[index] if columns is None else ref[index, :, :, columns]
    return block.reshape(D, block.shape[-1])


def center_scale(rows):
    center = rows - jnp.mean(rows, axis=-1, keepdims=True)
    inverse = lax.rsqrt(jnp.mean(center * center, axis=-1, keepdims=True) + epsilon)
    return center * inverse, inverse


class Exchange:
    def __init__(self, place, kv, send, recv):
        self.place, self.kv, self.send, self.recv = place, kv, send, recv
        self.copies = []

    @staticmethod
    def count(ny):
        return 2 * ny

    def share(self, half, chip_row, slot, device):
        part = self.kv.at[:, half, 2 * chip_row + self.place.k]
        copy = remote(part, part, self.send.at[half, slot], self.recv.at[half, slot], device)
        self.copies.append(copy)
        return copy

    def start(self, half):
        place, ny = self.place, self.place.ny
        far = [self.share(half, place.y, o, place.row(o)) for o in range(1, ny)]
        near = [self.share(half, place.y, 0, place.core())]
        return far, near

    def forward(self, half, state):
        place, ny = self.place, self.place.ny
        far, near = state
        for o in range(1, ny):
            far[o - 1].wait_recv()
            near.append(self.share(half, lax.rem(place.y - o + ny, ny), ny + o - 1, place.core()))

    def finish(self, state):
        for copy in state[1]:
            copy.wait_recv()

    def drain(self):
        for copy in self.copies:
            copy.wait_send()


def spread_small(n, small_full, narrow, wide):
    width = small_full.shape[2]
    row = lax.broadcasted_iota(jnp.int32, (width, D), 0)
    column = lax.broadcasted_iota(jnp.int32, (width, D), 1)
    narrow[...] = jnp.zeros_like(narrow)
    wide[...] = jnp.zeros_like(wide)
    for m in range(n):
        place = jnp.where(column - row == m * width, 1.0, 0.0).astype(BF)
        for j in range(n):
            turns = [t for t in range(4) if (4 * j + t) % n == m]
            if j != m and not turns:
                continue
            placed = matmul(small_full[j], place)
            if j == m:
                narrow[...] += placed[:16]
            for t in turns:
                c = (4 * j + t) // n
                for b in range(2):
                    wide[b, c : c + 1] += placed[16 + 4 * b + t : 17 + 4 * b + t]


def side_mask(side):
    lane = lax.broadcasted_iota(jnp.int32, (1, 2 * HEAD), 1)
    inside = lane < HEAD if side == 0 else lane >= HEAD
    return jnp.where(inside, 1.0, 0.0).astype(BF)


def attend(query, kv, half, mask, out, stats, first_head):
    rows = query.shape[0]
    lane = lax.broadcasted_iota(jnp.int32, (rows, 2 * HEAD), 1)
    allowed = mask[0:1]

    def pair(p, _):
        columns = pl.ds(pl.multiple_of(p * 2 * HEAD, 2 * HEAD), 2 * HEAD)
        where = pl.ds(pl.multiple_of(half * (D // 2) + p * 2 * HEAD, 2 * HEAD), 2 * HEAD)
        keys = kv[0, half, :, :, columns].reshape(-1, 2 * HEAD)
        values = kv[1, half, :, :, columns].reshape(-1, 2 * HEAD)
        query_pair = query[:, where]
        mixed = []
        for side in range(2):
            scores = matmul_right_t(query_pair * side_mask(side), keys) + allowed
            peak = jnp.max(scores, axis=-1, keepdims=True)
            weight = jnp.exp(scores - peak)
            total = jnp.sum(weight, axis=-1, keepdims=True)
            mixed.append(matmul((weight / total).astype(BF), values))
            head = first_head + 2 * p + side
            stats[...] = jnp.where(lane == head, peak + jnp.log(total), stats[...])
        out[:, where] = jnp.where(lane < HEAD, mixed[0], mixed[1])
        return 0

    lax.fori_loop(0, HEADS // 4, pair, 0)


SAVED = ("x", "query", "mixed", "stats", "hat_one", "active", "slope", "hat_two")


def forward_kernel(n, ny, *refs):
    tokens, mask, qkv, ao, win, wout, small = refs[:7]
    outs = refs[7:13]
    kv_outs, saved_outs = refs[13:15], refs[15:23]
    narrow_out, wide_out, result = refs[23:26]
    refs = refs[26:]
    fulls, kvs, saved = refs[:6], refs[6:8], refs[8:16]
    carried, normed, normed_bf, small_full = refs[16:20]
    local, send, recv, small_send, small_recv, kv_send, kv_recv, save_sem = refs[20:]
    place = Place(n, ny)
    groups = []
    for g in range(6):
        b, kind = g // 3, g % 3
        group = Gather(place, fulls[g], kind == 2, local.at[g], send.at[g], recv.at[g])
        group.load(weight_sources(b, qkv, ao, win, wout)[kind])
        groups.append(group)
    own = pltpu.make_async_copy(small, small_full.at[place.z], small_send.at[0])
    own.start()
    place.greet()
    smalls = [
        remote(small, small_full.at[place.z], small_send.at[o], small_recv.at[o], place.up(o))
        for o in range(1, n)
    ]
    kept = []

    def keep(source, target, sem):
        copy = pltpu.make_async_copy(source, target, sem)
        copy.start()
        kept.append(copy)

    plans = [group.steps() for group in groups]
    queue = []
    for t in range(len(plans[0]) + 5):
        for g in range(6):
            if 0 <= t - g < len(plans[g]):
                queue.append((g, t - g))
    done = set()

    def pump(count=1):
        for _ in range(count):
            if queue:
                g, at = queue.pop(0)
                plans[g][at]()
                if at == len(plans[g]) - 1:
                    done.add(g)
                    keep(fulls[g], outs[g], local.at[g, 4])

    def need(g):
        while g not in done:
            pump()

    carried[...] = tokens[...].astype(F32)
    pump(3)
    own.wait()
    for copy in smalls:
        copy.wait_recv()
    spread_small(n, small_full, narrow_out, wide_out)
    x, query, mixed, stats, hat_one, active, slope, hat_two = saved
    for b in range(2):
        first, second, third = fulls[3 * b : 3 * b + 3]

        def save(*names):
            for name in names:
                i = SAVED.index(name)
                keep(saved[i].at[b], saved_outs[i].at[b], save_sem.at[b, i])

        need(3 * b)
        x[b] = carried[...].astype(BF)
        exchange = Exchange(place, kvs[b], kv_send.at[b], kv_recv.at[b])
        states = []
        for half in range(2):
            columns = slice(half * (D // 2), (half + 1) * (D // 2))
            kvs[b][0, half, place.c] = matmul(x[b], unit(first, 1, columns)).astype(BF)
            value_bias = narrow_out[2 + 3 * b : 3 + 3 * b, columns]
            kvs[b][1, half, place.c] = (matmul(x[b], unit(first, 2, columns)) + value_bias).astype(BF)
            states.append(exchange.start(half))
        pump(2)
        projected = (matmul(x[b], unit(first, 0)) + narrow_out[b : b + 1]).astype(BF)
        query[b] = projected * jnp.asarray(score_scale, BF)
        stats[b] = jnp.zeros_like(stats[b])
        save("x", "query")
        pump(2)
        for half in range(2):
            exchange.forward(half, states[half])
        for half in range(2):
            exchange.finish(states[half])
            attend(query.at[b], kvs[b], half, mask, mixed.at[b], stats.at[b], half * (HEADS // 2))
            pump(2)
        keep(kvs[b], kv_outs[b], save_sem.at[b, len(SAVED)])
        attended = matmul(mixed[b].astype(BF), unit(first, 3))
        hat, inverse = center_scale(carried[...] + attended + narrow_out[3 + 3 * b : 4 + 3 * b])
        hat_one[b] = hat
        lane = lax.broadcasted_iota(jnp.int32, stats.shape[1:], 1)
        stats[b] = jnp.where(lane == HEADS, inverse, stats[b])
        normed[...] = hat * narrow_out[8 + 2 * b : 9 + 2 * b] + narrow_out[12 + 2 * b : 13 + 2 * b]
        normed_bf[...] = normed[...].astype(BF)
        save("mixed", "hat_one")
        pump(2)
        need(3 * b + 1)
        for c in range(4):
            hidden = matmul(normed_bf[...], unit(second, c)) + wide_out[b, c : c + 1]
            cdf = 0.5 + 0.5 * lax.erf(hidden * (2.0**-0.5))
            pdf = jnp.exp(-0.5 * hidden * hidden) * ((2.0 * jnp.pi) ** -0.5)
            active[b, c] = (hidden * cdf).astype(BF)
            slope[b, c] = (cdf + hidden * pdf).astype(BF)
            pump()
        save("active", "slope")
        need(3 * b + 2)
        update = normed[...] + narrow_out[4 + 3 * b : 5 + 3 * b]
        for c in range(4):
            update = update + matmul(active[b, c], third[c * n // 4 : (c + 1) * n // 4].reshape(D, D))
        hat, inverse = center_scale(update)
        hat_two[b] = hat
        stats[b] = jnp.where(lane == HEADS + 1, inverse, stats[b])
        save("stats", "hat_two")
        carried[...] = hat * narrow_out[9 + 2 * b : 10 + 2 * b] + narrow_out[13 + 2 * b : 14 + 2 * b]
        exchange.drain()
    result[...] = carried[...].astype(BF)
    for group in groups:
        group.drain()
    for copy in smalls:
        copy.wait_send()
    for copy in kept:
        copy.wait()


def forward_pass(n, ny, tokens, mask, qkv, ao, win, wout, small):
    rows, width = tokens.shape[0], D // n
    nc = 2 * ny
    full_shapes = [(4, n, width, D), (4, n, width, D), (n, 4, width, D)] * 2
    kv_shape = (2, 2, nc, rows, D // 2)
    saved_shapes = {
        "x": ((2, rows, D), BF),
        "query": ((2, rows, D), BF),
        "mixed": ((2, rows, D), F32),
        "stats": ((2, rows, 128), F32),
        "hat_one": ((2, rows, D), F32),
        "active": ((2, 4, rows, D), BF),
        "slope": ((2, 4, rows, D), BF),
        "hat_two": ((2, rows, D), F32),
    }
    out = [jax.ShapeDtypeStruct(shape, BF) for shape in full_shapes]
    out += [jax.ShapeDtypeStruct(kv_shape, BF)] * 2
    out += [jax.ShapeDtypeStruct(*saved_shapes[name]) for name in SAVED]
    out += [
        jax.ShapeDtypeStruct((16, D), F32),
        jax.ShapeDtypeStruct((2, 4, D), F32),
        jax.ShapeDtypeStruct((rows, D), BF),
    ]
    anywhere = pl.BlockSpec(memory_space=pl.ANY)
    vmem = pl.BlockSpec(memory_space=pltpu.VMEM)
    scratch = [pltpu.VMEM(shape, BF) for shape in full_shapes]
    scratch += [pltpu.VMEM(kv_shape, BF)] * 2
    scratch += [pltpu.VMEM(*saved_shapes[name]) for name in SAVED]
    scratch += [
        pltpu.VMEM((rows, D), F32),
        pltpu.VMEM((rows, D), F32),
        pltpu.VMEM((rows, D), BF),
        pltpu.VMEM((n,) + small.shape, BF),
        pltpu.SemaphoreType.DMA((6, 5)),
        pltpu.SemaphoreType.DMA((6, Gather.count(n))),
        pltpu.SemaphoreType.DMA((6, Gather.count(n))),
        pltpu.SemaphoreType.DMA((n,)),
        pltpu.SemaphoreType.DMA((n,)),
        pltpu.SemaphoreType.DMA((2, 2, Exchange.count(ny))),
        pltpu.SemaphoreType.DMA((2, 2, Exchange.count(ny))),
        pltpu.SemaphoreType.DMA((2, len(SAVED) + 1)),
    ]
    return pl.pallas_call(
        functools.partial(forward_kernel, n, ny),
        out_shape=out,
        in_specs=[vmem, vmem] + [anywhere] * 4 + [vmem],
        out_specs=[anywhere] * 16 + [vmem] * 3,
        scratch_shapes=scratch,
        compiler_params=pltpu.CompilerParams(
            collective_id=0, has_side_effects=True, vmem_limit_bytes=60 * MIB
        ),
        name="forward_pass",
    )(tokens, mask, qkv, ao, win, wout, small)


def normal_back(grad_output, gain, hat, inverse):
    grad_hat = grad_output * gain
    mean = jnp.mean(grad_hat, axis=-1, keepdims=True)
    slant = jnp.mean(grad_hat * hat, axis=-1, keepdims=True)
    return inverse * (grad_hat - mean - hat * slant)


def column_sum(rows):
    return jnp.sum(rows.astype(F32), axis=0, keepdims=True)


class KeyGrads:
    def __init__(self, place, grads, core_in, far_in, send, recv, credit):
        self.place, self.grads, self.core_in, self.far_in = place, grads, core_in, far_in
        self.send, self.recv, self.credit = send, recv, credit
        self.copies = []
        self.cored, self.far = {}, {}

    def peers(self):
        return [self.place.core()] + [self.place.row(o) for o in range(1, self.place.ny)]

    def release(self):
        for other in self.peers():
            pl.semaphore_signal(self.credit, inc=1, device_id=other, device_id_type=MESH)

    def acquire(self):
        pl.semaphore_wait(self.credit, len(self.peers()))

    @staticmethod
    def count(ny):
        return 2 * ny - 1

    def share(self, half, slot, src, dst, device):
        copy = remote(src, dst, self.send.at[half, slot], self.recv.at[half, slot], device)
        self.copies.append(copy)
        return copy

    def start(self, half):
        place, ny = self.place, self.place.ny
        self.cored[half] = []
        for i in range(ny):
            y = lax.rem(place.y + i, ny)
            part = self.grads.at[:, half, 2 * y + 1 - place.k]
            self.cored[half].append(self.share(half, i, part, self.core_in.at[:, half, y], place.core()))

    def middle(self, half):
        place, ny = self.place, self.place.ny
        for copy in self.cored[half]:
            copy.wait_recv()
        for y in range(ny):
            for kind in range(2):
                part = self.grads.at[kind, half, 2 * y + place.k]
                part[...] = (part[...].astype(F32) + self.core_in[kind, half, y].astype(F32)).astype(BF)
        self.far[half] = []
        for o in range(1, ny):
            y = lax.rem(place.y + o, ny)
            part = self.grads.at[:, half, 2 * y + place.k]
            self.far[half].append(
                self.share(half, ny + o - 1, part, self.far_in.at[:, half, o - 1], place.row(o))
            )

    def end(self, half, kind):
        for copy in self.far[half]:
            if kind == 0:
                copy.wait_recv()
        total = self.grads[kind, half, self.place.c].astype(F32)
        for o in range(1, self.place.ny):
            total = total + self.far_in[kind, half, o - 1].astype(F32)
        return total.astype(BF)

    def drain(self):
        for copy in self.copies:
            copy.wait_send()


def attend_back(query, kv, half, mask, stats, mixed, grad_mixed, grad_query, grads):
    rows = query.shape[0]
    lane = lax.broadcasted_iota(jnp.int32, (rows, 2 * HEAD), 1)
    blocks = 4 if kv.shape[2] <= 4 else 2

    def pair(p, _):
        columns = pl.ds(pl.multiple_of(p * 2 * HEAD, 2 * HEAD), 2 * HEAD)
        where = pl.ds(pl.multiple_of(half * (D // 2) + p * 2 * HEAD, 2 * HEAD), 2 * HEAD)
        query_pair, grad_pair = query[:, where], grad_mixed[:, where]
        products = (mixed[:, where] * grad_pair.astype(F32)).T
        grad_queries = [0.0, 0.0]
        for at in range(0, kv.shape[2], blocks):
            some = slice(at, at + blocks)
            keys = kv[0, half, some, :, columns].reshape(-1, 2 * HEAD)
            values = kv[1, half, some, :, columns].reshape(-1, 2 * HEAD)
            blocked = mask[at * rows : (at + blocks) * rows, :]
            grad_keys, grad_values = 0.0, 0.0
            for side in range(2):
                query_side, grad_side = query_pair * side_mask(side), grad_pair * side_mask(side)
                log_sum = stats[pl.ds(half * (HEADS // 2) + 2 * p + side, 1), :]
                inner = jnp.sum(products[side * HEAD : (side + 1) * HEAD], axis=0, keepdims=True)
                probs = jnp.exp(matmul_right_t(keys, query_side) + blocked - log_sum)
                grad_probs = matmul_right_t(values, grad_side)
                grad_scores = (probs * (grad_probs - inner)).astype(BF)
                grad_keys = grad_keys + matmul(grad_scores, query_side)
                grad_values = grad_values + matmul(probs.astype(BF), grad_side)
                grad_queries[side] = grad_queries[side] + matmul_left_t(grad_scores, keys)
            grads[0, half, some, :, columns] = grad_keys.astype(BF).reshape(-1, rows, 2 * HEAD)
            grads[1, half, some, :, columns] = grad_values.astype(BF).reshape(-1, rows, 2 * HEAD)
        grad_query[:, where] = (
            jnp.where(lane < HEAD, grad_queries[0], grad_queries[1]) * score_scale
        ).astype(BF)
        return 0

    lax.fori_loop(0, HEADS // 4, pair, 0)


ROWS = 12


def backward_kernel(n, ny, *refs):
    upstream, mask, narrow = refs[:3]
    fulls, kvs, saved = refs[3:9], refs[9:11], refs[11:19]
    outs, out_small, out_tokens = refs[19:25], refs[25], refs[26]
    refs = refs[27:]
    window, held, kv = refs[0], refs[1:9], refs[9]
    grads, landings = refs[10:13], [refs[13 + 7 * i : 20 + 7 * i] for i in range(3)]
    refs = refs[34:]
    grad_kv, kv_core, kv_far = refs[:3]
    deeper, lower, grad_query, grad_rows, stats_rows = refs[3:8]
    small_total, small_landing = refs[8:10]
    carried = out_tokens
    load_sem, window_sem, local, send, recv, credit, kv_send, kv_recv, small_send, small_recv = refs[10:]
    place = Place(n, ny)
    x, query, mixed, stats, hat_one, active, slope, hat_two = held
    hidden = active
    ahead = window.shape[0]
    loads = {}

    def load(b, *names):
        for name in names:
            i = SAVED.index(name) if name != "kv" else len(SAVED)
            source, target = (kvs[b], kv) if name == "kv" else (saved[i].at[b], held[i])
            loads[(b, name)] = pltpu.make_async_copy(source, target, load_sem.at[i])
            loads[(b, name)].start()

    def ready(b, *names):
        for name in names:
            loads[(b, name)].wait()

    order = []
    for b in (1, 0):
        order += [(b, 2, c) for c in range(4)] + [(b, 1, c) for c in range(4)]
        order += [(b, 0, 3), (b, 0, 0), (b, 0, 1), (b, 0, 2)]
    fetched = []

    def fetch():
        i = len(fetched)
        if i < len(order):
            b, kind, c = order[i]
            copy = pltpu.make_async_copy(
                fulls[3 * b + kind].at[c], window.at[i % ahead], window_sem.at[i % ahead]
            )
            copy.start()
            fetched.append(copy)

    used = []

    def weight():
        i = len(used)
        if i > 0:
            fetch()
        fetched[i].wait()
        used.append(i)
        return window.at[i % ahead]

    load(1, "hat_two", "stats", "active", "slope", "hat_one", "mixed", "query", "kv", "x")
    for _ in range(ahead - 1):
        fetch()
    reduces = {}
    for b in (1, 0):
        for kind in range(3):
            g = 3 * b + kind
            reduces[(b, kind)] = Reduce(
                place, grads[kind], landings[kind], outs[g], local.at[g], send.at[g], recv.at[g], credit.at[kind]
            )
    active_plans = []
    steps = {key: list(group.plan) for key, group in reduces.items()}

    def step(key):
        steps[key].pop(0)()
        if len(steps[key]) == 2 and key[0] == 1:
            reduces[key].release()

    def pump(count=1):
        for _ in range(count):
            for key in list(active_plans):
                step(key)
                if not steps[key]:
                    active_plans.remove(key)

    def complete(key):
        while steps[key]:
            pump()
        reduces[key].drain()

    def begin(b, kind):
        if b == 0:
            complete((1, kind))

    def sent(b, kind):
        active_plans.append((b, kind))

    place.greet()
    carried[...] = upstream[...].astype(F32)
    for b in (1, 0):
        third, second, first = [reduces[(b, kind)] for kind in (2, 1, 0)]

        def note(i, row, b=b):
            small_total[0, ROWS * b + i : ROWS * b + i + 1] = row

        gain_one, gain_two = narrow[8 + 2 * b : 9 + 2 * b], narrow[9 + 2 * b : 10 + 2 * b]
        ready(b, "hat_two", "stats", "active")
        stats_rows[...] = stats[...].T
        inverse_one, inverse_two = stats[:, HEADS : HEADS + 1], stats[:, HEADS + 1 : HEADS + 2]
        note(5, column_sum(carried[...] * hat_two[...]))
        note(7, column_sum(carried[...]))
        grad = normal_back(carried[...], gain_two, hat_two[...], inverse_two)
        deeper[...] = grad
        lower[...] = grad.astype(BF)
        note(3, column_sum(lower[...]))
        if b == 1:
            load(0, "hat_two")
        begin(b, 2)
        part = n // 4
        for c in range(4):
            block = matmul_left_t(active[c], lower[...]).astype(BF)
            shards = pl.ds(c * part, part)
            grads[2][shards] = block.reshape(part, 4, D // n, D)
            if c == 0 and b == 0:
                third.acquire()
            third.core(shards, slice(None))
        sent(b, 2)
        ready(b, "slope", "hat_one")
        for c in range(4):
            flow = matmul_right_t(lower[...], weight()[...]) * slope[c].astype(F32)
            hidden[c] = flow.astype(BF)
            note(8 + c, column_sum(hidden[c]))
        if b == 1:
            load(0, "slope")
        pump()
        begin(b, 1)
        lower[...] = (hat_one[...] * gain_one + narrow[12 + 2 * b : 13 + 2 * b]).astype(BF)
        for c in range(4):
            block = matmul_left_t(lower[...], hidden[c]).astype(BF)
            grads[1][:, c] = block.reshape(n, D // n, D)
            if c == 0 and b == 0:
                second.acquire()
            second.core(slice(None), c)
        sent(b, 1)
        pump()
        for c in range(4):
            deeper[...] += matmul_right_t(hidden[c], weight()[...])
        note(4, column_sum(deeper[...] * hat_one[...]))
        note(6, column_sum(deeper[...]))
        carried[...] = normal_back(deeper[...], gain_one, hat_one[...], inverse_one)
        lower[...] = carried[...].astype(BF)
        note(2, column_sum(lower[...]))
        if b == 1:
            load(0, "hat_one", "stats", "active")
        grad_rows[...] = matmul_right_t(lower[...], weight()[...]).astype(BF)
        pump()
        ready(b, "mixed", "query", "kv")
        begin(b, 0)
        block = matmul_left_t(mixed[...].astype(BF), lower[...]).astype(BF)
        grads[0][:, 3] = block.reshape(n, D // n, D)
        if b == 0:
            first.acquire()
        first.core(slice(None), 3)
        keys = KeyGrads(place, grad_kv, kv_core, kv_far, kv_send.at[b], kv_recv.at[b], credit.at[3])
        if b == 0:
            keys.acquire()
        for half in range(2):
            attend_back(query, kv, half, mask, stats_rows, mixed, grad_rows, grad_query, grad_kv)
            keys.start(half)
            if half == 1:
                keys.middle(0)
        if b == 1:
            load(0, "mixed", "query", "kv")
        ready(b, "x")
        block = matmul_left_t(x[...], grad_query[...]).astype(BF)
        grads[0][:, 0] = block.reshape(n, D // n, D)
        first.core(slice(None), 0)
        keys.middle(1)
        note(0, column_sum(grad_query[...]))
        carried[...] += matmul_right_t(grad_query[...], weight()[...])
        for kind in range(2):
            for half in range(2):
                lower[:, half * (D // 2) : (half + 1) * (D // 2)] = keys.end(half, kind)
            block = matmul_left_t(x[...], lower[...]).astype(BF)
            grads[0][:, 1 + kind] = block.reshape(n, D // n, D)
            first.core(slice(None), 1 + kind)
            if kind == 1:
                note(1, column_sum(lower[...]))
            carried[...] += matmul_right_t(lower[...], weight()[...])
        sent(b, 0)
        keys.drain()
        if b == 1:
            keys.release()
            load(0, "x")
    small_sum = SmallReduce(place, small_total, small_landing, small_send, small_recv)
    small_steps = small_sum.steps()
    while active_plans or small_steps:
        if small_steps:
            small_steps.pop(0)()
        pump()
    out_small[...] = small_total[4]
    for key, group in reduces.items():
        group.finish()
        group.drain()
    for copy in small_sum.copies:
        copy.wait_send()


def backward_pass(n, ny, upstream, mask, narrow, fulls, kvs, saved):
    rows, width = upstream.shape[0], D // n
    nc = 2 * ny
    out = [jax.ShapeDtypeStruct((4, width, D), BF)] * 6
    out += [jax.ShapeDtypeStruct((2 * ROWS, D), F32), jax.ShapeDtypeStruct((rows, D), F32)]
    anywhere = pl.BlockSpec(memory_space=pl.ANY)
    vmem = pl.BlockSpec(memory_space=pltpu.VMEM)
    smalls = SmallReduce.count(n, ny)
    ahead = 4 if ny == 2 else 2
    scratch = [pltpu.VMEM((ahead, D, D), BF)]
    scratch += [pltpu.VMEM(item.shape[1:], item.dtype) for item in saved]
    scratch += [pltpu.VMEM(kvs[0].shape, BF)]
    scratch += [pltpu.VMEM((n, 4, width, D), BF)] * 3
    for _ in range(3):
        scratch += Reduce.landing_buffers(n, ny)
    scratch += [pltpu.VMEM((2, 2, nc, rows, D // 2), BF)]
    scratch += [pltpu.VMEM((2, 2, ny, rows, D // 2), BF), pltpu.VMEM((2, 2, ny - 1, rows, D // 2), BF)]
    scratch += [
        pltpu.VMEM((rows, D), F32),
        pltpu.VMEM((rows, D), BF),
        pltpu.VMEM((rows, D), BF),
        pltpu.VMEM((rows, D), BF),
        pltpu.VMEM((128, rows), F32),
        pltpu.VMEM((5, 2 * ROWS, D), F32),
        pltpu.VMEM((smalls, 2 * ROWS, D), F32),
        pltpu.SemaphoreType.DMA((len(SAVED) + 1,)),
        pltpu.SemaphoreType.DMA((ahead,)),
        pltpu.SemaphoreType.DMA((6,)),
        pltpu.SemaphoreType.DMA((6, Reduce.count(n, ny))),
        pltpu.SemaphoreType.DMA((6, Reduce.count(n, ny))),
        pltpu.SemaphoreType.REGULAR((4,)),
        pltpu.SemaphoreType.DMA((2, 2, KeyGrads.count(ny))),
        pltpu.SemaphoreType.DMA((2, 2, KeyGrads.count(ny))),
        pltpu.SemaphoreType.DMA((smalls,)),
        pltpu.SemaphoreType.DMA((smalls,)),
    ]
    return pl.pallas_call(
        functools.partial(backward_kernel, n, ny),
        out_shape=out,
        in_specs=[vmem] * 3 + [anywhere] * 16,
        out_specs=[anywhere] * 6 + [vmem] * 2,
        scratch_shapes=scratch,
        compiler_params=pltpu.CompilerParams(
            collective_id=1, has_side_effects=True, vmem_limit_bytes=63 * MIB
        ),
        name="backward_pass",
    )(upstream, mask, narrow, *fulls, *kvs, *saved)


def body(
    tokens,
    lengths,
    cotangent,
    w_qkv,
    w_attn_out,
    w_in,
    w_out,
    bias_q,
    bias_d,
    bias_ff,
    norm_gain,
    norm_shift,
    n,
    ny,
):
    row_count = tokens.shape[1]
    width = D // n
    z = lax.axis_index("fsdp")
    first_row = lax.axis_index("ctx") * row_count
    upstream = jnp.where((first_row + jnp.arange(row_count) < lengths[0])[:, None], cotangent[0], 0)
    mask = jnp.where(jnp.arange(2 * ny * row_count) < lengths[0], 0.0, masked_value).astype(F32)
    mask_row = jnp.broadcast_to(mask[None], (8, mask.shape[0]))
    small = jnp.concatenate(
        [
            bias_q,
            bias_d.reshape(6, width),
            norm_gain.reshape(4, width),
            norm_shift.reshape(4, width),
            bias_ff.reshape(8, width),
            jnp.zeros((8, width), BF),
        ],
        axis=0,
    )
    made = forward_pass(
        n, ny, tokens[0], mask_row, w_qkv, w_attn_out, w_in, w_out.reshape(2, 4, width, D), small
    )
    fulls, kvs, saved = made[:6], made[6:8], made[8:16]
    narrow, _, result = made[16:]
    fulls = [full.reshape(4, D, D) for full in fulls]
    *sums, small_sum, grad_tokens = backward_pass(n, ny, upstream, mask[:, None], narrow, fulls, kvs, saved)
    small_sum = small_sum.reshape(2, ROWS, D)
    own = lax.dynamic_slice_in_dim(small_sum, z * width, width, 2)
    own_ff = lax.dynamic_slice_in_dim(small_sum[:, 8:].reshape(2, 4 * D), z * 4 * width, 4 * width, 1)
    return (
        result[None],
        grad_tokens[None],
        jnp.stack([sums[0][:3], sums[3][:3]]).astype(F32),
        jnp.stack([sums[0][3], sums[3][3]]).astype(F32),
        jnp.stack([sums[1], sums[4]]).transpose(0, 2, 1, 3).reshape(2, width, 4 * D).astype(F32),
        jnp.stack([sums[2], sums[5]]).reshape(2, 4 * width, D).astype(F32),
        own[:, 0],
        own[:, 1:4],
        own_ff,
        own[:, 4:6],
        own[:, 6:8],
    )


def solution(mesh):
    placed = (
        P(("rep", "fsdp"), "ctx", None),
        P(("rep", "fsdp")),
        P(("rep", "fsdp"), "ctx", None),
        P(None, None, "fsdp", None),
        P(None, "fsdp", None),
        P(None, "fsdp", None),
        P(None, "fsdp", None),
        P(None, "fsdp"),
        P(None, None, "fsdp"),
        P(None, "fsdp"),
        P(None, None, "fsdp"),
        P(None, None, "fsdp"),
    )
    n, ny = mesh.shape["fsdp"], mesh.shape["ctx"] // 2
    return jax.shard_map(
        functools.partial(body, n=n, ny=ny),
        mesh=mesh,
        in_specs=placed,
        out_specs=(
            P(("rep", "fsdp"), "ctx", None),
            P(("rep", "fsdp"), "ctx", None),
            P(None, None, "fsdp", None),
            P(None, "fsdp", None),
            P(None, "fsdp", None),
            P(None, "fsdp", None),
            P(None, "fsdp"),
            P(None, None, "fsdp"),
            P(None, "fsdp"),
            P(None, None, "fsdp"),
            P(None, None, "fsdp"),
        ),
        check_vma=False,
    )
```

```python
import functools

import jax
import jax.numpy as jnp
from jax import lax
from jax.experimental import pallas as pl
from jax.experimental.pallas import tpu as pltpu
from jax.sharding import PartitionSpec as P

HEADS = 12
HEAD = 64
D = HEADS * HEAD
MESH = pl.DeviceIdType.MESH
BF = jnp.bfloat16
F32 = jnp.float32
MIB = 2**20
GATHER_CUT, REDUCE_CUT = 2, 3

epsilon = 1e-05
score_scale = 0.125
masked_value = -1e30


class Place:
    def __init__(self, n, ny):
        self.n, self.ny = n, ny
        self.r = lax.axis_index("rep")
        self.z = lax.axis_index("fsdp")
        self.c = lax.axis_index("ctx")
        self.y, self.k = lax.div(self.c, 2), lax.rem(self.c, 2)
        self.e = lax.rem(self.y, 2)
        self.q = 2 * self.e + self.r
        self.qx = 2 * self.e + (1 - self.r)
        self.qy = 2 * (1 - self.e) + self.r
        self.qd = 2 * (1 - self.e) + (1 - self.r)

    def shard(self, offset):
        return lax.rem(self.z + (offset + self.n), self.n)

    def up(self, offset):
        return (self.r, self.shard(offset), self.c)

    def x(self):
        return (1 - self.r, self.z, self.c)

    def across(self):
        return (self.r, self.z, 2 * (self.y + 1 - 2 * self.e) + self.k)

    def row(self, offset, flip=0):
        y = lax.rem(self.y + offset, self.ny)
        k = self.k + flip * (1 - 2 * self.k)
        return (self.r, self.z, 2 * y + k)

    def core(self):
        return self.row(0, 1)

    def greet(self):
        others = [self.up(o) for o in range(1, self.n)]
        others += [self.x(), self.core()]
        others += [self.row(o) for o in range(1, self.ny)]
        barrier = pltpu.get_barrier_semaphore()
        for other in others:
            pl.semaphore_signal(barrier, inc=1, device_id=other, device_id_type=MESH)
        pl.semaphore_wait(barrier, len(others))


def remote(src, dst, send, recv, device):
    copy = pltpu.make_async_remote_copy(
        src_ref=src, dst_ref=dst, send_sem=send, recv_sem=recv, device_id=device, device_id_type=MESH
    )
    copy.start()
    return copy


def cut(half, sixths):
    first = max(8, half * sixths // 96 * 16)
    return [(0, first), (first, half - first)]


class Gather:
    def __init__(self, place, full, by_shard, local, send, recv):
        self.place, self.full, self.by_shard = place, full, by_shard
        self.local, self.send, self.recv = local, send, recv
        self.n = place.n
        self.half = full.shape[2] // 2
        self.pieces = cut(self.half, GATHER_CUT)
        self.copies, self.core_copies = [], []

    @staticmethod
    def count(n):
        return 10 * (n - 1)

    def part(self, shard, q, piece=None):
        start, size = (0, self.half) if piece is None else piece
        rows = pl.ds(pl.multiple_of(self.place.k * self.half + start, 8), size)
        return self.full.at[shard, q, rows] if self.by_shard else self.full.at[q, shard, rows]

    def load(self, sources):
        self.loads = []
        z = self.place.z
        for i, (q, count, source) in enumerate(sources):
            if self.by_shard:
                target = self.full.at[z]
            elif count is None:
                target = self.full.at[q, z]
            else:
                target = self.full.at[pl.ds(q, count), z]
            copy = pltpu.make_async_copy(source, target, self.local.at[i])
            copy.start()
            self.loads.append(copy)

    def share(self, kind, offset, piece, device):
        slot = kind * (self.n - 1) + offset - 1
        copy = remote(piece, piece, self.send.at[slot], self.recv.at[slot], device)
        self.copies.append(copy)
        return copy

    def core_share(self, kind, offset, piece):
        copy = self.share(5 + kind, offset, piece, self.place.core())
        self.core_copies.append(copy)

    def start(self):
        place = self.place
        for copy in self.loads:
            copy.wait()
        mine = self.part(place.z, place.q)
        self.ups = [self.share(0, o, mine, place.up(o)) for o in range(1, self.n)]

    def to_x(self):
        place = self.place
        self.xs = []
        for o in range(1, self.n):
            self.ups[o - 1].wait_recv()
            piece = self.part(place.shard(-o), place.q)
            self.xs.append(self.share(1, o, piece, place.x()))
            self.core_share(0, o, piece)

    def to_y(self):
        place = self.place
        self.ys = [
            self.share(2, o, self.part(place.shard(-o), place.q), place.across()) for o in range(1, self.n)
        ]

    def from_x(self):
        place = self.place
        self.dys = []
        for o in range(1, self.n):
            shard = place.shard(-o)
            self.xs[o - 1].wait_recv()
            self.dys.append(self.share(3, o, self.part(shard, place.qx, self.pieces[0]), place.across()))
            self.core_share(1, o, self.part(shard, place.qx))

    def from_y(self):
        place = self.place
        self.dxs = []
        for o in range(1, self.n):
            shard = place.shard(-o)
            self.ys[o - 1].wait_recv()
            self.dxs.append(self.share(4, o, self.part(shard, place.qy, self.pieces[1]), place.x()))
            self.core_share(2, o, self.part(shard, place.qy))

    def last(self):
        place = self.place
        for o in range(1, self.n):
            shard = place.shard(-o)
            self.dys[o - 1].wait_recv()
            self.core_share(3, o, self.part(shard, place.qd, self.pieces[0]))
        for o in range(1, self.n):
            shard = place.shard(-o)
            self.dxs[o - 1].wait_recv()
            self.core_share(4, o, self.part(shard, place.qd, self.pieces[1]))

    def finish(self):
        for copy in self.core_copies:
            copy.wait_recv()

    def drain(self):
        for copy in self.copies:
            copy.wait_send()

    def steps(self):
        return dict(A=self.start, B=self.to_x, Y=self.to_y, C=self.from_x, E=self.from_y, L=self.last, F=self.finish)


def weight_sources(b, qkv, ao, win, wout):
    return [
        [(0, 3, qkv.at[b]), (3, None, ao.at[b])],
        [(q, None, win.at[b, :, pl.ds(q * D, D)]) for q in range(4)],
        [(None, None, wout.at[b])],
    ]


class Reduce:
    def __init__(self, place, grad, landing, out, wide, local, send, recv, credit):
        self.place, self.grad, self.out, self.wide = place, grad, out, wide
        self.core_in, self.x_in, self.y_in, self.dx_in, self.dy_in, self.z_in, self.far_in = landing
        self.local, self.send, self.recv, self.credit = local, send, recv, credit
        self.n, self.ny = place.n, place.ny
        self.half = grad.shape[2] // 2
        self.low, self.top = cut(self.half, REDUCE_CUT)
        self.copies, self.cored, self.owns = [], [], []
        self.slot = 0
        self.plan = [self.add_cores, self.plane, self.depth, self.total, self.turn, self.last]

    @staticmethod
    def count(n, ny):
        return 4 + 6 + (n - 1) + (ny // 2 - 1) + 9

    @staticmethod
    def landing_buffers(n, ny):
        half = D // n // 2
        (_, second), (_, first) = cut(half, REDUCE_CUT)
        return [
            pltpu.VMEM((n, 4, half, D), BF),
            pltpu.VMEM((n, half, D), BF),
            pltpu.VMEM((n, half, D), BF),
            pltpu.VMEM((n, first, D), BF),
            pltpu.VMEM((n, second, D), BF),
            pltpu.VMEM((n - 1, half, D), BF),
            pltpu.VMEM((max(1, ny // 2 - 1), half, D), BF),
        ]

    def peers(self):
        place = self.place
        others = [place.up(o) for o in range(1, self.n)] + [place.x(), place.across(), place.core()]
        return others + [place.row(2 * i + 2) for i in range(self.ny // 2 - 1)]

    def release(self):
        for other in self.peers():
            pl.semaphore_signal(self.credit, inc=1, device_id=other, device_id_type=MESH)

    def acquire(self):
        pl.semaphore_wait(self.credit, len(self.peers()))

    def share(self, src, dst, device):
        copy = remote(src, dst, self.send.at[self.slot], self.recv.at[self.slot], device)
        self.slot += 1
        self.copies.append(copy)
        return copy

    def rows(self, k, piece=None):
        start, size = (0, self.half) if piece is None else piece
        return pl.ds(pl.multiple_of(k * self.half + start, 8), size)

    def own(self, shards, q, piece=None):
        return self.grad.at[shards, q, self.rows(self.place.k, piece)]

    def core(self, shards, q):
        source = self.grad.at[shards, q, self.rows(1 - self.place.k)]
        self.cored.append(self.share(source, self.core_in.at[shards, q], self.place.core()))

    def add_into(self, target, *sources):
        total = target[...].astype(F32)
        for source in sources:
            total = total + source[...].astype(F32)
        target[...] = total.astype(BF)

    def add_cores(self):
        for copy in self.cored:
            copy.wait_recv()

        def one(i, _):
            shard, q = lax.div(i, 4), lax.rem(i, 4)
            self.add_into(self.own(shard, q), self.core_in.at[shard, q])
            return 0

        lax.fori_loop(0, 4 * self.n, one, 0)
        place, every = self.place, slice(None)
        top, low = pl.ds(*self.top), pl.ds(*self.low)
        self.dx = self.share(self.own(every, place.qd, self.top), self.dx_in, place.x())
        self.dy = self.share(self.own(every, place.qd, self.low), self.dy_in, place.across())
        self.planes = [
            self.share(self.own(every, place.qx, self.top), self.x_in.at[:, top], place.x()),
            self.share(self.own(every, place.qy, self.low), self.y_in.at[:, low], place.across()),
        ]

    def plane(self):
        place, every = self.place, slice(None)
        top, low = pl.ds(*self.top), pl.ds(*self.low)
        self.dx.wait_recv()

        def one(j, _):
            self.add_into(self.own(j, place.qy, self.top), self.dx_in.at[j])
            return 0

        lax.fori_loop(0, self.n, one, 0)
        self.planes.append(
            self.share(self.own(every, place.qy, self.top), self.y_in.at[:, top], place.across())
        )
        self.dy.wait_recv()

        def two(j, _):
            self.add_into(self.own(j, place.qx, self.low), self.dy_in.at[j])
            return 0

        lax.fori_loop(0, self.n, two, 0)
        self.planes.append(self.share(self.own(every, place.qx, self.low), self.x_in.at[:, low], place.x()))

    def depth(self):
        place = self.place
        for copy in self.planes:
            copy.wait_recv()

        def one(j, _):
            self.add_into(self.own(j, place.q), self.x_in.at[j], self.y_in.at[j])
            return 0

        lax.fori_loop(0, self.n, one, 0)
        self.deep = [
            self.share(self.own(place.shard(o), place.q), self.z_in.at[o - 1], place.up(o))
            for o in range(1, self.n)
        ]

    def mine(self, q, piece=None):
        rows = self.rows(self.place.k, piece)
        if self.wide:
            return self.out.at[rows, pl.ds(pl.multiple_of(q * D, D), D)]
        return self.out.at[q, rows]

    def total(self):
        place = self.place
        for copy in self.deep:
            copy.wait_recv()
        own = self.own(place.z, place.q)
        self.add_into(own, *[self.z_in.at[o - 1] for o in range(1, self.n)])
        if self.ny > 2:
            far = [self.share(own, self.far_in.at[i], place.row(2 * i + 2)) for i in range(self.ny // 2 - 1)]
            for copy in far:
                copy.wait_recv()
            mine = own[...].astype(F32)
            terms = [mine] + [self.far_in[i].astype(F32) for i in range(self.ny // 2 - 1)]
            total = jnp.zeros_like(mine)
            for y in range(0, self.ny, 2):
                offset = lax.rem(place.y - place.e - y + self.ny, self.ny)
                for i, term in enumerate(terms):
                    total = total + jnp.where(offset == 2 * i, term, 0.0)
            for copy in far:
                copy.wait_send()
            self.copies = [copy for copy in self.copies if all(copy is not other for other in far)]
            own[...] = total.astype(BF)
        copy = pltpu.make_async_copy(own, self.mine(place.q), self.local)
        copy.start()
        self.owns.append(copy)
        self.spread = [
            self.share(own, self.mine(place.q), place.x()),
            self.share(own, self.mine(place.q), place.across()),
        ]
        self.cores = [self.share(own, self.mine(place.q), place.core())]

    def forward(self, q, device, piece=None):
        return self.share(self.mine(q, piece), self.mine(q, piece), device)

    def turn(self):
        place = self.place
        self.spread[0].wait_recv()
        self.dy = self.forward(place.qx, place.across(), self.top)
        self.cores.append(self.forward(place.qx, place.core()))
        self.spread[1].wait_recv()
        self.dx = self.forward(place.qy, place.x(), self.low)
        self.cores.append(self.forward(place.qy, place.core()))

    def last(self):
        place = self.place
        self.dy.wait_recv()
        self.cores.append(self.forward(place.qd, place.core(), self.top))
        self.dx.wait_recv()
        self.cores.append(self.forward(place.qd, place.core(), self.low))

    def finish(self):
        for copy in self.cores:
            copy.wait_recv()

    def drain(self):
        for copy in self.copies:
            copy.wait_send()
        for copy in self.owns:
            copy.wait()
        self.copies, self.owns = [], []


class SmallReduce:
    def __init__(self, place, total, landing, send, recv):
        self.place, self.total, self.landing, self.send, self.recv = place, total, landing, send, recv
        n, ny = place.n, place.ny
        self.stages = [
            [place.core()],
            [place.up(o) for o in range(1, n)],
            [place.x()],
            [place.row(o) for o in range(1, ny)],
        ]
        self.copies = []
        self.slot = 0

    @staticmethod
    def count(n, ny):
        return 1 + (n - 1) + 1 + (ny - 1)

    def start(self, stage):
        self.current = []
        for device in self.stages[stage]:
            slot = self.slot
            copy = remote(
                self.total.at[stage], self.landing.at[slot], self.send.at[slot], self.recv.at[slot], device
            )
            self.current.append((slot, copy))
            self.copies.append(copy)
            self.slot += 1

    def end(self, stage):
        place, ny = self.place, self.place.ny
        for _, copy in self.current:
            copy.wait_recv()
        terms = [self.total[stage]] + [self.landing[slot] for slot, _ in self.current]
        if stage == 3 and ny > 2:
            total = jnp.zeros_like(terms[0])
            for y in range(ny):
                offset = lax.rem(place.y - y + ny, ny)
                for o in range(ny):
                    total = total + jnp.where(offset == o, terms[o], 0.0)
        else:
            total = functools.reduce(lambda a, b: a + b, terms)
        self.total[stage + 1] = total

    def steps(self):
        out = [functools.partial(self.start, 0)]
        for stage in range(4):
            out.append(functools.partial(self.end, stage))
            if stage < 3:
                out.append(functools.partial(self.start, stage + 1))
        return out


def matmul(operand_a, operand_b):
    return jnp.dot(operand_a, operand_b, preferred_element_type=F32)


def matmul_left_t(operand_a, operand_b):
    return lax.dot_general(operand_a, operand_b, (((0,), (0,)), ((), ())), preferred_element_type=F32)


def matmul_right_t(operand_a, operand_b):
    return lax.dot_general(operand_a, operand_b, (((1,), (1,)), ((), ())), preferred_element_type=F32)


def unit(ref, index, columns=None):
    block = ref[index] if columns is None else ref[index, :, :, columns]
    return block.reshape(D, block.shape[-1])


def center_scale(rows):
    center = rows - jnp.mean(rows, axis=-1, keepdims=True)
    inverse = lax.rsqrt(jnp.mean(center * center, axis=-1, keepdims=True) + epsilon)
    return center * inverse, inverse


class Exchange:
    def __init__(self, place, kv, send, recv):
        self.place, self.kv, self.send, self.recv = place, kv, send, recv
        self.copies = []

    @staticmethod
    def count(ny):
        return 2 * ny

    def share(self, half, chip_row, slot, device):
        part = self.kv.at[:, half, 2 * chip_row + self.place.k]
        copy = remote(part, part, self.send.at[half, slot], self.recv.at[half, slot], device)
        self.copies.append(copy)
        return copy

    def start(self, half):
        place, ny = self.place, self.place.ny
        far = [self.share(half, place.y, o, place.row(o)) for o in range(1, ny)]
        near = [self.share(half, place.y, 0, place.core())]
        return far, near

    def forward(self, half, state):
        place, ny = self.place, self.place.ny
        far, near = state
        for o in range(1, ny):
            far[o - 1].wait_recv()
            near.append(self.share(half, lax.rem(place.y - o + ny, ny), ny + o - 1, place.core()))

    def finish(self, state):
        for copy in state[1]:
            copy.wait_recv()

    def drain(self):
        for copy in self.copies:
            copy.wait_send()


def spread_small(n, small_full, narrow, wide):
    width = small_full.shape[2]
    row = lax.broadcasted_iota(jnp.int32, (width, D), 0)
    column = lax.broadcasted_iota(jnp.int32, (width, D), 1)
    narrow[...] = jnp.zeros_like(narrow)
    wide[...] = jnp.zeros_like(wide)
    for m in range(n):
        place = jnp.where(column - row == m * width, 1.0, 0.0).astype(BF)
        for j in range(n):
            turns = [t for t in range(4) if (4 * j + t) % n == m]
            if j != m and not turns:
                continue
            placed = matmul(small_full[j], place)
            if j == m:
                narrow[...] += placed[:16]
            for t in turns:
                c = (4 * j + t) // n
                for b in range(2):
                    wide[b, c : c + 1] += placed[16 + 4 * b + t : 17 + 4 * b + t]


def side_mask(side):
    lane = lax.broadcasted_iota(jnp.int32, (1, 2 * HEAD), 1)
    inside = lane < HEAD if side == 0 else lane >= HEAD
    return jnp.where(inside, 1.0, 0.0).astype(BF)


def attend(query, kv, half, mask, out, stats, first_head):
    rows = query.shape[0]
    lane = lax.broadcasted_iota(jnp.int32, (rows, 2 * HEAD), 1)
    allowed = mask[0:1]

    def pair(p, _):
        columns = pl.ds(pl.multiple_of(p * 2 * HEAD, 2 * HEAD), 2 * HEAD)
        where = pl.ds(pl.multiple_of(half * (D // 2) + p * 2 * HEAD, 2 * HEAD), 2 * HEAD)
        keys = kv[0, half, :, :, columns].reshape(-1, 2 * HEAD)
        values = kv[1, half, :, :, columns].reshape(-1, 2 * HEAD)
        query_pair = query[:, where]
        mixed = []
        for side in range(2):
            scores = matmul_right_t(query_pair * side_mask(side), keys) + allowed
            peak = jnp.max(scores, axis=-1, keepdims=True)
            weight = jnp.exp(scores - peak)
            total = jnp.sum(weight, axis=-1, keepdims=True)
            mixed.append(matmul((weight / total).astype(BF), values))
            head = first_head + 2 * p + side
            stats[...] = jnp.where(lane == head, peak + jnp.log(total), stats[...])
        out[:, where] = jnp.where(lane < HEAD, mixed[0], mixed[1])
        return 0

    lax.fori_loop(0, HEADS // 4, pair, 0)


SCHEDULE = [
    "A0 B0 Y0 A1",
    [
        "C0 E0 B1 Y1 A2 L0 C1 E1 B2 Y2 A3 F0",
        "L1 C2 E2 B3 Y3 A4",
        "F1 L2",
        "C3 E3 B4 Y4",
        "A5 F2",
        "L3",
        "C4 E4",
        "B5 Y5",
        "F3",
        "",
    ],
    ["L4", "C5 E5 F4", "L5", "F5", "", "", "", "", "", ""],
]

SAVED = ("x", "query", "mixed", "stats", "hat_one", "active", "slope", "hat_two")


def forward_kernel(n, ny, *refs):
    tokens, mask, qkv, ao, win, wout, small = refs[:7]
    outs = refs[7:13]
    kv_outs, saved_outs = refs[13:15], refs[15:23]
    narrow_out, wide_out, result = refs[23:26]
    refs = refs[26:]
    fulls, kvs, saved = refs[:6], refs[6:8], refs[8:16]
    carried, normed, normed_bf, small_full = refs[16:20]
    local, send, recv, small_send, small_recv, kv_send, kv_recv, save_sem = refs[20:]
    place = Place(n, ny)
    groups = []
    for g in range(6):
        b, kind = g // 3, g % 3
        group = Gather(place, fulls[g], kind == 2, local.at[g], send.at[g], recv.at[g])
        group.load(weight_sources(b, qkv, ao, win, wout)[kind])
        groups.append(group)
    own = pltpu.make_async_copy(small, small_full.at[place.z], small_send.at[0])
    own.start()
    place.greet()
    smalls = [
        remote(small, small_full.at[place.z], small_send.at[o], small_recv.at[o], place.up(o))
        for o in range(1, n)
    ]
    kept = []

    def keep(source, target, sem):
        copy = pltpu.make_async_copy(source, target, sem)
        copy.start()
        kept.append(copy)

    plans = [group.steps() for group in groups]

    def run(steps):
        for name in steps.split():
            g = int(name[1])
            plans[g].pop(name[0])()
            if name[0] == "F":
                keep(fulls[g], outs[g], local.at[g, 4])

    carried[...] = tokens[...].astype(F32)
    run(SCHEDULE[0])
    own.wait()
    for copy in smalls:
        copy.wait_recv()
    spread_small(n, small_full, narrow_out, wide_out)
    x, query, mixed, stats, hat_one, active, slope, hat_two = saved
    for b in range(2):
        first, second, third = fulls[3 * b : 3 * b + 3]

        def save(*names):
            for name in names:
                i = SAVED.index(name)
                keep(saved[i].at[b], saved_outs[i].at[b], save_sem.at[b, i])

        turn = iter(SCHEDULE[1 + b])
        run(next(turn))
        x[b] = carried[...].astype(BF)
        exchange = Exchange(place, kvs[b], kv_send.at[b], kv_recv.at[b])
        states = []
        for half in range(2):
            columns = slice(half * (D // 2), (half + 1) * (D // 2))
            kvs[b][0, half, place.c] = matmul(x[b], unit(first, 1, columns)).astype(BF)
            value_bias = narrow_out[2 + 3 * b : 3 + 3 * b, columns]
            kvs[b][1, half, place.c] = (matmul(x[b], unit(first, 2, columns)) + value_bias).astype(BF)
            states.append(exchange.start(half))
        run(next(turn))
        projected = (matmul(x[b], unit(first, 0)) + narrow_out[b : b + 1]).astype(BF)
        query[b] = projected * jnp.asarray(score_scale, BF)
        stats[b] = jnp.zeros_like(stats[b])
        save("x", "query")
        for half in range(2):
            exchange.forward(half, states[half])
            exchange.finish(states[half])
            if half == 1:
                run(next(turn))
            attend(query.at[b], kvs[b], half, mask, mixed.at[b], stats.at[b], half * (HEADS // 2))
        run(next(turn))
        keep(kvs[b], kv_outs[b], save_sem.at[b, len(SAVED)])
        attended = matmul(mixed[b].astype(BF), unit(first, 3))
        hat, inverse = center_scale(carried[...] + attended + narrow_out[3 + 3 * b : 4 + 3 * b])
        hat_one[b] = hat
        lane = lax.broadcasted_iota(jnp.int32, stats.shape[1:], 1)
        stats[b] = jnp.where(lane == HEADS, inverse, stats[b])
        normed[...] = hat * narrow_out[8 + 2 * b : 9 + 2 * b] + narrow_out[12 + 2 * b : 13 + 2 * b]
        normed_bf[...] = normed[...].astype(BF)
        save("mixed", "hat_one")
        run(next(turn))
        for c in range(4):
            hidden = matmul(normed_bf[...], unit(second, c)) + wide_out[b, c : c + 1]
            cdf = 0.5 + 0.5 * lax.erf(hidden * (2.0**-0.5))
            pdf = jnp.exp(-0.5 * hidden * hidden) * ((2.0 * jnp.pi) ** -0.5)
            active[b, c] = (hidden * cdf).astype(BF)
            slope[b, c] = (cdf + hidden * pdf).astype(BF)
            run(next(turn))
        save("active", "slope")
        run(next(turn))
        update = normed[...] + narrow_out[4 + 3 * b : 5 + 3 * b]
        for c in range(4):
            update = update + matmul(active[b, c], third[c * n // 4 : (c + 1) * n // 4].reshape(D, D))
        hat, inverse = center_scale(update)
        hat_two[b] = hat
        stats[b] = jnp.where(lane == HEADS + 1, inverse, stats[b])
        save("stats", "hat_two")
        carried[...] = hat * narrow_out[9 + 2 * b : 10 + 2 * b] + narrow_out[13 + 2 * b : 14 + 2 * b]
        exchange.drain()
    result[...] = carried[...].astype(BF)
    for group in groups:
        group.drain()
    for copy in smalls:
        copy.wait_send()
    for copy in kept:
        copy.wait()


def forward_pass(n, ny, tokens, mask, qkv, ao, win, wout, small):
    rows, width = tokens.shape[0], D // n
    nc = 2 * ny
    full_shapes = [(4, n, width, D), (4, n, width, D), (n, 4, width, D)] * 2
    kv_shape = (2, 2, nc, rows, D // 2)
    saved_shapes = {
        "x": ((2, rows, D), BF),
        "query": ((2, rows, D), BF),
        "mixed": ((2, rows, D), F32),
        "stats": ((2, rows, 128), F32),
        "hat_one": ((2, rows, D), F32),
        "active": ((2, 4, rows, D), BF),
        "slope": ((2, 4, rows, D), BF),
        "hat_two": ((2, rows, D), F32),
    }
    out = [jax.ShapeDtypeStruct(shape, BF) for shape in full_shapes]
    out += [jax.ShapeDtypeStruct(kv_shape, BF)] * 2
    out += [jax.ShapeDtypeStruct(*saved_shapes[name]) for name in SAVED]
    out += [
        jax.ShapeDtypeStruct((16, D), F32),
        jax.ShapeDtypeStruct((2, 4, D), F32),
        jax.ShapeDtypeStruct((rows, D), BF),
    ]
    anywhere = pl.BlockSpec(memory_space=pl.ANY)
    vmem = pl.BlockSpec(memory_space=pltpu.VMEM)
    scratch = [pltpu.VMEM(shape, BF) for shape in full_shapes]
    scratch += [pltpu.VMEM(kv_shape, BF)] * 2
    scratch += [pltpu.VMEM(*saved_shapes[name]) for name in SAVED]
    scratch += [
        pltpu.VMEM((rows, D), F32),
        pltpu.VMEM((rows, D), F32),
        pltpu.VMEM((rows, D), BF),
        pltpu.VMEM((n,) + small.shape, BF),
        pltpu.SemaphoreType.DMA((6, 5)),
        pltpu.SemaphoreType.DMA((6, Gather.count(n))),
        pltpu.SemaphoreType.DMA((6, Gather.count(n))),
        pltpu.SemaphoreType.DMA((n,)),
        pltpu.SemaphoreType.DMA((n,)),
        pltpu.SemaphoreType.DMA((2, 2, Exchange.count(ny))),
        pltpu.SemaphoreType.DMA((2, 2, Exchange.count(ny))),
        pltpu.SemaphoreType.DMA((2, len(SAVED) + 1)),
    ]
    return pl.pallas_call(
        functools.partial(forward_kernel, n, ny),
        out_shape=out,
        in_specs=[vmem, vmem] + [anywhere] * 4 + [vmem],
        out_specs=[anywhere] * 16 + [vmem] * 3,
        scratch_shapes=scratch,
        compiler_params=pltpu.CompilerParams(
            collective_id=0, has_side_effects=True, vmem_limit_bytes=60 * MIB
        ),
        name="forward_pass",
    )(tokens, mask, qkv, ao, win, wout, small)


def normal_back(grad_output, gain, hat, inverse):
    grad_hat = grad_output * gain
    mean = jnp.mean(grad_hat, axis=-1, keepdims=True)
    slant = jnp.mean(grad_hat * hat, axis=-1, keepdims=True)
    return inverse * (grad_hat - mean - hat * slant)


def column_sum(rows):
    return jnp.sum(rows.astype(F32), axis=0, keepdims=True)


class KeyGrads:
    def __init__(self, place, grads, core_in, far_in, send, recv, credit):
        self.place, self.grads, self.core_in, self.far_in = place, grads, core_in, far_in
        self.send, self.recv, self.credit = send, recv, credit
        self.copies = []
        self.cored, self.far = {}, {}

    def peers(self):
        return [self.place.core()] + [self.place.row(o) for o in range(1, self.place.ny)]

    def release(self):
        for other in self.peers():
            pl.semaphore_signal(self.credit, inc=1, device_id=other, device_id_type=MESH)

    def acquire(self):
        pl.semaphore_wait(self.credit, len(self.peers()))

    @staticmethod
    def count(ny):
        return 2 * ny - 1

    def share(self, half, slot, src, dst, device):
        copy = remote(src, dst, self.send.at[half, slot], self.recv.at[half, slot], device)
        self.copies.append(copy)
        return copy

    def start(self, half):
        place, ny = self.place, self.place.ny
        self.cored[half] = []
        for i in range(ny):
            y = lax.rem(place.y + i, ny)
            part = self.grads.at[:, half, 2 * y + 1 - place.k]
            self.cored[half].append(self.share(half, i, part, self.core_in.at[:, half, y], place.core()))

    def middle(self, half):
        place, ny = self.place, self.place.ny
        for copy in self.cored[half]:
            copy.wait_recv()
        for y in range(ny):
            for kind in range(2):
                part = self.grads.at[kind, half, 2 * y + place.k]
                part[...] = (part[...].astype(F32) + self.core_in[kind, half, y].astype(F32)).astype(BF)
        self.far[half] = []
        for o in range(1, ny):
            y = lax.rem(place.y + o, ny)
            part = self.grads.at[:, half, 2 * y + place.k]
            self.far[half].append(
                self.share(half, ny + o - 1, part, self.far_in.at[:, half, o - 1], place.row(o))
            )

    def end(self, half, kind):
        for copy in self.far[half]:
            if kind == 0:
                copy.wait_recv()
        total = self.grads[kind, half, self.place.c].astype(F32)
        for o in range(1, self.place.ny):
            total = total + self.far_in[kind, half, o - 1].astype(F32)
        return total.astype(BF)

    def drain(self):
        for copy in self.copies:
            copy.wait_send()


def attend_back(query, kv, half, mask, stats, mixed, grad_mixed, grad_query, grads):
    rows = query.shape[0]
    lane = lax.broadcasted_iota(jnp.int32, (rows, 2 * HEAD), 1)
    blocks = 4 if kv.shape[2] <= 4 else 2

    def pair(p, _):
        columns = pl.ds(pl.multiple_of(p * 2 * HEAD, 2 * HEAD), 2 * HEAD)
        where = pl.ds(pl.multiple_of(half * (D // 2) + p * 2 * HEAD, 2 * HEAD), 2 * HEAD)
        query_pair, grad_pair = query[:, where], grad_mixed[:, where]
        products = (mixed[:, where] * grad_pair.astype(F32)).T
        grad_queries = [0.0, 0.0]
        for at in range(0, kv.shape[2], blocks):
            some = slice(at, at + blocks)
            keys = kv[0, half, some, :, columns].reshape(-1, 2 * HEAD)
            values = kv[1, half, some, :, columns].reshape(-1, 2 * HEAD)
            blocked = mask[at * rows : (at + blocks) * rows, :]
            grad_keys, grad_values = 0.0, 0.0
            for side in range(2):
                query_side, grad_side = query_pair * side_mask(side), grad_pair * side_mask(side)
                log_sum = stats[pl.ds(half * (HEADS // 2) + 2 * p + side, 1), :]
                inner = jnp.sum(products[side * HEAD : (side + 1) * HEAD], axis=0, keepdims=True)
                probs = jnp.exp(matmul_right_t(keys, query_side) + blocked - log_sum)
                grad_probs = matmul_right_t(values, grad_side)
                grad_scores = (probs * (grad_probs - inner)).astype(BF)
                grad_keys = grad_keys + matmul(grad_scores, query_side)
                grad_values = grad_values + matmul(probs.astype(BF), grad_side)
                grad_queries[side] = grad_queries[side] + matmul_left_t(grad_scores, keys)
            grads[0, half, some, :, columns] = grad_keys.astype(BF).reshape(-1, rows, 2 * HEAD)
            grads[1, half, some, :, columns] = grad_values.astype(BF).reshape(-1, rows, 2 * HEAD)
        grad_query[:, where] = (
            jnp.where(lane < HEAD, grad_queries[0], grad_queries[1]) * score_scale
        ).astype(BF)
        return 0

    lax.fori_loop(0, HEADS // 4, pair, 0)


ROWS = 12
PUMPS = [[1, 1, 1, 0, 0, 1, 0, 0], [1, 1, 1, 0, 0, 1, 0, 0]]
OUT_LATE, IN_LATE = [False, False], [True, False]


def backward_kernel(n, ny, *refs):
    upstream, mask, narrow = refs[:3]
    fulls, kvs, saved = refs[3:9], refs[9:11], refs[11:19]
    outs, out_small, out_tokens = refs[19:22], refs[22], refs[23]
    refs = refs[24:]
    window, held, kv = refs[0], refs[1:9], refs[9]
    grads, landings = refs[10:13], [refs[13 + 7 * i : 20 + 7 * i] for i in range(3)]
    refs = refs[34:]
    grad_kv, kv_core, kv_far = refs[:3]
    deeper, lower, update_rows, normed_rows, grad_query, grad_rows, stats_rows = refs[3:10]
    small_total, small_landing = refs[10:12]
    hidden = refs[12]
    carried = out_tokens
    load_sem, window_sem, local, send, recv, credit, kv_send, kv_recv, small_send, small_recv = refs[13:]
    place = Place(n, ny)
    roomy = ny == 2
    x, query, mixed, stats, hat_one, active, slope, hat_two = held
    if not roomy:
        hidden, update_rows, normed_rows = active, lower, lower
    ahead = window.shape[0]
    loads = {}

    def load(b, *names):
        for name in names:
            i = SAVED.index(name) if name != "kv" else len(SAVED)
            source, target = (kvs[b], kv) if name == "kv" else (saved[i].at[b], held[i])
            loads[(b, name)] = pltpu.make_async_copy(source, target, load_sem.at[i])
            loads[(b, name)].start()

    def ready(b, *names):
        for name in names:
            loads[(b, name)].wait()

    order = []
    for b in (1, 0):
        order += [(b, 2, c) for c in range(4)] + [(b, 1, c) for c in range(4)]
        order += [(b, 0, 3), (b, 0, 0), (b, 0, 1), (b, 0, 2)]
    fetched = []

    def fetch():
        i = len(fetched)
        if i < len(order):
            b, kind, c = order[i]
            copy = pltpu.make_async_copy(
                fulls[3 * b + kind].at[c], window.at[i % ahead], window_sem.at[i % ahead]
            )
            copy.start()
            fetched.append(copy)

    used = []

    def weight():
        i = len(used)
        if i > 0:
            fetch()
        fetched[i].wait()
        used.append(i)
        return window.at[i % ahead]

    load(1, "hat_two", "stats", "active", "slope", "hat_one", "mixed", "query", "kv", "x")
    for _ in range(ahead - 1):
        fetch()
    reduces = {}
    for b in (1, 0):
        for kind in range(3):
            g = 3 * b + kind
            reduces[(b, kind)] = Reduce(
                place,
                grads[kind],
                landings[kind],
                outs[kind].at[b],
                kind == 1,
                local.at[g],
                send.at[g],
                recv.at[g],
                credit.at[kind],
            )
    active_plans = []
    steps = {key: list(group.plan) for key, group in reduces.items()}

    def step(key):
        steps[key].pop(0)()
        if len(steps[key]) == 2 and key[0] == 1:
            reduces[key].release()

    def pump(count=1):
        for _ in range(count):
            for key in list(active_plans):
                step(key)
                if not steps[key]:
                    active_plans.remove(key)

    def complete(key):
        while steps[key]:
            pump()
        reduces[key].drain()

    def begin(b, kind):
        if b == 0:
            complete((1, kind))

    def sent(b, kind):
        active_plans.append((b, kind))

    place.greet()
    carried[...] = upstream[...].astype(F32)
    for b in (1, 0):
        third, second, first = [reduces[(b, kind)] for kind in (2, 1, 0)]

        def note(i, row, b=b):
            small_total[0, ROWS * b + i : ROWS * b + i + 1] = row

        turn = iter(PUMPS[b])
        gain_one, gain_two = narrow[8 + 2 * b : 9 + 2 * b], narrow[9 + 2 * b : 10 + 2 * b]
        ready(b, "hat_two", "stats", "active")
        stats_rows[...] = stats[...].T
        inverse_one, inverse_two = stats[:, HEADS : HEADS + 1], stats[:, HEADS + 1 : HEADS + 2]
        note(5, column_sum(carried[...] * hat_two[...]))
        note(7, column_sum(carried[...]))
        grad = normal_back(carried[...], gain_two, hat_two[...], inverse_two)
        deeper[...] = grad
        update_rows[...] = grad.astype(BF)
        note(3, column_sum(update_rows[...]))
        if b == 1:
            load(0, "hat_two")
        part = n // 4

        def out_grads(c):
            if c == 0:
                begin(b, 2)
            block = matmul_left_t(active[c], update_rows[...]).astype(BF)
            shards = pl.ds(c * part, part)
            grads[2][shards] = block.reshape(part, 4, D // n, D)
            if c == 0 and b == 0:
                third.acquire()
            third.core(shards, slice(None))
            if c == 3:
                sent(b, 2)

        def in_grads(c):
            if c == 0:
                begin(b, 1)
                normed_rows[...] = (hat_one[...] * gain_one + narrow[12 + 2 * b : 13 + 2 * b]).astype(BF)
            block = matmul_left_t(normed_rows[...], hidden[c]).astype(BF)
            grads[1][:, c] = block.reshape(n, D // n, D)
            if c == 0 and b == 0:
                second.acquire()
            second.core(slice(None), c)
            if c == 3:
                sent(b, 1)

        def attention_grads(i, left, right):
            if i == 3:
                begin(b, 0)
            block = matmul_left_t(left, right).astype(BF)
            grads[0][:, i] = block.reshape(n, D // n, D)
            if i == 3 and b == 0:
                first.acquire()
            first.core(slice(None), i)

        out_late, in_late = roomy and OUT_LATE[b], roomy and IN_LATE[b]
        if not out_late:
            for c in range(4):
                out_grads(c)
        ready(b, "slope", "hat_one")
        for c in range(4):
            flow = matmul_right_t(update_rows[...], weight()[...]) * slope[c].astype(F32)
            hidden[c] = flow.astype(BF)
            note(8 + c, column_sum(hidden[c]))
        if b == 1:
            load(0, "slope")
        pump(next(turn))
        if not in_late:
            for c in range(4):
                in_grads(c)
        pump(next(turn))
        for c in range(4):
            deeper[...] += matmul_right_t(hidden[c], weight()[...])
        note(4, column_sum(deeper[...] * hat_one[...]))
        note(6, column_sum(deeper[...]))
        carried[...] = normal_back(deeper[...], gain_one, hat_one[...], inverse_one)
        lower[...] = carried[...].astype(BF)
        note(2, column_sum(lower[...]))
        grad_rows[...] = matmul_right_t(lower[...], weight()[...]).astype(BF)
        pump(next(turn))
        ready(b, "mixed", "query", "kv")
        if not in_late:
            attention_grads(3, mixed[...].astype(BF), lower[...])
        keys = KeyGrads(place, grad_kv, kv_core, kv_far, kv_send.at[b], kv_recv.at[b], credit.at[3])
        if b == 0:
            keys.acquire()
        for half in range(2):
            attend_back(query, kv, half, mask, stats_rows, mixed, grad_rows, grad_query, grad_kv)
            keys.start(half)
            if half == 1:
                keys.middle(0)
            pump(next(turn))
        keys.middle(1)
        if out_late:
            for c in range(4):
                out_grads(c)
        pump(next(turn))
        if in_late:
            for c in range(4):
                in_grads(c)
            attention_grads(3, mixed[...].astype(BF), lower[...])
        if b == 1:
            load(0, "hat_one", "stats", "active", "mixed", "query", "kv")
        ready(b, "x")
        attention_grads(0, x[...], grad_query[...])
        note(0, column_sum(grad_query[...]))
        carried[...] += matmul_right_t(grad_query[...], weight()[...])
        pump(next(turn))
        for kind in range(2):
            for half in range(2):
                lower[:, half * (D // 2) : (half + 1) * (D // 2)] = keys.end(half, kind)
            attention_grads(1 + kind, x[...], lower[...])
            if kind == 1:
                note(1, column_sum(lower[...]))
            carried[...] += matmul_right_t(lower[...], weight()[...])
        sent(b, 0)
        pump(next(turn))
        keys.drain()
        if b == 1:
            keys.release()
            load(0, "x")
    small_sum = SmallReduce(place, small_total, small_landing, small_send, small_recv)
    small_steps = small_sum.steps()
    while active_plans or small_steps:
        if small_steps:
            small_steps.pop(0)()
        pump()
    out_small[...] = small_total[4]
    for key, group in reduces.items():
        group.finish()
        group.drain()
    for copy in small_sum.copies:
        copy.wait_send()


def backward_pass(n, ny, upstream, mask, narrow, fulls, kvs, saved):
    rows, width = upstream.shape[0], D // n
    nc = 2 * ny
    out = [jax.ShapeDtypeStruct((2,) + shape, BF) for shape in ((4, width, D), (width, 4 * D), (4, width, D))]
    out += [jax.ShapeDtypeStruct((2 * ROWS, D), F32), jax.ShapeDtypeStruct((rows, D), F32)]
    anywhere = pl.BlockSpec(memory_space=pl.ANY)
    vmem = pl.BlockSpec(memory_space=pltpu.VMEM)
    smalls = SmallReduce.count(n, ny)
    ahead = 4 if ny == 2 else 2
    scratch = [pltpu.VMEM((ahead, D, D), BF)]
    scratch += [pltpu.VMEM(item.shape[1:], item.dtype) for item in saved]
    scratch += [pltpu.VMEM(kvs[0].shape, BF)]
    scratch += [pltpu.VMEM((n, 4, width, D), BF)] * 3
    for _ in range(3):
        scratch += Reduce.landing_buffers(n, ny)
    scratch += [pltpu.VMEM((2, 2, nc, rows, D // 2), BF)]
    scratch += [pltpu.VMEM((2, 2, ny, rows, D // 2), BF), pltpu.VMEM((2, 2, ny - 1, rows, D // 2), BF)]
    scratch += [
        pltpu.VMEM((rows, D), F32),
        pltpu.VMEM((rows, D), BF),
        pltpu.VMEM((rows, D) if ny == 2 else (16, 128), BF),
        pltpu.VMEM((rows, D) if ny == 2 else (16, 128), BF),
        pltpu.VMEM((rows, D), BF),
        pltpu.VMEM((rows, D), BF),
        pltpu.VMEM((128, rows), F32),
        pltpu.VMEM((5, 2 * ROWS, D), F32),
        pltpu.VMEM((smalls, 2 * ROWS, D), F32),
        pltpu.VMEM((4, rows, D) if ny == 2 else (16, 128), BF),
        pltpu.SemaphoreType.DMA((len(SAVED) + 1,)),
        pltpu.SemaphoreType.DMA((ahead,)),
        pltpu.SemaphoreType.DMA((6,)),
        pltpu.SemaphoreType.DMA((6, Reduce.count(n, ny))),
        pltpu.SemaphoreType.DMA((6, Reduce.count(n, ny))),
        pltpu.SemaphoreType.REGULAR((4,)),
        pltpu.SemaphoreType.DMA((2, 2, KeyGrads.count(ny))),
        pltpu.SemaphoreType.DMA((2, 2, KeyGrads.count(ny))),
        pltpu.SemaphoreType.DMA((smalls,)),
        pltpu.SemaphoreType.DMA((smalls,)),
    ]
    return pl.pallas_call(
        functools.partial(backward_kernel, n, ny),
        out_shape=out,
        in_specs=[vmem] * 3 + [anywhere] * 16,
        out_specs=[anywhere] * 3 + [vmem] * 2,
        scratch_shapes=scratch,
        compiler_params=pltpu.CompilerParams(
            collective_id=1, has_side_effects=True, vmem_limit_bytes=63 * MIB
        ),
        name="backward_pass",
    )(upstream, mask, narrow, *fulls, *kvs, *saved)


def body(
    tokens,
    lengths,
    cotangent,
    w_qkv,
    w_attn_out,
    w_in,
    w_out,
    bias_q,
    bias_d,
    bias_ff,
    norm_gain,
    norm_shift,
    n,
    ny,
):
    row_count = tokens.shape[1]
    width = D // n
    z = lax.axis_index("fsdp")
    first_row = lax.axis_index("ctx") * row_count
    upstream = jnp.where((first_row + jnp.arange(row_count) < lengths[0])[:, None], cotangent[0], 0)
    mask = jnp.where(jnp.arange(2 * ny * row_count) < lengths[0], 0.0, masked_value).astype(F32)
    mask_row = jnp.broadcast_to(mask[None], (8, mask.shape[0]))
    small = jnp.concatenate(
        [
            bias_q,
            bias_d.reshape(6, width),
            norm_gain.reshape(4, width),
            norm_shift.reshape(4, width),
            bias_ff.reshape(8, width),
            jnp.zeros((8, width), BF),
        ],
        axis=0,
    )
    made = forward_pass(
        n, ny, tokens[0], mask_row, w_qkv, w_attn_out, w_in, w_out.reshape(2, 4, width, D), small
    )
    fulls, kvs, saved = made[:6], made[6:8], made[8:16]
    narrow, _, result = made[16:]
    fulls = [full.reshape(4, D, D) for full in fulls]
    *sums, small_sum, grad_tokens = backward_pass(n, ny, upstream, mask[:, None], narrow, fulls, kvs, saved)
    small_sum = small_sum.reshape(2, ROWS, D)
    own = lax.dynamic_slice_in_dim(small_sum, z * width, width, 2)
    own_ff = lax.dynamic_slice_in_dim(small_sum[:, 8:].reshape(2, 4 * D), z * 4 * width, 4 * width, 1)
    return (
        result[None],
        grad_tokens[None],
        sums[0][:, :3].astype(F32),
        sums[0][:, 3].astype(F32),
        sums[1].astype(F32),
        sums[2].reshape(2, 4 * width, D).astype(F32),
        own[:, 0],
        own[:, 1:4],
        own_ff,
        own[:, 4:6],
        own[:, 6:8],
    )


def solution(mesh):
    placed = (
        P(("rep", "fsdp"), "ctx", None),
        P(("rep", "fsdp")),
        P(("rep", "fsdp"), "ctx", None),
        P(None, None, "fsdp", None),
        P(None, "fsdp", None),
        P(None, "fsdp", None),
        P(None, "fsdp", None),
        P(None, "fsdp"),
        P(None, None, "fsdp"),
        P(None, "fsdp"),
        P(None, None, "fsdp"),
        P(None, None, "fsdp"),
    )
    n, ny = mesh.shape["fsdp"], mesh.shape["ctx"] // 2
    return jax.shard_map(
        functools.partial(body, n=n, ny=ny),
        mesh=mesh,
        in_specs=placed,
        out_specs=(
            P(("rep", "fsdp"), "ctx", None),
            P(("rep", "fsdp"), "ctx", None),
            P(None, None, "fsdp", None),
            P(None, "fsdp", None),
            P(None, "fsdp", None),
            P(None, "fsdp", None),
            P(None, "fsdp"),
            P(None, None, "fsdp"),
            P(None, "fsdp"),
            P(None, None, "fsdp"),
            P(None, None, "fsdp"),
        ),
        check_vma=False,
    )
```

```python
import functools

import jax
import jax.numpy as jnp
from jax import lax
from jax.experimental import pallas as pl
from jax.experimental.pallas import tpu as pltpu
from jax.sharding import PartitionSpec as P

HEADS = 12
HEAD = 64
D = HEADS * HEAD
MESH = pl.DeviceIdType.MESH
BF = jnp.bfloat16
F32 = jnp.float32
MIB = 2**20
GATHER_CUT, REDUCE_CUT = 1, 3

epsilon = 1e-05
score_scale = 0.125
masked_value = -1e30


class Place:
    def __init__(self, n, ny):
        self.n, self.ny = n, ny
        self.r = lax.axis_index("rep")
        self.z = lax.axis_index("fsdp")
        self.c = lax.axis_index("ctx")
        self.y, self.k = lax.div(self.c, 2), lax.rem(self.c, 2)
        self.e = lax.rem(self.y, 2)
        self.q = 2 * self.e + self.r
        self.qx = 2 * self.e + (1 - self.r)
        self.qy = 2 * (1 - self.e) + self.r
        self.qd = 2 * (1 - self.e) + (1 - self.r)

    def shard(self, offset):
        return lax.rem(self.z + (offset + self.n), self.n)

    def up(self, offset):
        return (self.r, self.shard(offset), self.c)

    def x(self):
        return (1 - self.r, self.z, self.c)

    def across(self):
        return (self.r, self.z, 2 * (self.y + 1 - 2 * self.e) + self.k)

    def row(self, offset, flip=0):
        y = lax.rem(self.y + offset, self.ny)
        k = self.k + flip * (1 - 2 * self.k)
        return (self.r, self.z, 2 * y + k)

    def core(self):
        return self.row(0, 1)

    def greet(self):
        others = [self.up(o) for o in range(1, self.n)]
        others += [self.x(), self.core()]
        others += [self.row(o) for o in range(1, self.ny)]
        barrier = pltpu.get_barrier_semaphore()
        for other in others:
            pl.semaphore_signal(barrier, inc=1, device_id=other, device_id_type=MESH)
        pl.semaphore_wait(barrier, len(others))


def remote(src, dst, send, recv, device):
    copy = pltpu.make_async_remote_copy(
        src_ref=src, dst_ref=dst, send_sem=send, recv_sem=recv, device_id=device, device_id_type=MESH
    )
    copy.start()
    return copy


def cut(half, sixths):
    first = max(8, half * sixths // 96 * 16)
    return [(0, first), (first, half - first)]


class Gather:
    def __init__(self, place, full, by_shard, local, send, recv):
        self.place, self.full, self.by_shard = place, full, by_shard
        self.local, self.send, self.recv = local, send, recv
        self.n = place.n
        self.half = full.shape[2] // 2
        self.pieces = cut(self.half, GATHER_CUT)
        self.copies, self.core_copies = [], []

    @staticmethod
    def count(n):
        return 10 * (n - 1)

    def part(self, shard, q, piece=None):
        start, size = (0, self.half) if piece is None else piece
        rows = pl.ds(pl.multiple_of(self.place.k * self.half + start, 8), size)
        return self.full.at[shard, q, rows] if self.by_shard else self.full.at[q, shard, rows]

    def load(self, sources):
        self.loads = []
        z = self.place.z
        for i, (q, count, source) in enumerate(sources):
            if self.by_shard:
                target = self.full.at[z]
            elif count is None:
                target = self.full.at[q, z]
            else:
                target = self.full.at[pl.ds(q, count), z]
            copy = pltpu.make_async_copy(source, target, self.local.at[i])
            copy.start()
            self.loads.append(copy)

    def share(self, kind, offset, piece, device):
        slot = kind * (self.n - 1) + offset - 1
        copy = remote(piece, piece, self.send.at[slot], self.recv.at[slot], device)
        self.copies.append(copy)
        return copy

    def core_share(self, kind, offset, piece):
        copy = self.share(5 + kind, offset, piece, self.place.core())
        self.core_copies.append(copy)

    def start(self):
        place = self.place
        for copy in self.loads:
            copy.wait()
        mine = self.part(place.z, place.q)
        self.ups = [self.share(0, o, mine, place.up(o)) for o in range(1, self.n)]

    def to_x(self):
        place = self.place
        self.xs = []
        for o in range(1, self.n):
            self.ups[o - 1].wait_recv()
            piece = self.part(place.shard(-o), place.q)
            self.xs.append(self.share(1, o, piece, place.x()))
            self.core_share(0, o, piece)

    def to_y(self):
        place = self.place
        self.ys = [
            self.share(2, o, self.part(place.shard(-o), place.q), place.across()) for o in range(1, self.n)
        ]

    def from_x(self):
        place = self.place
        self.dys = []
        for o in range(1, self.n):
            shard = place.shard(-o)
            self.xs[o - 1].wait_recv()
            self.dys.append(self.share(3, o, self.part(shard, place.qx, self.pieces[0]), place.across()))
            self.core_share(1, o, self.part(shard, place.qx))

    def from_y(self):
        place = self.place
        self.dxs = []
        for o in range(1, self.n):
            shard = place.shard(-o)
            self.ys[o - 1].wait_recv()
            self.dxs.append(self.share(4, o, self.part(shard, place.qy, self.pieces[1]), place.x()))
            self.core_share(2, o, self.part(shard, place.qy))

    def last(self):
        place = self.place
        for o in range(1, self.n):
            shard = place.shard(-o)
            self.dys[o - 1].wait_recv()
            self.core_share(3, o, self.part(shard, place.qd, self.pieces[0]))
        for o in range(1, self.n):
            shard = place.shard(-o)
            self.dxs[o - 1].wait_recv()
            self.core_share(4, o, self.part(shard, place.qd, self.pieces[1]))

    def finish(self):
        for copy in self.core_copies:
            copy.wait_recv()

    def drain(self):
        for copy in self.copies:
            copy.wait_send()

    def steps(self):
        return dict(A=self.start, B=self.to_x, Y=self.to_y, C=self.from_x, E=self.from_y, L=self.last, F=self.finish)


def weight_sources(b, qkv, ao, win, wout):
    return [
        [(0, 3, qkv.at[b]), (3, None, ao.at[b])],
        [(q, None, win.at[b, :, pl.ds(q * D, D)]) for q in range(4)],
        [(None, None, wout.at[b])],
    ]


class Reduce:
    def __init__(self, place, grad, landing, out, wide, local, send, recv, credit):
        self.place, self.grad, self.out, self.wide = place, grad, out, wide
        self.core_in, self.x_in, self.y_in, self.dx_in, self.dy_in, self.z_in, self.far_in = landing
        self.local, self.send, self.recv, self.credit = local, send, recv, credit
        self.n, self.ny = place.n, place.ny
        self.half = grad.shape[2] // 2
        self.low, self.top = cut(self.half, REDUCE_CUT)
        self.copies, self.cored, self.owns = [], [], []
        self.slot = 0
        self.plan = [self.add_cores, self.plane, self.depth, self.total, self.turn, self.last]

    @staticmethod
    def count(n, ny):
        return 4 + 6 + (n - 1) + (ny // 2 - 1) + 9

    @staticmethod
    def landing_buffers(n, ny):
        half = D // n // 2
        (_, second), (_, first) = cut(half, REDUCE_CUT)
        return [
            pltpu.VMEM((n, 4, half, D), BF),
            pltpu.VMEM((n, half, D), BF),
            pltpu.VMEM((n, half, D), BF),
            pltpu.VMEM((n, first, D), BF),
            pltpu.VMEM((n, second, D), BF),
            pltpu.VMEM((n - 1, half, D), BF),
            pltpu.VMEM((max(1, ny // 2 - 1), half, D), BF),
        ]

    def peers(self):
        place = self.place
        others = [place.up(o) for o in range(1, self.n)] + [place.x(), place.across(), place.core()]
        return others + [place.row(2 * i + 2) for i in range(self.ny // 2 - 1)]

    def release(self):
        for other in self.peers():
            pl.semaphore_signal(self.credit, inc=1, device_id=other, device_id_type=MESH)

    def acquire(self):
        pl.semaphore_wait(self.credit, len(self.peers()))

    def share(self, src, dst, device):
        copy = remote(src, dst, self.send.at[self.slot], self.recv.at[self.slot], device)
        self.slot += 1
        self.copies.append(copy)
        return copy

    def rows(self, k, piece=None):
        start, size = (0, self.half) if piece is None else piece
        return pl.ds(pl.multiple_of(k * self.half + start, 8), size)

    def own(self, shards, q, piece=None):
        return self.grad.at[shards, q, self.rows(self.place.k, piece)]

    def core(self, shards, q):
        source = self.grad.at[shards, q, self.rows(1 - self.place.k)]
        self.cored.append(self.share(source, self.core_in.at[shards, q], self.place.core()))

    def add_into(self, target, *sources):
        total = target[...].astype(F32)
        for source in sources:
            total = total + source[...].astype(F32)
        target[...] = total.astype(BF)

    def add_cores(self):
        for copy in self.cored:
            copy.wait_recv()

        def one(i, _):
            shard, q = lax.div(i, 4), lax.rem(i, 4)
            self.add_into(self.own(shard, q), self.core_in.at[shard, q])
            return 0

        lax.fori_loop(0, 4 * self.n, one, 0)
        place, every = self.place, slice(None)
        top, low = pl.ds(*self.top), pl.ds(*self.low)
        self.dx = self.share(self.own(every, place.qd, self.top), self.dx_in, place.x())
        self.dy = self.share(self.own(every, place.qd, self.low), self.dy_in, place.across())
        self.planes = [
            self.share(self.own(every, place.qx, self.top), self.x_in.at[:, top], place.x()),
            self.share(self.own(every, place.qy, self.low), self.y_in.at[:, low], place.across()),
        ]

    def plane(self):
        place, every = self.place, slice(None)
        top, low = pl.ds(*self.top), pl.ds(*self.low)
        self.dx.wait_recv()

        def one(j, _):
            self.add_into(self.own(j, place.qy, self.top), self.dx_in.at[j])
            return 0

        lax.fori_loop(0, self.n, one, 0)
        self.planes.append(
            self.share(self.own(every, place.qy, self.top), self.y_in.at[:, top], place.across())
        )
        self.dy.wait_recv()

        def two(j, _):
            self.add_into(self.own(j, place.qx, self.low), self.dy_in.at[j])
            return 0

        lax.fori_loop(0, self.n, two, 0)
        self.planes.append(self.share(self.own(every, place.qx, self.low), self.x_in.at[:, low], place.x()))

    def depth(self):
        place = self.place
        for copy in self.planes:
            copy.wait_recv()

        def one(j, _):
            self.add_into(self.own(j, place.q), self.x_in.at[j], self.y_in.at[j])
            return 0

        lax.fori_loop(0, self.n, one, 0)
        self.deep = [
            self.share(self.own(place.shard(o), place.q), self.z_in.at[o - 1], place.up(o))
            for o in range(1, self.n)
        ]

    def mine(self, q, piece=None):
        rows = self.rows(self.place.k, piece)
        if self.wide:
            return self.out.at[rows, pl.ds(pl.multiple_of(q * D, D), D)]
        return self.out.at[q, rows]

    def total(self):
        place = self.place
        for copy in self.deep:
            copy.wait_recv()
        own = self.own(place.z, place.q)
        self.add_into(own, *[self.z_in.at[o - 1] for o in range(1, self.n)])
        if self.ny > 2:
            far = [self.share(own, self.far_in.at[i], place.row(2 * i + 2)) for i in range(self.ny // 2 - 1)]
            for copy in far:
                copy.wait_recv()
            mine = own[...].astype(F32)
            terms = [mine] + [self.far_in[i].astype(F32) for i in range(self.ny // 2 - 1)]
            total = jnp.zeros_like(mine)
            for y in range(0, self.ny, 2):
                offset = lax.rem(place.y - place.e - y + self.ny, self.ny)
                for i, term in enumerate(terms):
                    total = total + jnp.where(offset == 2 * i, term, 0.0)
            for copy in far:
                copy.wait_send()
            self.copies = [copy for copy in self.copies if all(copy is not other for other in far)]
            own[...] = total.astype(BF)
        copy = pltpu.make_async_copy(own, self.mine(place.q), self.local)
        copy.start()
        self.owns.append(copy)
        self.spread = [
            self.share(own, self.mine(place.q), place.x()),
            self.share(own, self.mine(place.q), place.across()),
        ]
        self.cores = [self.share(own, self.mine(place.q), place.core())]

    def forward(self, q, device, piece=None):
        return self.share(self.mine(q, piece), self.mine(q, piece), device)

    def turn(self):
        place = self.place
        self.spread[0].wait_recv()
        self.dy = self.forward(place.qx, place.across(), self.top)
        self.cores.append(self.forward(place.qx, place.core()))
        self.spread[1].wait_recv()
        self.dx = self.forward(place.qy, place.x(), self.low)
        self.cores.append(self.forward(place.qy, place.core()))

    def last(self):
        place = self.place
        self.dy.wait_recv()
        self.cores.append(self.forward(place.qd, place.core(), self.top))
        self.dx.wait_recv()
        self.cores.append(self.forward(place.qd, place.core(), self.low))

    def finish(self):
        for copy in self.cores:
            copy.wait_recv()

    def drain(self):
        for copy in self.copies:
            copy.wait_send()
        for copy in self.owns:
            copy.wait()
        self.copies, self.owns = [], []


class SmallReduce:
    def __init__(self, place, total, landing, send, recv):
        self.place, self.total, self.landing, self.send, self.recv = place, total, landing, send, recv
        n, ny = place.n, place.ny
        self.stages = [
            [place.core()],
            [place.up(o) for o in range(1, n)],
            [place.x()],
            [place.row(o) for o in range(1, ny)],
        ]
        self.copies = []
        self.slot = 0

    @staticmethod
    def count(n, ny):
        return 1 + (n - 1) + 1 + (ny - 1)

    def start(self, stage):
        self.current = []
        for device in self.stages[stage]:
            slot = self.slot
            copy = remote(
                self.total.at[stage], self.landing.at[slot], self.send.at[slot], self.recv.at[slot], device
            )
            self.current.append((slot, copy))
            self.copies.append(copy)
            self.slot += 1

    def end(self, stage):
        place, ny = self.place, self.place.ny
        for _, copy in self.current:
            copy.wait_recv()
        terms = [self.total[stage]] + [self.landing[slot] for slot, _ in self.current]
        if stage == 3 and ny > 2:
            total = jnp.zeros_like(terms[0])
            for y in range(ny):
                offset = lax.rem(place.y - y + ny, ny)
                for o in range(ny):
                    total = total + jnp.where(offset == o, terms[o], 0.0)
        else:
            total = functools.reduce(lambda a, b: a + b, terms)
        self.total[stage + 1] = total

    def steps(self):
        out = [functools.partial(self.start, 0)]
        for stage in range(4):
            out.append(functools.partial(self.end, stage))
            if stage < 3:
                out.append(functools.partial(self.start, stage + 1))
        return out


def matmul(operand_a, operand_b):
    return jnp.dot(operand_a, operand_b, preferred_element_type=F32)


def matmul_left_t(operand_a, operand_b):
    return lax.dot_general(operand_a, operand_b, (((0,), (0,)), ((), ())), preferred_element_type=F32)


def matmul_right_t(operand_a, operand_b):
    return lax.dot_general(operand_a, operand_b, (((1,), (1,)), ((), ())), preferred_element_type=F32)


def unit(ref, index, columns=None):
    block = ref[index] if columns is None else ref[index, :, :, columns]
    return block.reshape(D, block.shape[-1])


def center_scale(rows):
    center = rows - jnp.mean(rows, axis=-1, keepdims=True)
    inverse = lax.rsqrt(jnp.mean(center * center, axis=-1, keepdims=True) + epsilon)
    return center * inverse, inverse


class Exchange:
    def __init__(self, place, kv, send, recv):
        self.place, self.kv, self.send, self.recv = place, kv, send, recv
        self.copies = []

    @staticmethod
    def count(ny):
        return 2 * ny

    def share(self, half, chip_row, slot, device):
        part = self.kv.at[:, half, 2 * chip_row + self.place.k]
        copy = remote(part, part, self.send.at[half, slot], self.recv.at[half, slot], device)
        self.copies.append(copy)
        return copy

    def start(self, half):
        place, ny = self.place, self.place.ny
        far = [self.share(half, place.y, o, place.row(o)) for o in range(1, ny)]
        near = [self.share(half, place.y, 0, place.core())]
        return far, near

    def forward(self, half, state):
        place, ny = self.place, self.place.ny
        far, near = state
        for o in range(1, ny):
            far[o - 1].wait_recv()
            near.append(self.share(half, lax.rem(place.y - o + ny, ny), ny + o - 1, place.core()))

    def finish(self, state):
        for copy in state[1]:
            copy.wait_recv()

    def drain(self):
        for copy in self.copies:
            copy.wait_send()


def spread_small(n, small_full, wide_full, narrow, wide):
    width = small_full.shape[2]
    row = lax.broadcasted_iota(jnp.int32, (width, D), 0)
    column = lax.broadcasted_iota(jnp.int32, (width, D), 1)
    total = 0.0
    for j in range(n):
        place = jnp.where(column - row == j * width, 1.0, 0.0).astype(BF)
        total = total + matmul(small_full[j], place)
    narrow[...] = total
    turns = n // 4
    for c in range(4):
        if turns == 1:
            total = wide_full[c].astype(F32)
        else:
            row = lax.broadcasted_iota(jnp.int32, (4 * width, D), 0)
            column = lax.broadcasted_iota(jnp.int32, (4 * width, D), 1)
            total = 0.0
            for t in range(turns):
                place = jnp.where(column - row == t * 4 * width, 1.0, 0.0).astype(BF)
                total = total + matmul(wide_full[c * turns + t], place)
        for b in range(2):
            wide[b, c : c + 1] = total[b : b + 1]


def side_mask(side):
    lane = lax.broadcasted_iota(jnp.int32, (1, 2 * HEAD), 1)
    inside = lane < HEAD if side == 0 else lane >= HEAD
    return jnp.where(inside, 1.0, 0.0).astype(BF)


def attend(query, kv, half, mask, out, stats, first_head):
    rows = query.shape[0]
    lane = lax.broadcasted_iota(jnp.int32, (rows, 2 * HEAD), 1)
    allowed = mask[0:1]

    def pair(p, _):
        columns = pl.ds(pl.multiple_of(p * 2 * HEAD, 2 * HEAD), 2 * HEAD)
        where = pl.ds(pl.multiple_of(half * (D // 2) + p * 2 * HEAD, 2 * HEAD), 2 * HEAD)
        keys = kv[0, half, :, :, columns].reshape(-1, 2 * HEAD)
        values = kv[1, half, :, :, columns].reshape(-1, 2 * HEAD)
        query_pair = query[:, where]
        mixed = []
        for side in range(2):
            scores = matmul_right_t(query_pair * side_mask(side), keys) + allowed
            peak = jnp.max(scores, axis=-1, keepdims=True)
            weight = jnp.exp(scores - peak)
            total = jnp.sum(weight, axis=-1, keepdims=True)
            mixed.append(matmul((weight / total).astype(BF), values))
            head = first_head + 2 * p + side
            stats[...] = jnp.where(lane == head, peak + jnp.log(total), stats[...])
        out[:, where] = jnp.where(lane < HEAD, mixed[0], mixed[1])
        return 0

    lax.fori_loop(0, HEADS // 4, pair, 0)


SCHEDULE = [
    "A0 B0 Y0 A1",
    [
        "C0 E0 B1 Y1 A2 L0 C1 E1 B2 Y2 A3 F0",
        "L1 C2 E2 B3 Y3 A4",
        "F1 L2",
        "C3 E3 B4 Y4",
        "A5 F2",
        "L3",
        "C4 E4",
        "B5 Y5",
        "F3",
        "",
    ],
    ["L4", "C5 E5 F4", "L5", "F5", "", "", "", "", "", ""],
]

SAVED = ("x", "query", "mixed", "stats", "hat_one", "active", "slope", "hat_two")


def forward_kernel(n, ny, *refs):
    tokens, mask, qkv, ao, win, wout, query_bias, bias_rows, wide_bias, gains, shifts = refs[:11]
    refs = refs[11:]
    outs = refs[:6]
    kv_outs, saved_outs = refs[6:8], refs[8:16]
    narrow_out, wide_out, result = refs[16:19]
    refs = refs[19:]
    fulls, kvs, saved = refs[:6], refs[6:8], refs[8:16]
    carried, normed, normed_bf, small_full, wide_full, small_rows, wide_rows = refs[16:23]
    local, send, recv, small_send, small_recv, kv_send, kv_recv, save_sem = refs[23:]
    place = Place(n, ny)
    groups = []
    for g in range(6):
        b, kind = g // 3, g % 3
        group = Gather(place, fulls[g], kind == 2, local.at[g], send.at[g], recv.at[g])
        group.load(weight_sources(b, qkv, ao, win, wout)[kind])
        groups.append(group)
    small_rows[0:2] = query_bias[...].astype(F32)
    for b in range(2):
        small_rows[2 + 3 * b : 5 + 3 * b] = bias_rows[b].astype(F32)
        small_rows[8 + 2 * b : 10 + 2 * b] = gains[b].astype(F32)
        small_rows[12 + 2 * b : 14 + 2 * b] = shifts[b].astype(F32)
    wide_rows[...] = jnp.zeros_like(wide_rows)
    wide_rows[0:2] = wide_bias[...].astype(F32)
    small_full[place.z] = small_rows[...].astype(BF)
    wide_full[place.z] = wide_rows[...].astype(BF)
    place.greet()
    smalls = []
    for i, ref in enumerate((small_full, wide_full)):
        own = ref.at[place.z]
        smalls += [
            remote(own, own, small_send.at[i, o], small_recv.at[i, o], place.up(o)) for o in range(1, n)
        ]
    kept = []

    def keep(source, target, sem):
        copy = pltpu.make_async_copy(source, target, sem)
        copy.start()
        kept.append(copy)

    plans = [group.steps() for group in groups]

    def run(steps):
        for name in steps.split():
            g = int(name[1])
            plans[g].pop(name[0])()
            if name[0] == "F":
                keep(fulls[g], outs[g], local.at[g, 4])

    carried[...] = tokens[...].astype(F32)
    run(SCHEDULE[0])
    for copy in smalls:
        copy.wait_recv()
    spread_small(n, small_full, wide_full, narrow_out, wide_out)
    x, query, mixed, stats, hat_one, active, slope, hat_two = saved
    for b in range(2):
        first, second, third = fulls[3 * b : 3 * b + 3]

        def save(*names):
            for name in names:
                i = SAVED.index(name)
                keep(saved[i].at[b], saved_outs[i].at[b], save_sem.at[b, i])

        turn = iter(SCHEDULE[1 + b])
        run(next(turn))
        x[b] = carried[...].astype(BF)
        exchange = Exchange(place, kvs[b], kv_send.at[b], kv_recv.at[b])
        states = []
        for half in range(2):
            columns = slice(half * (D // 2), (half + 1) * (D // 2))
            kvs[b][0, half, place.c] = matmul(x[b], unit(first, 1, columns)).astype(BF)
            value_bias = narrow_out[2 + 3 * b : 3 + 3 * b, columns]
            kvs[b][1, half, place.c] = (matmul(x[b], unit(first, 2, columns)) + value_bias).astype(BF)
            states.append(exchange.start(half))
        run(next(turn))
        projected = (matmul(x[b], unit(first, 0)) + narrow_out[b : b + 1]).astype(BF)
        query[b] = projected * jnp.asarray(score_scale, BF)
        stats[b] = jnp.zeros_like(stats[b])
        save("x", "query")
        for half in range(2):
            exchange.forward(half, states[half])
            exchange.finish(states[half])
            if half == 1:
                run(next(turn))
            attend(query.at[b], kvs[b], half, mask, mixed.at[b], stats.at[b], half * (HEADS // 2))
        run(next(turn))
        keep(kvs[b], kv_outs[b], save_sem.at[b, len(SAVED)])
        attended = matmul(mixed[b].astype(BF), unit(first, 3))
        hat, inverse = center_scale(carried[...] + attended + narrow_out[3 + 3 * b : 4 + 3 * b])
        hat_one[b] = hat
        lane = lax.broadcasted_iota(jnp.int32, stats.shape[1:], 1)
        stats[b] = jnp.where(lane == HEADS, inverse, stats[b])
        normed[...] = hat * narrow_out[8 + 2 * b : 9 + 2 * b] + narrow_out[12 + 2 * b : 13 + 2 * b]
        normed_bf[...] = normed[...].astype(BF)
        save("mixed", "hat_one")
        run(next(turn))
        for c in range(4):
            hidden = matmul(normed_bf[...], unit(second, c)) + wide_out[b, c : c + 1]
            cdf = 0.5 + 0.5 * lax.erf(hidden * (2.0**-0.5))
            pdf = jnp.exp(-0.5 * hidden * hidden) * ((2.0 * jnp.pi) ** -0.5)
            active[b, c] = (hidden * cdf).astype(BF)
            slope[b, c] = (cdf + hidden * pdf).astype(BF)
            run(next(turn))
        save("active", "slope")
        run(next(turn))
        update = normed[...] + narrow_out[4 + 3 * b : 5 + 3 * b]
        for c in range(4):
            update = update + matmul(active[b, c], third[c * n // 4 : (c + 1) * n // 4].reshape(D, D))
        hat, inverse = center_scale(update)
        hat_two[b] = hat
        stats[b] = jnp.where(lane == HEADS + 1, inverse, stats[b])
        save("stats", "hat_two")
        carried[...] = hat * narrow_out[9 + 2 * b : 10 + 2 * b] + narrow_out[13 + 2 * b : 14 + 2 * b]
        exchange.drain()
    result[...] = carried[...].astype(BF)
    for group in groups:
        group.drain()
    for copy in smalls:
        copy.wait_send()
    for copy in kept:
        copy.wait()


def forward_pass(n, ny, tokens, mask, qkv, ao, win, wout, *smalls):
    rows, width = tokens.shape[0], D // n
    nc = 2 * ny
    full_shapes = [(4, n, width, D), (4, n, width, D), (n, 4, width, D)] * 2
    kv_shape = (2, 2, nc, rows, D // 2)
    saved_shapes = {
        "x": ((2, rows, D), BF),
        "query": ((2, rows, D), BF),
        "mixed": ((2, rows, D), F32),
        "stats": ((2, rows, 128), F32),
        "hat_one": ((2, rows, D), F32),
        "active": ((2, 4, rows, D), BF),
        "slope": ((2, 4, rows, D), BF),
        "hat_two": ((2, rows, D), F32),
    }
    out = [jax.ShapeDtypeStruct(shape, BF) for shape in full_shapes]
    out += [jax.ShapeDtypeStruct(kv_shape, BF)] * 2
    out += [jax.ShapeDtypeStruct(*saved_shapes[name]) for name in SAVED]
    out += [
        jax.ShapeDtypeStruct((16, D), F32),
        jax.ShapeDtypeStruct((2, 4, D), F32),
        jax.ShapeDtypeStruct((rows, D), BF),
    ]
    anywhere = pl.BlockSpec(memory_space=pl.ANY)
    vmem = pl.BlockSpec(memory_space=pltpu.VMEM)
    scratch = [pltpu.VMEM(shape, BF) for shape in full_shapes]
    scratch += [pltpu.VMEM(kv_shape, BF)] * 2
    scratch += [pltpu.VMEM(*saved_shapes[name]) for name in SAVED]
    scratch += [
        pltpu.VMEM((rows, D), F32),
        pltpu.VMEM((rows, D), F32),
        pltpu.VMEM((rows, D), BF),
        pltpu.VMEM((n, 16, width), BF),
        pltpu.VMEM((n, 16, 4 * width), BF),
        pltpu.VMEM((16, width), F32),
        pltpu.VMEM((16, 4 * width), F32),
        pltpu.SemaphoreType.DMA((6, 5)),
        pltpu.SemaphoreType.DMA((6, Gather.count(n))),
        pltpu.SemaphoreType.DMA((6, Gather.count(n))),
        pltpu.SemaphoreType.DMA((2, n)),
        pltpu.SemaphoreType.DMA((2, n)),
        pltpu.SemaphoreType.DMA((2, 2, Exchange.count(ny))),
        pltpu.SemaphoreType.DMA((2, 2, Exchange.count(ny))),
        pltpu.SemaphoreType.DMA((2, len(SAVED) + 1)),
    ]
    return pl.pallas_call(
        functools.partial(forward_kernel, n, ny),
        out_shape=out,
        in_specs=[vmem, vmem] + [anywhere] * 4 + [vmem] * 5,
        out_specs=[anywhere] * 16 + [vmem] * 3,
        scratch_shapes=scratch,
        compiler_params=pltpu.CompilerParams(
            collective_id=0, has_side_effects=True, vmem_limit_bytes=60 * MIB
        ),
        name="forward_pass",
    )(tokens, mask, qkv, ao, win, wout, *smalls)


def normal_back(grad_output, gain, hat, inverse):
    grad_hat = grad_output * gain
    mean = jnp.mean(grad_hat, axis=-1, keepdims=True)
    slant = jnp.mean(grad_hat * hat, axis=-1, keepdims=True)
    return inverse * (grad_hat - mean - hat * slant)


def column_sum(rows):
    return jnp.sum(rows.astype(F32), axis=0, keepdims=True)


class KeyGrads:
    def __init__(self, place, grads, core_in, far_in, send, recv, credit):
        self.place, self.grads, self.core_in, self.far_in = place, grads, core_in, far_in
        self.send, self.recv, self.credit = send, recv, credit
        self.copies = []
        self.cored, self.far = {}, {}

    def peers(self):
        return [self.place.core()] + [self.place.row(o) for o in range(1, self.place.ny)]

    def release(self):
        for other in self.peers():
            pl.semaphore_signal(self.credit, inc=1, device_id=other, device_id_type=MESH)

    def acquire(self):
        pl.semaphore_wait(self.credit, len(self.peers()))

    @staticmethod
    def count(ny):
        return 2 * ny - 1

    def share(self, half, slot, src, dst, device):
        copy = remote(src, dst, self.send.at[half, slot], self.recv.at[half, slot], device)
        self.copies.append(copy)
        return copy

    def start(self, half):
        place, ny = self.place, self.place.ny
        self.cored[half] = []
        for i in range(ny):
            y = lax.rem(place.y + i, ny)
            part = self.grads.at[:, half, 2 * y + 1 - place.k]
            self.cored[half].append(self.share(half, i, part, self.core_in.at[:, half, y], place.core()))

    def middle(self, half):
        place, ny = self.place, self.place.ny
        for copy in self.cored[half]:
            copy.wait_recv()
        for y in range(ny):
            for kind in range(2):
                part = self.grads.at[kind, half, 2 * y + place.k]
                part[...] = (part[...].astype(F32) + self.core_in[kind, half, y].astype(F32)).astype(BF)
        self.far[half] = []
        for o in range(1, ny):
            y = lax.rem(place.y + o, ny)
            part = self.grads.at[:, half, 2 * y + place.k]
            self.far[half].append(
                self.share(half, ny + o - 1, part, self.far_in.at[:, half, o - 1], place.row(o))
            )

    def end(self, half, kind):
        for copy in self.far[half]:
            if kind == 0:
                copy.wait_recv()
        total = self.grads[kind, half, self.place.c].astype(F32)
        for o in range(1, self.place.ny):
            total = total + self.far_in[kind, half, o - 1].astype(F32)
        return total.astype(BF)

    def drain(self):
        for copy in self.copies:
            copy.wait_send()


def attend_back(query, kv, half, mask, stats, mixed, grad_mixed, grad_query, grads):
    rows = query.shape[0]
    lane = lax.broadcasted_iota(jnp.int32, (rows, 2 * HEAD), 1)
    blocks = 4 if kv.shape[2] <= 4 else 2

    def pair(p, _):
        columns = pl.ds(pl.multiple_of(p * 2 * HEAD, 2 * HEAD), 2 * HEAD)
        where = pl.ds(pl.multiple_of(half * (D // 2) + p * 2 * HEAD, 2 * HEAD), 2 * HEAD)
        query_pair, grad_pair = query[:, where], grad_mixed[:, where]
        products = (mixed[:, where] * grad_pair.astype(F32)).T
        grad_queries = [0.0, 0.0]
        for at in range(0, kv.shape[2], blocks):
            some = slice(at, at + blocks)
            keys = kv[0, half, some, :, columns].reshape(-1, 2 * HEAD)
            values = kv[1, half, some, :, columns].reshape(-1, 2 * HEAD)
            blocked = mask[at * rows : (at + blocks) * rows, :]
            grad_keys, grad_values = 0.0, 0.0
            for side in range(2):
                query_side, grad_side = query_pair * side_mask(side), grad_pair * side_mask(side)
                log_sum = stats[pl.ds(half * (HEADS // 2) + 2 * p + side, 1), :]
                inner = jnp.sum(products[side * HEAD : (side + 1) * HEAD], axis=0, keepdims=True)
                probs = jnp.exp(matmul_right_t(keys, query_side) + blocked - log_sum)
                grad_probs = matmul_right_t(values, grad_side)
                grad_scores = (probs * (grad_probs - inner)).astype(BF)
                grad_keys = grad_keys + matmul(grad_scores, query_side)
                grad_values = grad_values + matmul(probs.astype(BF), grad_side)
                grad_queries[side] = grad_queries[side] + matmul_left_t(grad_scores, keys)
            grads[0, half, some, :, columns] = grad_keys.astype(BF).reshape(-1, rows, 2 * HEAD)
            grads[1, half, some, :, columns] = grad_values.astype(BF).reshape(-1, rows, 2 * HEAD)
        grad_query[:, where] = (
            jnp.where(lane < HEAD, grad_queries[0], grad_queries[1]) * score_scale
        ).astype(BF)
        return 0

    lax.fori_loop(0, HEADS // 4, pair, 0)


ROWS = 12
PUMPS = [[1, 1, 1, 0, 0, 1, 0, 0], [1, 1, 1, 0, 0, 1, 0, 0]]
OUT_LATE, IN_LATE = [False, False], [True, False]


def backward_kernel(n, ny, *refs):
    upstream, mask, narrow = refs[:3]
    fulls, kvs, saved = refs[3:9], refs[9:11], refs[11:19]
    outs, out_small, out_tokens = refs[19:22], refs[22], refs[23]
    refs = refs[24:]
    window, held, kv = refs[0], refs[1:9], refs[9]
    grads, landings = refs[10:13], [refs[13 + 7 * i : 20 + 7 * i] for i in range(3)]
    refs = refs[34:]
    grad_kv, kv_core, kv_far = refs[:3]
    deeper, lower, update_rows, normed_rows, grad_query, grad_rows, stats_rows = refs[3:10]
    small_total, small_landing = refs[10:12]
    hidden = refs[12]
    carried = out_tokens
    load_sem, window_sem, local, send, recv, credit, kv_send, kv_recv, small_send, small_recv = refs[13:]
    place = Place(n, ny)
    roomy = ny == 2
    x, query, mixed, stats, hat_one, active, slope, hat_two = held
    if not roomy:
        hidden, update_rows, normed_rows = active, lower, lower
    ahead = window.shape[0]
    loads = {}

    def load(b, *names):
        for name in names:
            i = SAVED.index(name) if name != "kv" else len(SAVED)
            source, target = (kvs[b], kv) if name == "kv" else (saved[i].at[b], held[i])
            loads[(b, name)] = pltpu.make_async_copy(source, target, load_sem.at[i])
            loads[(b, name)].start()

    def ready(b, *names):
        for name in names:
            loads[(b, name)].wait()

    order = []
    for b in (1, 0):
        order += [(b, 2, c) for c in range(4)] + [(b, 1, c) for c in range(4)]
        order += [(b, 0, 3), (b, 0, 0), (b, 0, 1), (b, 0, 2)]
    fetched = []

    def fetch():
        i = len(fetched)
        if i < len(order):
            b, kind, c = order[i]
            copy = pltpu.make_async_copy(
                fulls[3 * b + kind].at[c], window.at[i % ahead], window_sem.at[i % ahead]
            )
            copy.start()
            fetched.append(copy)

    used = []

    def weight():
        i = len(used)
        if i > 0:
            fetch()
        fetched[i].wait()
        used.append(i)
        return window.at[i % ahead]

    load(1, "hat_two", "stats", "active", "slope", "hat_one", "mixed", "query", "kv", "x")
    for _ in range(ahead - 1):
        fetch()
    reduces = {}
    for b in (1, 0):
        for kind in range(3):
            g = 3 * b + kind
            reduces[(b, kind)] = Reduce(
                place,
                grads[kind],
                landings[kind],
                outs[kind].at[b],
                kind == 1,
                local.at[g],
                send.at[g],
                recv.at[g],
                credit.at[kind],
            )
    active_plans = []
    steps = {key: list(group.plan) for key, group in reduces.items()}

    def step(key):
        steps[key].pop(0)()
        if len(steps[key]) == 2 and key[0] == 1:
            reduces[key].release()

    def pump(count=1):
        for _ in range(count):
            for key in list(active_plans):
                step(key)
                if not steps[key]:
                    active_plans.remove(key)

    def complete(key):
        while steps[key]:
            pump()
        reduces[key].drain()

    def begin(b, kind):
        if b == 0:
            complete((1, kind))

    def sent(b, kind):
        active_plans.append((b, kind))

    place.greet()
    carried[...] = upstream[...].astype(F32)
    for b in (1, 0):
        third, second, first = [reduces[(b, kind)] for kind in (2, 1, 0)]

        def note(i, row, b=b):
            small_total[0, ROWS * b + i : ROWS * b + i + 1] = row

        turn = iter(PUMPS[b])
        gain_one, gain_two = narrow[8 + 2 * b : 9 + 2 * b], narrow[9 + 2 * b : 10 + 2 * b]
        ready(b, "hat_two", "stats", "active")
        stats_rows[...] = stats[...].T
        inverse_one, inverse_two = stats[:, HEADS : HEADS + 1], stats[:, HEADS + 1 : HEADS + 2]
        note(5, column_sum(carried[...] * hat_two[...]))
        note(7, column_sum(carried[...]))
        grad = normal_back(carried[...], gain_two, hat_two[...], inverse_two)
        deeper[...] = grad
        update_rows[...] = grad.astype(BF)
        note(3, column_sum(update_rows[...]))
        if b == 1:
            load(0, "hat_two")
        part = n // 4

        def out_grads(c):
            if c == 0:
                begin(b, 2)
            block = matmul_left_t(active[c], update_rows[...]).astype(BF)
            shards = pl.ds(c * part, part)
            grads[2][shards] = block.reshape(part, 4, D // n, D)
            if c == 0 and b == 0:
                third.acquire()
            third.core(shards, slice(None))
            if c == 3:
                sent(b, 2)

        def in_grads(c):
            if c == 0:
                begin(b, 1)
                normed_rows[...] = (hat_one[...] * gain_one + narrow[12 + 2 * b : 13 + 2 * b]).astype(BF)
            block = matmul_left_t(normed_rows[...], hidden[c]).astype(BF)
            grads[1][:, c] = block.reshape(n, D // n, D)
            if c == 0 and b == 0:
                second.acquire()
            second.core(slice(None), c)
            if c == 3:
                sent(b, 1)

        def attention_grads(i, left, right):
            if i == 3:
                begin(b, 0)
            block = matmul_left_t(left, right).astype(BF)
            grads[0][:, i] = block.reshape(n, D // n, D)
            if i == 3 and b == 0:
                first.acquire()
            first.core(slice(None), i)

        out_late, in_late = roomy and OUT_LATE[b], roomy and IN_LATE[b]
        if not out_late:
            for c in range(4):
                out_grads(c)
        ready(b, "slope", "hat_one")
        for c in range(4):
            flow = matmul_right_t(update_rows[...], weight()[...]) * slope[c].astype(F32)
            hidden[c] = flow.astype(BF)
            note(8 + c, column_sum(hidden[c]))
        if b == 1:
            load(0, "slope")
        pump(next(turn))
        if not in_late:
            for c in range(4):
                in_grads(c)
        pump(next(turn))
        for c in range(4):
            deeper[...] += matmul_right_t(hidden[c], weight()[...])
        note(4, column_sum(deeper[...] * hat_one[...]))
        note(6, column_sum(deeper[...]))
        carried[...] = normal_back(deeper[...], gain_one, hat_one[...], inverse_one)
        lower[...] = carried[...].astype(BF)
        note(2, column_sum(lower[...]))
        grad_rows[...] = matmul_right_t(lower[...], weight()[...]).astype(BF)
        pump(next(turn))
        ready(b, "mixed", "query", "kv")
        if not in_late:
            attention_grads(3, mixed[...].astype(BF), lower[...])
        keys = KeyGrads(place, grad_kv, kv_core, kv_far, kv_send.at[b], kv_recv.at[b], credit.at[3])
        if b == 0:
            keys.acquire()
        for half in range(2):
            attend_back(query, kv, half, mask, stats_rows, mixed, grad_rows, grad_query, grad_kv)
            keys.start(half)
            if half == 1:
                keys.middle(0)
            pump(next(turn))
        keys.middle(1)
        if out_late:
            for c in range(4):
                out_grads(c)
        pump(next(turn))
        if in_late:
            for c in range(4):
                in_grads(c)
            attention_grads(3, mixed[...].astype(BF), lower[...])
        if b == 1:
            load(0, "hat_one", "stats", "active", "mixed", "query", "kv")
        ready(b, "x")
        attention_grads(0, x[...], grad_query[...])
        note(0, column_sum(grad_query[...]))
        carried[...] += matmul_right_t(grad_query[...], weight()[...])
        pump(next(turn))
        for kind in range(2):
            for half in range(2):
                lower[:, half * (D // 2) : (half + 1) * (D // 2)] = keys.end(half, kind)
            attention_grads(1 + kind, x[...], lower[...])
            if kind == 1:
                note(1, column_sum(lower[...]))
            carried[...] += matmul_right_t(lower[...], weight()[...])
        sent(b, 0)
        pump(next(turn))
        keys.drain()
        if b == 1:
            keys.release()
            load(0, "x")
    small_sum = SmallReduce(place, small_total, small_landing, small_send, small_recv)
    small_steps = small_sum.steps()
    while active_plans or small_steps:
        if small_steps:
            small_steps.pop(0)()
        pump()
    out_small[...] = small_total[4]
    for key, group in reduces.items():
        group.finish()
        group.drain()
    for copy in small_sum.copies:
        copy.wait_send()


def backward_pass(n, ny, upstream, mask, narrow, fulls, kvs, saved):
    rows, width = upstream.shape[0], D // n
    nc = 2 * ny
    out = [jax.ShapeDtypeStruct((2,) + shape, BF) for shape in ((4, width, D), (width, 4 * D), (4, width, D))]
    out += [jax.ShapeDtypeStruct((2 * ROWS, D), F32), jax.ShapeDtypeStruct((rows, D), F32)]
    anywhere = pl.BlockSpec(memory_space=pl.ANY)
    vmem = pl.BlockSpec(memory_space=pltpu.VMEM)
    smalls = SmallReduce.count(n, ny)
    ahead = 4 if ny == 2 else 2
    scratch = [pltpu.VMEM((ahead, D, D), BF)]
    scratch += [pltpu.VMEM(item.shape[1:], item.dtype) for item in saved]
    scratch += [pltpu.VMEM(kvs[0].shape, BF)]
    scratch += [pltpu.VMEM((n, 4, width, D), BF)] * 3
    for _ in range(3):
        scratch += Reduce.landing_buffers(n, ny)
    scratch += [pltpu.VMEM((2, 2, nc, rows, D // 2), BF)]
    scratch += [pltpu.VMEM((2, 2, ny, rows, D // 2), BF), pltpu.VMEM((2, 2, ny - 1, rows, D // 2), BF)]
    scratch += [
        pltpu.VMEM((rows, D), F32),
        pltpu.VMEM((rows, D), BF),
        pltpu.VMEM((rows, D) if ny == 2 else (16, 128), BF),
        pltpu.VMEM((rows, D) if ny == 2 else (16, 128), BF),
        pltpu.VMEM((rows, D), BF),
        pltpu.VMEM((rows, D), BF),
        pltpu.VMEM((128, rows), F32),
        pltpu.VMEM((5, 2 * ROWS, D), F32),
        pltpu.VMEM((smalls, 2 * ROWS, D), F32),
        pltpu.VMEM((4, rows, D) if ny == 2 else (16, 128), BF),
        pltpu.SemaphoreType.DMA((len(SAVED) + 1,)),
        pltpu.SemaphoreType.DMA((ahead,)),
        pltpu.SemaphoreType.DMA((6,)),
        pltpu.SemaphoreType.DMA((6, Reduce.count(n, ny))),
        pltpu.SemaphoreType.DMA((6, Reduce.count(n, ny))),
        pltpu.SemaphoreType.REGULAR((4,)),
        pltpu.SemaphoreType.DMA((2, 2, KeyGrads.count(ny))),
        pltpu.SemaphoreType.DMA((2, 2, KeyGrads.count(ny))),
        pltpu.SemaphoreType.DMA((smalls,)),
        pltpu.SemaphoreType.DMA((smalls,)),
    ]
    return pl.pallas_call(
        functools.partial(backward_kernel, n, ny),
        out_shape=out,
        in_specs=[vmem] * 3 + [anywhere] * 16,
        out_specs=[anywhere] * 3 + [vmem] * 2,
        scratch_shapes=scratch,
        compiler_params=pltpu.CompilerParams(
            collective_id=1, has_side_effects=True, vmem_limit_bytes=63 * MIB
        ),
        name="backward_pass",
    )(upstream, mask, narrow, *fulls, *kvs, *saved)


def body(
    tokens,
    lengths,
    cotangent,
    w_qkv,
    w_attn_out,
    w_in,
    w_out,
    bias_q,
    bias_d,
    bias_ff,
    norm_gain,
    norm_shift,
    n,
    ny,
):
    row_count = tokens.shape[1]
    width = D // n
    z = lax.axis_index("fsdp")
    first_row = lax.axis_index("ctx") * row_count
    upstream = jnp.where((first_row + jnp.arange(row_count) < lengths[0])[:, None], cotangent[0], 0)
    mask = jnp.where(jnp.arange(2 * ny * row_count) < lengths[0], 0.0, masked_value).astype(F32)
    mask_row = jnp.broadcast_to(mask[None], (8, mask.shape[0]))
    made = forward_pass(
        n, ny, tokens[0], mask_row, w_qkv, w_attn_out, w_in, w_out.reshape(2, 4, width, D),
        bias_q, bias_d, bias_ff, norm_gain, norm_shift
    )
    fulls, kvs, saved = made[:6], made[6:8], made[8:16]
    narrow, _, result = made[16:]
    fulls = [full.reshape(4, D, D) for full in fulls]
    *sums, small_sum, grad_tokens = backward_pass(n, ny, upstream, mask[:, None], narrow, fulls, kvs, saved)
    small_sum = small_sum.reshape(2, ROWS, D)
    own = lax.dynamic_slice_in_dim(small_sum, z * width, width, 2)
    own_ff = lax.dynamic_slice_in_dim(small_sum[:, 8:].reshape(2, 4 * D), z * 4 * width, 4 * width, 1)
    return (
        result[None],
        grad_tokens[None],
        sums[0][:, :3].astype(F32),
        sums[0][:, 3].astype(F32),
        sums[1].astype(F32),
        sums[2].reshape(2, 4 * width, D).astype(F32),
        own[:, 0],
        own[:, 1:4],
        own_ff,
        own[:, 4:6],
        own[:, 6:8],
    )


def solution(mesh):
    placed = (
        P(("rep", "fsdp"), "ctx", None),
        P(("rep", "fsdp")),
        P(("rep", "fsdp"), "ctx", None),
        P(None, None, "fsdp", None),
        P(None, "fsdp", None),
        P(None, "fsdp", None),
        P(None, "fsdp", None),
        P(None, "fsdp"),
        P(None, None, "fsdp"),
        P(None, "fsdp"),
        P(None, None, "fsdp"),
        P(None, None, "fsdp"),
    )
    n, ny = mesh.shape["fsdp"], mesh.shape["ctx"] // 2
    return jax.shard_map(
        functools.partial(body, n=n, ny=ny),
        mesh=mesh,
        in_specs=placed,
        out_specs=(
            P(("rep", "fsdp"), "ctx", None),
            P(("rep", "fsdp"), "ctx", None),
            P(None, None, "fsdp", None),
            P(None, "fsdp", None),
            P(None, "fsdp", None),
            P(None, "fsdp", None),
            P(None, "fsdp"),
            P(None, None, "fsdp"),
            P(None, "fsdp"),
            P(None, None, "fsdp"),
            P(None, None, "fsdp"),
        ),
        check_vma=False,
    )
```

```python
import functools

import jax
import jax.numpy as jnp
from jax import lax
from jax.experimental import pallas as pl
from jax.experimental.pallas import tpu as pltpu
from jax.sharding import PartitionSpec as P

HEADS = 12
HEAD = 64
D = HEADS * HEAD
MESH = pl.DeviceIdType.MESH
BF = jnp.bfloat16
F32 = jnp.float32
MIB = 2**20
GATHER_CUT, REDUCE_CUT = 1, 3

epsilon = 1e-05
score_scale = 0.125
masked_value = -1e30


class Place:
    def __init__(self, n, ny):
        self.n, self.ny = n, ny
        self.r = lax.axis_index("rep")
        self.z = lax.axis_index("fsdp")
        self.c = lax.axis_index("ctx")
        self.y, self.k = lax.div(self.c, 2), lax.rem(self.c, 2)
        self.e = lax.rem(self.y, 2)
        self.q = 2 * self.e + self.r
        self.qx = 2 * self.e + (1 - self.r)
        self.qy = 2 * (1 - self.e) + self.r
        self.qd = 2 * (1 - self.e) + (1 - self.r)

    def shard(self, offset):
        return lax.rem(self.z + (offset + self.n), self.n)

    def up(self, offset):
        return (self.r, self.shard(offset), self.c)

    def x(self):
        return (1 - self.r, self.z, self.c)

    def across(self):
        return (self.r, self.z, 2 * (self.y + 1 - 2 * self.e) + self.k)

    def row(self, offset, flip=0):
        y = lax.rem(self.y + offset, self.ny)
        k = self.k + flip * (1 - 2 * self.k)
        return (self.r, self.z, 2 * y + k)

    def core(self):
        return self.row(0, 1)

    def greet(self):
        others = [self.up(o) for o in range(1, self.n)]
        others += [self.x(), self.core()]
        others += [self.row(o) for o in range(1, self.ny)]
        barrier = pltpu.get_barrier_semaphore()
        for other in others:
            pl.semaphore_signal(barrier, inc=1, device_id=other, device_id_type=MESH)
        pl.semaphore_wait(barrier, len(others))


def remote(src, dst, send, recv, device):
    copy = pltpu.make_async_remote_copy(
        src_ref=src, dst_ref=dst, send_sem=send, recv_sem=recv, device_id=device, device_id_type=MESH
    )
    copy.start()
    return copy


def cut(half, sixths):
    first = max(8, half * sixths // 96 * 16)
    return [(0, first), (first, half - first)]


class Gather:
    def __init__(self, place, full, by_shard, local, send, recv):
        self.place, self.full, self.by_shard = place, full, by_shard
        self.local, self.send, self.recv = local, send, recv
        self.n = place.n
        self.half = full.shape[2] // 2
        self.pieces = cut(self.half, GATHER_CUT)
        self.copies, self.core_copies = [], []

    @staticmethod
    def count(n):
        return 10 * (n - 1)

    def part(self, shard, q, piece=None):
        start, size = (0, self.half) if piece is None else piece
        rows = pl.ds(pl.multiple_of(self.place.k * self.half + start, 8), size)
        return self.full.at[shard, q, rows] if self.by_shard else self.full.at[q, shard, rows]

    def load(self, sources):
        self.loads = []
        z = self.place.z
        for i, (q, count, source) in enumerate(sources):
            if self.by_shard:
                target = self.full.at[z]
            elif count is None:
                target = self.full.at[q, z]
            else:
                target = self.full.at[pl.ds(q, count), z]
            copy = pltpu.make_async_copy(source, target, self.local.at[i])
            copy.start()
            self.loads.append(copy)

    def share(self, kind, offset, piece, device):
        slot = kind * (self.n - 1) + offset - 1
        copy = remote(piece, piece, self.send.at[slot], self.recv.at[slot], device)
        self.copies.append(copy)
        return copy

    def core_share(self, kind, offset, piece):
        copy = self.share(5 + kind, offset, piece, self.place.core())
        self.core_copies.append(copy)

    def start(self):
        place = self.place
        for copy in self.loads:
            copy.wait()
        mine = self.part(place.z, place.q)
        self.ups = [self.share(0, o, mine, place.up(o)) for o in range(1, self.n)]

    def to_x(self):
        place = self.place
        self.xs = []
        for o in range(1, self.n):
            self.ups[o - 1].wait_recv()
            piece = self.part(place.shard(-o), place.q)
            self.xs.append(self.share(1, o, piece, place.x()))
            self.core_share(0, o, piece)

    def to_y(self):
        place = self.place
        self.ys = [
            self.share(2, o, self.part(place.shard(-o), place.q), place.across()) for o in range(1, self.n)
        ]

    def from_x(self):
        place = self.place
        self.dys = []
        for o in range(1, self.n):
            shard = place.shard(-o)
            self.xs[o - 1].wait_recv()
            self.dys.append(self.share(3, o, self.part(shard, place.qx, self.pieces[0]), place.across()))
            self.core_share(1, o, self.part(shard, place.qx))

    def from_y(self):
        place = self.place
        self.dxs = []
        for o in range(1, self.n):
            shard = place.shard(-o)
            self.ys[o - 1].wait_recv()
            self.dxs.append(self.share(4, o, self.part(shard, place.qy, self.pieces[1]), place.x()))
            self.core_share(2, o, self.part(shard, place.qy))

    def last(self):
        place = self.place
        for o in range(1, self.n):
            shard = place.shard(-o)
            self.dys[o - 1].wait_recv()
            self.core_share(3, o, self.part(shard, place.qd, self.pieces[0]))
        for o in range(1, self.n):
            shard = place.shard(-o)
            self.dxs[o - 1].wait_recv()
            self.core_share(4, o, self.part(shard, place.qd, self.pieces[1]))

    def finish(self):
        for copy in self.core_copies:
            copy.wait_recv()

    def drain(self):
        for copy in self.copies:
            copy.wait_send()

    def steps(self):
        return dict(A=self.start, B=self.to_x, Y=self.to_y, C=self.from_x, E=self.from_y, L=self.last, F=self.finish)


def weight_sources(b, qkv, ao, win, wout):
    return [
        [(0, 3, qkv.at[b]), (3, None, ao.at[b])],
        [(q, None, win.at[b, :, pl.ds(q * D, D)]) for q in range(4)],
        [(None, None, wout.at[b])],
    ]


class Reduce:
    def __init__(self, place, grad, landing, out, wide, local, send, recv, credit):
        self.place, self.grad, self.out, self.wide = place, grad, out, wide
        self.core_in, self.x_in, self.y_in, self.dx_in, self.dy_in, self.z_in, self.far_in = landing
        self.local, self.send, self.recv, self.credit = local, send, recv, credit
        self.n, self.ny = place.n, place.ny
        self.half = grad.shape[2] // 2
        self.low, self.top = cut(self.half, REDUCE_CUT)
        self.copies, self.cored, self.owns = [], [], []
        self.slot = 0
        self.plan = [self.add_cores, self.plane, self.depth, self.total, self.turn, self.last]

    @staticmethod
    def count(n, ny):
        return 4 + 6 + (n - 1) + (ny // 2 - 1) + 9

    @staticmethod
    def landing_buffers(n, ny):
        half = D // n // 2
        (_, second), (_, first) = cut(half, REDUCE_CUT)
        return [
            pltpu.VMEM((n, 4, half, D), BF),
            pltpu.VMEM((n, half, D), BF),
            pltpu.VMEM((n, half, D), BF),
            pltpu.VMEM((n, first, D), BF),
            pltpu.VMEM((n, second, D), BF),
            pltpu.VMEM((n - 1, half, D), BF),
            pltpu.VMEM((max(1, ny // 2 - 1), half, D), BF),
        ]

    def peers(self):
        place = self.place
        others = [place.up(o) for o in range(1, self.n)] + [place.x(), place.across(), place.core()]
        return others + [place.row(2 * i + 2) for i in range(self.ny // 2 - 1)]

    def release(self):
        for other in self.peers():
            pl.semaphore_signal(self.credit, inc=1, device_id=other, device_id_type=MESH)

    def acquire(self):
        pl.semaphore_wait(self.credit, len(self.peers()))

    def share(self, src, dst, device):
        copy = remote(src, dst, self.send.at[self.slot], self.recv.at[self.slot], device)
        self.slot += 1
        self.copies.append(copy)
        return copy

    def rows(self, k, piece=None):
        start, size = (0, self.half) if piece is None else piece
        return pl.ds(pl.multiple_of(k * self.half + start, 8), size)

    def own(self, shards, q, piece=None):
        return self.grad.at[shards, q, self.rows(self.place.k, piece)]

    def core(self, shards, q):
        source = self.grad.at[shards, q, self.rows(1 - self.place.k)]
        self.cored.append(self.share(source, self.core_in.at[shards, q], self.place.core()))

    def add_into(self, target, *sources):
        total = target[...].astype(F32)
        for source in sources:
            total = total + source[...].astype(F32)
        target[...] = total.astype(BF)

    def add_cores(self):
        for copy in self.cored:
            copy.wait_recv()

        def one(i, _):
            shard, q = lax.div(i, 4), lax.rem(i, 4)
            self.add_into(self.own(shard, q), self.core_in.at[shard, q])
            return 0

        lax.fori_loop(0, 4 * self.n, one, 0)
        place, every = self.place, slice(None)
        top, low = pl.ds(*self.top), pl.ds(*self.low)
        self.dx = self.share(self.own(every, place.qd, self.top), self.dx_in, place.x())
        self.dy = self.share(self.own(every, place.qd, self.low), self.dy_in, place.across())
        self.planes = [
            self.share(self.own(every, place.qx, self.top), self.x_in.at[:, top], place.x()),
            self.share(self.own(every, place.qy, self.low), self.y_in.at[:, low], place.across()),
        ]

    def plane(self):
        place, every = self.place, slice(None)
        top, low = pl.ds(*self.top), pl.ds(*self.low)
        self.dx.wait_recv()

        def one(j, _):
            self.add_into(self.own(j, place.qy, self.top), self.dx_in.at[j])
            return 0

        lax.fori_loop(0, self.n, one, 0)
        self.planes.append(
            self.share(self.own(every, place.qy, self.top), self.y_in.at[:, top], place.across())
        )
        self.dy.wait_recv()

        def two(j, _):
            self.add_into(self.own(j, place.qx, self.low), self.dy_in.at[j])
            return 0

        lax.fori_loop(0, self.n, two, 0)
        self.planes.append(self.share(self.own(every, place.qx, self.low), self.x_in.at[:, low], place.x()))

    def depth(self):
        place = self.place
        for copy in self.planes:
            copy.wait_recv()

        def one(j, _):
            self.add_into(self.own(j, place.q), self.x_in.at[j], self.y_in.at[j])
            return 0

        lax.fori_loop(0, self.n, one, 0)
        self.deep = [
            self.share(self.own(place.shard(o), place.q), self.z_in.at[o - 1], place.up(o))
            for o in range(1, self.n)
        ]

    def mine(self, q, piece=None):
        rows = self.rows(self.place.k, piece)
        if self.wide:
            return self.out.at[rows, pl.ds(pl.multiple_of(q * D, D), D)]
        return self.out.at[q, rows]

    def total(self):
        place = self.place
        for copy in self.deep:
            copy.wait_recv()
        own = self.own(place.z, place.q)
        self.add_into(own, *[self.z_in.at[o - 1] for o in range(1, self.n)])
        if self.ny > 2:
            far = [self.share(own, self.far_in.at[i], place.row(2 * i + 2)) for i in range(self.ny // 2 - 1)]
            for copy in far:
                copy.wait_recv()
            mine = own[...].astype(F32)
            terms = [mine] + [self.far_in[i].astype(F32) for i in range(self.ny // 2 - 1)]
            total = jnp.zeros_like(mine)
            for y in range(0, self.ny, 2):
                offset = lax.rem(place.y - place.e - y + self.ny, self.ny)
                for i, term in enumerate(terms):
                    total = total + jnp.where(offset == 2 * i, term, 0.0)
            for copy in far:
                copy.wait_send()
            self.copies = [copy for copy in self.copies if all(copy is not other for other in far)]
            own[...] = total.astype(BF)
        copy = pltpu.make_async_copy(own, self.mine(place.q), self.local)
        copy.start()
        self.owns.append(copy)
        self.spread = [
            self.share(own, self.mine(place.q), place.x()),
            self.share(own, self.mine(place.q), place.across()),
        ]
        self.cores = [self.share(own, self.mine(place.q), place.core())]

    def forward(self, q, device, piece=None):
        return self.share(self.mine(q, piece), self.mine(q, piece), device)

    def turn(self):
        place = self.place
        self.spread[0].wait_recv()
        self.dy = self.forward(place.qx, place.across(), self.top)
        self.cores.append(self.forward(place.qx, place.core()))
        self.spread[1].wait_recv()
        self.dx = self.forward(place.qy, place.x(), self.low)
        self.cores.append(self.forward(place.qy, place.core()))

    def last(self):
        place = self.place
        self.dy.wait_recv()
        self.cores.append(self.forward(place.qd, place.core(), self.top))
        self.dx.wait_recv()
        self.cores.append(self.forward(place.qd, place.core(), self.low))

    def finish(self):
        for copy in self.cores:
            copy.wait_recv()

    def drain(self):
        for copy in self.copies:
            copy.wait_send()
        for copy in self.owns:
            copy.wait()
        self.copies, self.owns = [], []


class SmallReduce:
    def __init__(self, place, total, landing, send, recv):
        self.place, self.total, self.landing, self.send, self.recv = place, total, landing, send, recv
        n, ny = place.n, place.ny
        self.stages = [
            [place.core()],
            [place.up(o) for o in range(1, n)],
            [place.x()],
            [place.row(o) for o in range(1, ny)],
        ]
        self.copies = []
        self.slot = 0

    @staticmethod
    def count(n, ny):
        return 1 + (n - 1) + 1 + (ny - 1)

    def start(self, stage):
        self.current = []
        for device in self.stages[stage]:
            slot = self.slot
            copy = remote(
                self.total.at[stage], self.landing.at[slot], self.send.at[slot], self.recv.at[slot], device
            )
            self.current.append((slot, copy))
            self.copies.append(copy)
            self.slot += 1

    def end(self, stage):
        place, ny = self.place, self.place.ny
        for _, copy in self.current:
            copy.wait_recv()
        terms = [self.total[stage]] + [self.landing[slot] for slot, _ in self.current]
        if stage == 3 and ny > 2:
            total = jnp.zeros_like(terms[0])
            for y in range(ny):
                offset = lax.rem(place.y - y + ny, ny)
                for o in range(ny):
                    total = total + jnp.where(offset == o, terms[o], 0.0)
        else:
            total = functools.reduce(lambda a, b: a + b, terms)
        self.total[stage + 1] = total

    def steps(self):
        out = [functools.partial(self.start, 0)]
        for stage in range(4):
            out.append(functools.partial(self.end, stage))
            if stage < 3:
                out.append(functools.partial(self.start, stage + 1))
        return out


def matmul(operand_a, operand_b):
    return jnp.dot(operand_a, operand_b, preferred_element_type=F32)


def matmul_left_t(operand_a, operand_b):
    return lax.dot_general(operand_a, operand_b, (((0,), (0,)), ((), ())), preferred_element_type=F32)


def matmul_right_t(operand_a, operand_b):
    return lax.dot_general(operand_a, operand_b, (((1,), (1,)), ((), ())), preferred_element_type=F32)


def unit(ref, index, columns=None):
    block = ref[index] if columns is None else ref[index, :, :, columns]
    return block.reshape(D, block.shape[-1])


def center_scale(rows):
    center = rows - jnp.mean(rows, axis=-1, keepdims=True)
    inverse = lax.rsqrt(jnp.mean(center * center, axis=-1, keepdims=True) + epsilon)
    return center * inverse, inverse


class Exchange:
    def __init__(self, place, kv, send, recv):
        self.place, self.kv, self.send, self.recv = place, kv, send, recv
        self.copies = []

    @staticmethod
    def count(ny):
        return 2 * ny

    def share(self, half, chip_row, slot, device):
        part = self.kv.at[:, half, 2 * chip_row + self.place.k]
        copy = remote(part, part, self.send.at[half, slot], self.recv.at[half, slot], device)
        self.copies.append(copy)
        return copy

    def start(self, half):
        place, ny = self.place, self.place.ny
        far = [self.share(half, place.y, o, place.row(o)) for o in range(1, ny)]
        near = [self.share(half, place.y, 0, place.core())]
        return far, near

    def forward(self, half, state):
        place, ny = self.place, self.place.ny
        far, near = state
        for o in range(1, ny):
            far[o - 1].wait_recv()
            near.append(self.share(half, lax.rem(place.y - o + ny, ny), ny + o - 1, place.core()))

    def finish(self, state):
        for copy in state[1]:
            copy.wait_recv()

    def drain(self):
        for copy in self.copies:
            copy.wait_send()


def spread_small(n, small_full, wide_full, narrow, wide):
    width = small_full.shape[2]
    row = lax.broadcasted_iota(jnp.int32, (width, D), 0)
    column = lax.broadcasted_iota(jnp.int32, (width, D), 1)
    total = 0.0
    for j in range(n):
        place = jnp.where(column - row == j * width, 1.0, 0.0).astype(BF)
        total = total + matmul(small_full[j], place)
    narrow[...] = total
    turns = n // 4
    for c in range(4):
        if turns == 1:
            total = wide_full[c].astype(F32)
        else:
            row = lax.broadcasted_iota(jnp.int32, (4 * width, D), 0)
            column = lax.broadcasted_iota(jnp.int32, (4 * width, D), 1)
            total = 0.0
            for t in range(turns):
                place = jnp.where(column - row == t * 4 * width, 1.0, 0.0).astype(BF)
                total = total + matmul(wide_full[c * turns + t], place)
        for b in range(2):
            wide[b, c : c + 1] = total[b : b + 1]


def side_mask(side):
    lane = lax.broadcasted_iota(jnp.int32, (1, 2 * HEAD), 1)
    inside = lane < HEAD if side == 0 else lane >= HEAD
    return jnp.where(inside, 1.0, 0.0).astype(BF)


def attend(query, kv, half, mask, out, stats, first_head):
    rows = query.shape[0]
    lane = lax.broadcasted_iota(jnp.int32, (rows, 2 * HEAD), 1)
    allowed = mask[0:1]

    def pair(p, _):
        columns = pl.ds(pl.multiple_of(p * 2 * HEAD, 2 * HEAD), 2 * HEAD)
        where = pl.ds(pl.multiple_of(half * (D // 2) + p * 2 * HEAD, 2 * HEAD), 2 * HEAD)
        keys = kv[0, half, :, :, columns].reshape(-1, 2 * HEAD)
        values = kv[1, half, :, :, columns].reshape(-1, 2 * HEAD)
        query_pair = query[:, where]
        mixed = []
        for side in range(2):
            scores = matmul_right_t(query_pair * side_mask(side), keys) + allowed
            peak = jnp.max(scores, axis=-1, keepdims=True)
            weight = jnp.exp(scores - peak)
            total = jnp.sum(weight, axis=-1, keepdims=True)
            mixed.append(matmul((weight / total).astype(BF), values))
            head = first_head + 2 * p + side
            stats[...] = jnp.where(lane == head, peak + jnp.log(total), stats[...])
        out[:, where] = jnp.where(lane < HEAD, mixed[0], mixed[1])
        return 0

    lax.fori_loop(0, HEADS // 4, pair, 0)


SCHEDULE = [
    "A0 B0 Y0 A1",
    [
        "C0 E0 B1 Y1 A2 L0 C1 E1 B2 Y2 A3 F0",
        "L1 C2 E2 B3 Y3 A4",
        "F1 L2",
        "C3 E3 B4 Y4",
        "A5 F2",
        "L3",
        "C4 E4",
        "B5 Y5",
        "F3",
        "",
    ],
    ["L4", "C5 E5 F4", "L5", "F5", "", "", "", "", "", ""],
]

SAVED = ("x", "query", "mixed", "stats", "hat_one", "active", "slope", "hat_two")


def forward_kernel(n, ny, *refs):
    tokens, mask, qkv, ao, win, wout, query_bias, bias_rows, wide_bias, gains, shifts = refs[:11]
    refs = refs[11:]
    outs = refs[:6]
    kv_outs, saved_outs = refs[6:8], refs[8:16]
    narrow_out, wide_out, result = refs[16:19]
    refs = refs[19:]
    fulls, kvs, saved = refs[:6], refs[6:8], refs[8:16]
    carried, normed, normed_bf, small_full, wide_full, small_rows, wide_rows = refs[16:23]
    local, send, recv, small_send, small_recv, kv_send, kv_recv, save_sem = refs[23:]
    place = Place(n, ny)
    groups = []
    for g in range(6):
        b, kind = g // 3, g % 3
        group = Gather(place, fulls[g], kind == 2, local.at[g], send.at[g], recv.at[g])
        group.load(weight_sources(b, qkv, ao, win, wout)[kind])
        groups.append(group)
    small_rows[0:2] = query_bias[...].astype(F32)
    for b in range(2):
        small_rows[2 + 3 * b : 5 + 3 * b] = bias_rows[b].astype(F32)
        small_rows[8 + 2 * b : 10 + 2 * b] = gains[b].astype(F32)
        small_rows[12 + 2 * b : 14 + 2 * b] = shifts[b].astype(F32)
    wide_rows[...] = jnp.zeros_like(wide_rows)
    wide_rows[0:2] = wide_bias[...].astype(F32)
    small_full[place.z] = small_rows[...].astype(BF)
    wide_full[place.z] = wide_rows[...].astype(BF)
    place.greet()
    smalls = []
    for i, ref in enumerate((small_full, wide_full)):
        own = ref.at[place.z]
        smalls += [
            remote(own, own, small_send.at[i, o], small_recv.at[i, o], place.up(o)) for o in range(1, n)
        ]
    kept = []

    def keep(source, target, sem):
        copy = pltpu.make_async_copy(source, target, sem)
        copy.start()
        kept.append(copy)

    plans = [group.steps() for group in groups]

    def run(steps):
        for name in steps.split():
            g = int(name[1])
            plans[g].pop(name[0])()
            if name[0] == "F":
                keep(fulls[g], outs[g], local.at[g, 4])

    carried[...] = tokens[...].astype(F32)
    run(SCHEDULE[0])
    for copy in smalls:
        copy.wait_recv()
    spread_small(n, small_full, wide_full, narrow_out, wide_out)
    x, query, mixed, stats, hat_one, active, slope, hat_two = saved
    for b in range(2):
        first, second, third = fulls[3 * b : 3 * b + 3]

        def save(*names):
            for name in names:
                i = SAVED.index(name)
                keep(saved[i].at[b], saved_outs[i].at[b], save_sem.at[b, i])

        turn = iter(SCHEDULE[1 + b])
        run(next(turn))
        x[b] = carried[...].astype(BF)
        exchange = Exchange(place, kvs[b], kv_send.at[b], kv_recv.at[b])
        states = []
        for half in range(2):
            columns = slice(half * (D // 2), (half + 1) * (D // 2))
            kvs[b][0, half, place.c] = matmul(x[b], unit(first, 1, columns)).astype(BF)
            value_bias = narrow_out[2 + 3 * b : 3 + 3 * b, columns]
            kvs[b][1, half, place.c] = (matmul(x[b], unit(first, 2, columns)) + value_bias).astype(BF)
            states.append(exchange.start(half))
        run(next(turn))
        projected = (matmul(x[b], unit(first, 0)) + narrow_out[b : b + 1]).astype(BF)
        query[b] = projected * jnp.asarray(score_scale, BF)
        stats[b] = jnp.zeros_like(stats[b])
        save("x", "query")
        for half in range(2):
            exchange.forward(half, states[half])
            exchange.finish(states[half])
            if half == 1:
                run(next(turn))
            attend(query.at[b], kvs[b], half, mask, mixed.at[b], stats.at[b], half * (HEADS // 2))
        run(next(turn))
        keep(kvs[b], kv_outs[b], save_sem.at[b, len(SAVED)])
        attended = matmul(mixed[b].astype(BF), unit(first, 3))
        hat, inverse = center_scale(carried[...] + attended + narrow_out[3 + 3 * b : 4 + 3 * b])
        hat_one[b] = hat
        lane = lax.broadcasted_iota(jnp.int32, stats.shape[1:], 1)
        stats[b] = jnp.where(lane == HEADS, inverse, stats[b])
        normed[...] = hat * narrow_out[8 + 2 * b : 9 + 2 * b] + narrow_out[12 + 2 * b : 13 + 2 * b]
        normed_bf[...] = normed[...].astype(BF)
        save("mixed", "hat_one")
        run(next(turn))
        for c in range(4):
            hidden = matmul(normed_bf[...], unit(second, c)) + wide_out[b, c : c + 1]
            cdf = 0.5 + 0.5 * lax.erf(hidden * (2.0**-0.5))
            pdf = jnp.exp(-0.5 * hidden * hidden) * ((2.0 * jnp.pi) ** -0.5)
            active[b, c] = (hidden * cdf).astype(BF)
            slope[b, c] = (cdf + hidden * pdf).astype(BF)
            run(next(turn))
        save("active", "slope")
        run(next(turn))
        update = normed[...] + narrow_out[4 + 3 * b : 5 + 3 * b]
        for c in range(4):
            update = update + matmul(active[b, c], third[c * n // 4 : (c + 1) * n // 4].reshape(D, D))
        hat, inverse = center_scale(update)
        hat_two[b] = hat
        stats[b] = jnp.where(lane == HEADS + 1, inverse, stats[b])
        save("stats", "hat_two")
        carried[...] = hat * narrow_out[9 + 2 * b : 10 + 2 * b] + narrow_out[13 + 2 * b : 14 + 2 * b]
        exchange.drain()
    result[...] = carried[...].astype(BF)
    for group in groups:
        group.drain()
    for copy in smalls:
        copy.wait_send()
    for copy in kept:
        copy.wait()


def forward_pass(n, ny, tokens, mask, qkv, ao, win, wout, *smalls):
    rows, width = tokens.shape[0], D // n
    nc = 2 * ny
    full_shapes = [(4, n, width, D), (4, n, width, D), (n, 4, width, D)] * 2
    kv_shape = (2, 2, nc, rows, D // 2)
    saved_shapes = {
        "x": ((2, rows, D), BF),
        "query": ((2, rows, D), BF),
        "mixed": ((2, rows, D), F32),
        "stats": ((2, rows, 128), F32),
        "hat_one": ((2, rows, D), F32),
        "active": ((2, 4, rows, D), BF),
        "slope": ((2, 4, rows, D), BF),
        "hat_two": ((2, rows, D), F32),
    }
    out = [jax.ShapeDtypeStruct(shape, BF) for shape in full_shapes]
    out += [jax.ShapeDtypeStruct(kv_shape, BF)] * 2
    out += [jax.ShapeDtypeStruct(*saved_shapes[name]) for name in SAVED]
    out += [
        jax.ShapeDtypeStruct((16, D), F32),
        jax.ShapeDtypeStruct((2, 4, D), F32),
        jax.ShapeDtypeStruct((rows, D), BF),
    ]
    anywhere = pl.BlockSpec(memory_space=pl.ANY)
    vmem = pl.BlockSpec(memory_space=pltpu.VMEM)
    scratch = [pltpu.VMEM(shape, BF) for shape in full_shapes]
    scratch += [pltpu.VMEM(kv_shape, BF)] * 2
    scratch += [pltpu.VMEM(*saved_shapes[name]) for name in SAVED]
    scratch += [
        pltpu.VMEM((rows, D), F32),
        pltpu.VMEM((rows, D), F32),
        pltpu.VMEM((rows, D), BF),
        pltpu.VMEM((n, 16, width), BF),
        pltpu.VMEM((n, 16, 4 * width), BF),
        pltpu.VMEM((16, width), F32),
        pltpu.VMEM((16, 4 * width), F32),
        pltpu.SemaphoreType.DMA((6, 5)),
        pltpu.SemaphoreType.DMA((6, Gather.count(n))),
        pltpu.SemaphoreType.DMA((6, Gather.count(n))),
        pltpu.SemaphoreType.DMA((2, n)),
        pltpu.SemaphoreType.DMA((2, n)),
        pltpu.SemaphoreType.DMA((2, 2, Exchange.count(ny))),
        pltpu.SemaphoreType.DMA((2, 2, Exchange.count(ny))),
        pltpu.SemaphoreType.DMA((2, len(SAVED) + 1)),
    ]
    return pl.pallas_call(
        functools.partial(forward_kernel, n, ny),
        out_shape=out,
        in_specs=[vmem, vmem] + [anywhere] * 4 + [vmem] * 5,
        out_specs=[anywhere] * 16 + [vmem] * 3,
        scratch_shapes=scratch,
        compiler_params=pltpu.CompilerParams(
            collective_id=0, has_side_effects=True, vmem_limit_bytes=60 * MIB
        ),
        name="forward_pass",
    )(tokens, mask, qkv, ao, win, wout, *smalls)


def normal_back(grad_output, gain, hat, inverse):
    grad_hat = grad_output * gain
    mean = jnp.mean(grad_hat, axis=-1, keepdims=True)
    slant = jnp.mean(grad_hat * hat, axis=-1, keepdims=True)
    return inverse * (grad_hat - mean - hat * slant)


def column_sum(rows):
    return jnp.sum(rows.astype(F32), axis=0, keepdims=True)


class KeyGrads:
    def __init__(self, place, grads, core_in, far_in, send, recv, credit):
        self.place, self.grads, self.core_in, self.far_in = place, grads, core_in, far_in
        self.send, self.recv, self.credit = send, recv, credit
        self.copies = []
        self.cored, self.far = {}, {}

    def peers(self):
        return [self.place.core()] + [self.place.row(o) for o in range(1, self.place.ny)]

    def release(self):
        for other in self.peers():
            pl.semaphore_signal(self.credit, inc=1, device_id=other, device_id_type=MESH)

    def acquire(self):
        pl.semaphore_wait(self.credit, len(self.peers()))

    @staticmethod
    def count(ny):
        return 2 * ny - 1

    def share(self, half, slot, src, dst, device):
        copy = remote(src, dst, self.send.at[half, slot], self.recv.at[half, slot], device)
        self.copies.append(copy)
        return copy

    def start(self, half):
        place, ny = self.place, self.place.ny
        self.cored[half] = []
        for i in range(ny):
            y = lax.rem(place.y + i, ny)
            part = self.grads.at[:, half, 2 * y + 1 - place.k]
            self.cored[half].append(self.share(half, i, part, self.core_in.at[:, half, y], place.core()))

    def middle(self, half):
        place, ny = self.place, self.place.ny
        for copy in self.cored[half]:
            copy.wait_recv()
        for y in range(ny):
            for kind in range(2):
                part = self.grads.at[kind, half, 2 * y + place.k]
                part[...] = (part[...].astype(F32) + self.core_in[kind, half, y].astype(F32)).astype(BF)
        self.far[half] = []
        for o in range(1, ny):
            y = lax.rem(place.y + o, ny)
            part = self.grads.at[:, half, 2 * y + place.k]
            self.far[half].append(
                self.share(half, ny + o - 1, part, self.far_in.at[:, half, o - 1], place.row(o))
            )

    def end(self, half, kind):
        for copy in self.far[half]:
            if kind == 0:
                copy.wait_recv()
        total = self.grads[kind, half, self.place.c].astype(F32)
        for o in range(1, self.place.ny):
            total = total + self.far_in[kind, half, o - 1].astype(F32)
        return total.astype(BF)

    def drain(self):
        for copy in self.copies:
            copy.wait_send()


def attend_back(query, kv, half, mask, stats, mixed, grad_mixed, grad_query, grads):
    rows = query.shape[0]
    lane = lax.broadcasted_iota(jnp.int32, (rows, 2 * HEAD), 1)
    blocks = 4 if kv.shape[2] <= 4 else 2

    def pair(p, _):
        columns = pl.ds(pl.multiple_of(p * 2 * HEAD, 2 * HEAD), 2 * HEAD)
        where = pl.ds(pl.multiple_of(half * (D // 2) + p * 2 * HEAD, 2 * HEAD), 2 * HEAD)
        query_pair, grad_pair = query[:, where], grad_mixed[:, where]
        products = (mixed[:, where] * grad_pair.astype(F32)).T
        grad_queries = [0.0, 0.0]
        for at in range(0, kv.shape[2], blocks):
            some = slice(at, at + blocks)
            keys = kv[0, half, some, :, columns].reshape(-1, 2 * HEAD)
            values = kv[1, half, some, :, columns].reshape(-1, 2 * HEAD)
            blocked = mask[at * rows : (at + blocks) * rows, :]
            grad_keys, grad_values = 0.0, 0.0
            for side in range(2):
                query_side, grad_side = query_pair * side_mask(side), grad_pair * side_mask(side)
                log_sum = stats[pl.ds(half * (HEADS // 2) + 2 * p + side, 1), :]
                inner = jnp.sum(products[side * HEAD : (side + 1) * HEAD], axis=0, keepdims=True)
                probs = jnp.exp(matmul_right_t(keys, query_side) + blocked - log_sum)
                grad_probs = matmul_right_t(values, grad_side)
                grad_scores = (probs * (grad_probs - inner)).astype(BF)
                grad_keys = grad_keys + matmul(grad_scores, query_side)
                grad_values = grad_values + matmul(probs.astype(BF), grad_side)
                grad_queries[side] = grad_queries[side] + matmul_left_t(grad_scores, keys)
            grads[0, half, some, :, columns] = grad_keys.astype(BF).reshape(-1, rows, 2 * HEAD)
            grads[1, half, some, :, columns] = grad_values.astype(BF).reshape(-1, rows, 2 * HEAD)
        grad_query[:, where] = (
            jnp.where(lane < HEAD, grad_queries[0], grad_queries[1]) * score_scale
        ).astype(BF)
        return 0

    lax.fori_loop(0, HEADS // 4, pair, 0)


ROWS = 12
PUMPS = [[1, 0, 0, 0, 0, 1, 0, 0], [1, 1, 1, 0, 0, 1, 0, 0]]
OUT_LATE, IN_LATE = [False, False], [True, False]


def backward_kernel(n, ny, *refs):
    upstream, mask, narrow = refs[:3]
    fulls, kvs, saved = refs[3:9], refs[9:11], refs[11:19]
    outs, out_small, out_tokens = refs[19:22], refs[22], refs[23]
    refs = refs[24:]
    window, held, kv = refs[0], refs[1:9], refs[9]
    grads, landings = refs[10:13], [refs[13 + 7 * i : 20 + 7 * i] for i in range(3)]
    refs = refs[34:]
    grad_kv, kv_core, kv_far = refs[:3]
    deeper, lower, update_rows, normed_rows, grad_query, grad_rows, stats_rows = refs[3:10]
    small_total, small_landing = refs[10:12]
    hidden = refs[12]
    carried = out_tokens
    load_sem, window_sem, local, send, recv, credit, kv_send, kv_recv, small_send, small_recv = refs[13:]
    place = Place(n, ny)
    roomy = ny == 2
    x, query, mixed, stats, hat_one, active, slope, hat_two = held
    if not roomy:
        hidden, update_rows, normed_rows = active, lower, lower
    ahead = window.shape[0]
    loads = {}

    def load(b, *names):
        for name in names:
            i = SAVED.index(name) if name != "kv" else len(SAVED)
            source, target = (kvs[b], kv) if name == "kv" else (saved[i].at[b], held[i])
            loads[(b, name)] = pltpu.make_async_copy(source, target, load_sem.at[i])
            loads[(b, name)].start()

    def ready(b, *names):
        for name in names:
            loads[(b, name)].wait()

    order = []
    for b in (1, 0):
        order += [(b, 2, c) for c in range(4)] + [(b, 1, c) for c in range(4)]
        order += [(b, 0, 3), (b, 0, 0), (b, 0, 1), (b, 0, 2)]
    fetched = []

    def fetch():
        i = len(fetched)
        if i < len(order):
            b, kind, c = order[i]
            copy = pltpu.make_async_copy(
                fulls[3 * b + kind].at[c], window.at[i % ahead], window_sem.at[i % ahead]
            )
            copy.start()
            fetched.append(copy)

    used = []

    def weight():
        i = len(used)
        if i > 0:
            fetch()
        fetched[i].wait()
        used.append(i)
        return window.at[i % ahead]

    load(1, "hat_two", "stats", "active", "slope", "hat_one", "mixed", "query", "kv", "x")
    for _ in range(ahead - 1):
        fetch()
    reduces = {}
    for b in (1, 0):
        for kind in range(3):
            g = 3 * b + kind
            reduces[(b, kind)] = Reduce(
                place,
                grads[kind],
                landings[kind],
                outs[kind].at[b],
                kind == 1,
                local.at[g],
                send.at[g],
                recv.at[g],
                credit.at[kind],
            )
    active_plans = []
    steps = {key: list(group.plan) for key, group in reduces.items()}

    def step(key):
        steps[key].pop(0)()
        if len(steps[key]) == 2 and key[0] == 1:
            reduces[key].release()

    def pump(count=1):
        for _ in range(count):
            for key in list(active_plans):
                step(key)
                if not steps[key]:
                    active_plans.remove(key)

    def complete(key):
        while steps[key]:
            pump()
        reduces[key].drain()

    def begin(b, kind):
        if b == 0:
            complete((1, kind))

    def sent(b, kind):
        active_plans.append((b, kind))

    place.greet()
    carried[...] = upstream[...].astype(F32)
    for b in (1, 0):
        third, second, first = [reduces[(b, kind)] for kind in (2, 1, 0)]

        def note(i, row, b=b):
            small_total[0, ROWS * b + i : ROWS * b + i + 1] = row

        turn = iter(PUMPS[b])
        gain_one, gain_two = narrow[8 + 2 * b : 9 + 2 * b], narrow[9 + 2 * b : 10 + 2 * b]
        ready(b, "hat_two", "stats", "active")
        stats_rows[...] = stats[...].T
        inverse_one, inverse_two = stats[:, HEADS : HEADS + 1], stats[:, HEADS + 1 : HEADS + 2]
        note(5, column_sum(carried[...] * hat_two[...]))
        note(7, column_sum(carried[...]))
        grad = normal_back(carried[...], gain_two, hat_two[...], inverse_two)
        deeper[...] = grad
        update_rows[...] = grad.astype(BF)
        note(3, column_sum(update_rows[...]))
        if b == 1:
            load(0, "hat_two")
        part = n // 4

        def out_grads(c):
            if c == 0:
                begin(b, 2)
            block = matmul_left_t(active[c], update_rows[...]).astype(BF)
            shards = pl.ds(c * part, part)
            grads[2][shards] = block.reshape(part, 4, D // n, D)
            if c == 0 and b == 0:
                third.acquire()
            third.core(shards, slice(None))
            if c == 3:
                sent(b, 2)

        def in_grads(c):
            if c == 0:
                begin(b, 1)
                normed_rows[...] = (hat_one[...] * gain_one + narrow[12 + 2 * b : 13 + 2 * b]).astype(BF)
            block = matmul_left_t(normed_rows[...], hidden[c]).astype(BF)
            grads[1][:, c] = block.reshape(n, D // n, D)
            if c == 0 and b == 0:
                second.acquire()
            second.core(slice(None), c)
            if c == 3:
                sent(b, 1)

        def attention_grads(i, left, right):
            if i == 3:
                begin(b, 0)
            block = matmul_left_t(left, right).astype(BF)
            grads[0][:, i] = block.reshape(n, D // n, D)
            if i == 3 and b == 0:
                first.acquire()
            first.core(slice(None), i)

        out_late, in_late = roomy and OUT_LATE[b], roomy and IN_LATE[b]
        if not out_late:
            for c in range(4):
                out_grads(c)
        ready(b, "slope", "hat_one")
        for c in range(4):
            flow = matmul_right_t(update_rows[...], weight()[...]) * slope[c].astype(F32)
            hidden[c] = flow.astype(BF)
            note(8 + c, column_sum(hidden[c]))
        if b == 1:
            load(0, "slope")
        pump(next(turn))
        if not in_late:
            for c in range(4):
                in_grads(c)
        pump(next(turn))
        for c in range(4):
            deeper[...] += matmul_right_t(hidden[c], weight()[...])
        note(4, column_sum(deeper[...] * hat_one[...]))
        note(6, column_sum(deeper[...]))
        carried[...] = normal_back(deeper[...], gain_one, hat_one[...], inverse_one)
        lower[...] = carried[...].astype(BF)
        note(2, column_sum(lower[...]))
        grad_rows[...] = matmul_right_t(lower[...], weight()[...]).astype(BF)
        pump(next(turn))
        ready(b, "mixed", "query", "kv")
        if not in_late:
            attention_grads(3, mixed[...].astype(BF), lower[...])
        keys = KeyGrads(place, grad_kv, kv_core, kv_far, kv_send.at[b], kv_recv.at[b], credit.at[3])
        if b == 0:
            keys.acquire()
        for half in range(2):
            attend_back(query, kv, half, mask, stats_rows, mixed, grad_rows, grad_query, grad_kv)
            keys.start(half)
            if half == 1:
                keys.middle(0)
            pump(next(turn))
        keys.middle(1)
        if out_late:
            for c in range(4):
                out_grads(c)
        pump(next(turn))
        if in_late:
            for c in range(4):
                in_grads(c)
            attention_grads(3, mixed[...].astype(BF), lower[...])
        if b == 1:
            load(0, "hat_one", "stats", "active", "mixed", "query", "kv")
        ready(b, "x")
        attention_grads(0, x[...], grad_query[...])
        note(0, column_sum(grad_query[...]))
        carried[...] += matmul_right_t(grad_query[...], weight()[...])
        pump(next(turn))
        for kind in range(2):
            for half in range(2):
                lower[:, half * (D // 2) : (half + 1) * (D // 2)] = keys.end(half, kind)
            attention_grads(1 + kind, x[...], lower[...])
            if kind == 1:
                note(1, column_sum(lower[...]))
            carried[...] += matmul_right_t(lower[...], weight()[...])
        sent(b, 0)
        pump(next(turn))
        keys.drain()
        if b == 1:
            keys.release()
            load(0, "x")
    small_sum = SmallReduce(place, small_total, small_landing, small_send, small_recv)
    small_steps = small_sum.steps()
    while active_plans or small_steps:
        if small_steps:
            small_steps.pop(0)()
        pump()
    out_small[...] = small_total[4]
    for key, group in reduces.items():
        group.finish()
        group.drain()
    for copy in small_sum.copies:
        copy.wait_send()


def backward_pass(n, ny, upstream, mask, narrow, fulls, kvs, saved):
    rows, width = upstream.shape[0], D // n
    nc = 2 * ny
    out = [jax.ShapeDtypeStruct((2,) + shape, BF) for shape in ((4, width, D), (width, 4 * D), (4, width, D))]
    out += [jax.ShapeDtypeStruct((2 * ROWS, D), F32), jax.ShapeDtypeStruct((rows, D), F32)]
    anywhere = pl.BlockSpec(memory_space=pl.ANY)
    vmem = pl.BlockSpec(memory_space=pltpu.VMEM)
    smalls = SmallReduce.count(n, ny)
    ahead = 4 if ny == 2 else 2
    scratch = [pltpu.VMEM((ahead, D, D), BF)]
    scratch += [pltpu.VMEM(item.shape[1:], item.dtype) for item in saved]
    scratch += [pltpu.VMEM(kvs[0].shape, BF)]
    scratch += [pltpu.VMEM((n, 4, width, D), BF)] * 3
    for _ in range(3):
        scratch += Reduce.landing_buffers(n, ny)
    scratch += [pltpu.VMEM((2, 2, nc, rows, D // 2), BF)]
    scratch += [pltpu.VMEM((2, 2, ny, rows, D // 2), BF), pltpu.VMEM((2, 2, ny - 1, rows, D // 2), BF)]
    scratch += [
        pltpu.VMEM((rows, D), F32),
        pltpu.VMEM((rows, D), BF),
        pltpu.VMEM((rows, D) if ny == 2 else (16, 128), BF),
        pltpu.VMEM((rows, D) if ny == 2 else (16, 128), BF),
        pltpu.VMEM((rows, D), BF),
        pltpu.VMEM((rows, D), BF),
        pltpu.VMEM((128, rows), F32),
        pltpu.VMEM((5, 2 * ROWS, D), F32),
        pltpu.VMEM((smalls, 2 * ROWS, D), F32),
        pltpu.VMEM((4, rows, D) if ny == 2 else (16, 128), BF),
        pltpu.SemaphoreType.DMA((len(SAVED) + 1,)),
        pltpu.SemaphoreType.DMA((ahead,)),
        pltpu.SemaphoreType.DMA((6,)),
        pltpu.SemaphoreType.DMA((6, Reduce.count(n, ny))),
        pltpu.SemaphoreType.DMA((6, Reduce.count(n, ny))),
        pltpu.SemaphoreType.REGULAR((4,)),
        pltpu.SemaphoreType.DMA((2, 2, KeyGrads.count(ny))),
        pltpu.SemaphoreType.DMA((2, 2, KeyGrads.count(ny))),
        pltpu.SemaphoreType.DMA((smalls,)),
        pltpu.SemaphoreType.DMA((smalls,)),
    ]
    return pl.pallas_call(
        functools.partial(backward_kernel, n, ny),
        out_shape=out,
        in_specs=[vmem] * 3 + [anywhere] * 16,
        out_specs=[anywhere] * 3 + [vmem] * 2,
        scratch_shapes=scratch,
        compiler_params=pltpu.CompilerParams(
            collective_id=1, has_side_effects=True, vmem_limit_bytes=63 * MIB
        ),
        name="backward_pass",
    )(upstream, mask, narrow, *fulls, *kvs, *saved)


def body(
    tokens,
    lengths,
    cotangent,
    w_qkv,
    w_attn_out,
    w_in,
    w_out,
    bias_q,
    bias_d,
    bias_ff,
    norm_gain,
    norm_shift,
    n,
    ny,
):
    row_count = tokens.shape[1]
    width = D // n
    z = lax.axis_index("fsdp")
    first_row = lax.axis_index("ctx") * row_count
    upstream = jnp.where((first_row + jnp.arange(row_count) < lengths[0])[:, None], cotangent[0], 0)
    mask = jnp.where(jnp.arange(2 * ny * row_count) < lengths[0], 0.0, masked_value).astype(F32)
    mask_row = jnp.broadcast_to(mask[None], (8, mask.shape[0]))
    made = forward_pass(
        n, ny, tokens[0], mask_row, w_qkv, w_attn_out, w_in, w_out.reshape(2, 4, width, D),
        bias_q, bias_d, bias_ff, norm_gain, norm_shift
    )
    fulls, kvs, saved = made[:6], made[6:8], made[8:16]
    narrow, _, result = made[16:]
    fulls = [full.reshape(4, D, D) for full in fulls]
    *sums, small_sum, grad_tokens = backward_pass(n, ny, upstream, mask[:, None], narrow, fulls, kvs, saved)
    small_sum = small_sum.reshape(2, ROWS, D)
    own = lax.dynamic_slice_in_dim(small_sum, z * width, width, 2)
    own_ff = lax.dynamic_slice_in_dim(small_sum[:, 8:].reshape(2, 4 * D), z * 4 * width, 4 * width, 1)
    return (
        result[None],
        grad_tokens[None],
        sums[0][:, :3].astype(F32),
        sums[0][:, 3].astype(F32),
        sums[1].astype(F32),
        sums[2].reshape(2, 4 * width, D).astype(F32),
        own[:, 0],
        own[:, 1:4],
        own_ff,
        own[:, 4:6],
        own[:, 6:8],
    )


def solution(mesh):
    placed = (
        P(("rep", "fsdp"), "ctx", None),
        P(("rep", "fsdp")),
        P(("rep", "fsdp"), "ctx", None),
        P(None, None, "fsdp", None),
        P(None, "fsdp", None),
        P(None, "fsdp", None),
        P(None, "fsdp", None),
        P(None, "fsdp"),
        P(None, None, "fsdp"),
        P(None, "fsdp"),
        P(None, None, "fsdp"),
        P(None, None, "fsdp"),
    )
    n, ny = mesh.shape["fsdp"], mesh.shape["ctx"] // 2
    return jax.shard_map(
        functools.partial(body, n=n, ny=ny),
        mesh=mesh,
        in_specs=placed,
        out_specs=(
            P(("rep", "fsdp"), "ctx", None),
            P(("rep", "fsdp"), "ctx", None),
            P(None, None, "fsdp", None),
            P(None, "fsdp", None),
            P(None, "fsdp", None),
            P(None, "fsdp", None),
            P(None, "fsdp"),
            P(None, None, "fsdp"),
            P(None, "fsdp"),
            P(None, None, "fsdp"),
            P(None, None, "fsdp"),
        ),
        check_vma=False,
    )
```
